32 devices in a mesh: dp: 4 (over z), ctx: 8 (over y, x, core).
Axes of the slice: x: 2, y: 2, z: 4, core: 2. Of those that a mesh axis runs over, the one named last changes fastest.
Arguments:
- tokens: bfloat16 [8, 2048, 768], P('dp', 'ctx'), may hold values from -6 to 6
- segments: int32 [8, 2048], P('dp', 'ctx'), may hold values from 0 to 15, as said below
- positions: int32 [8, 2048], P('dp', 'ctx'), may hold values from 0 to 6141, as said below
- gain_attn: bfloat16 [768], P(('dp', 'ctx')), may hold values from 0.099609375 to 1.8984375
- shift_attn: bfloat16 [768], P(('dp', 'ctx')), may hold values from -4 to 4
- gain_mlp: bfloat16 [768], P(('dp', 'ctx')), may hold values from 0.099609375 to 1.8984375
- shift_mlp: bfloat16 [768], P(('dp', 'ctx')), may hold values from -4 to 4
- qkv_weight: bfloat16 [768, 2304], P(('dp', 'ctx')), may hold values from -0.21875 to 0.21875
- query_bias: bfloat16 [768], P(('dp', 'ctx')), may hold values from -4 to 4
- key_bias: bfloat16 [768], P(('dp', 'ctx')), may hold values from -6 to 6
- value_bias: bfloat16 [768], P(('dp', 'ctx')), may hold values from -1.5 to 1.5
- dense_weight: bfloat16 [768, 768], P(('dp', 'ctx')), may hold values from -0.875 to 0.875
- expand_weight: bfloat16 [768, 3072], P(('dp', 'ctx')), may hold values from -0.21875 to 0.21875
- expand_bias: bfloat16 [3072], P(('dp', 'ctx')), may hold values from -4 to 4
- contract_weight: bfloat16 [3072, 768], P(('dp', 'ctx')), may hold values from -0.109375 to 0.109375
- output_bias: bfloat16 [768], P(('dp', 'ctx')), may hold values from -4 to 4
- cotangent: bfloat16 [8, 2048, 768], P('dp', 'ctx'), may hold values from -6 to 6
Outputs:
- output: bfloat16 [8, 2048, 768], P('dp', 'ctx')
- input_grad: bfloat16 [8, 2048, 768], P('dp', 'ctx')
- grad_gain_attn: float32 [768], P(('dp', 'ctx'))
- grad_shift_attn: float32 [768], P(('dp', 'ctx'))
- grad_gain_mlp: float32 [768], P(('dp', 'ctx'))
- grad_shift_mlp: float32 [768], P(('dp', 'ctx'))
- grad_qkv_weight: float32 [768, 2304], P(('dp', 'ctx'))
- grad_query_bias: float32 [768], P(('dp', 'ctx'))
- grad_key_bias: float32 [768], P(('dp', 'ctx'))
- grad_value_bias: float32 [768], P(('dp', 'ctx'))
- grad_dense_weight: float32 [768, 768], P(('dp', 'ctx'))
- grad_expand_weight: float32 [768, 3072], P(('dp', 'ctx'))
- grad_expand_bias: float32 [3072], P(('dp', 'ctx'))
- grad_contract_weight: float32 [3072, 768], P(('dp', 'ctx'))
- grad_output_bias: float32 [768], P(('dp', 'ctx'))
The draws below stay inside these ranges and needn't reach their ends.
Inputs may be any that keep to these rules, and one draw needn't show every extreme that they name: `segments`: along each sequence the document number is 0 at the first token and rises by 0 or 1 from one token to the next; a sequence holds at most 16 documents; among the 2 sequences of each index of dp, one is a single document and another holds exactly 16. `positions`: 0 at the first token of each document, rising by 1 to 3 from one token to the next within a document; in the single-document sequence of each index of dp it rises by exactly 3.
All inputs are finite; a program needn't handle non-finite values.
Results may differ from the reference program's by a relative error of at most 0.03.
Values may be sent and summed in bfloat16 or wider, within the bound.
No kernel may reach another device: no remote copies, remote signals or barrier semaphores. Data moves between devices by JAX's collectives and lax.ppermute only.
A program may use at most 192 MiB of HBM per device.

```python
import math
import jax
import jax.numpy as jnp
from jax import lax

HEADS = 12
HEAD_DIM = 64
D = 768
FF = 3072
ROT_DIMS = 16
SEQ_LEN = 2048
SEQS = 2
ALL_SEQS = 8
N_DP = 4


def document_table(key):
    seq_total = SEQS * N_DP
    score_key = jax.random.fold_in(key, 11)
    whole_key = jax.random.fold_in(key, 12)
    gap_key = jax.random.fold_in(key, 13)
    count_key = jax.random.fold_in(key, 14)
    token_index = jnp.arange(SEQ_LEN)
    scores = jax.random.randint(score_key, (seq_total, SEQ_LEN), 0, 131072) * SEQ_LEN + token_index[None, :]
    scores = jnp.where(token_index[None, :] == 0, -1, scores)
    starts = lax.top_k(scores, 15)[1]
    counts = jax.random.randint(count_key, (seq_total,), 1, 16)
    chosen_seq = jax.random.randint(whole_key, (N_DP,), 0, SEQS)
    seq_index = jnp.arange(seq_total)
    local_index = seq_index % SEQS
    own_choice = chosen_seq[seq_index // SEQS]
    single = local_index == own_choice
    fullest = local_index == (own_choice + 1) % SEQS
    counts = jnp.where(fullest, 15, counts)
    counts = jnp.where(single, 0, counts)
    keep = jnp.arange(15)[None, :] < counts[:, None]
    hits = (starts[:, :, None] == token_index[None, None, :]) & keep[:, :, None]
    opening = jnp.any(hits, axis=1) | (token_index[None, :] == 0)
    segment_ids = jnp.cumsum(opening.astype(jnp.int32), axis=1) - 1
    gap_sizes = jax.random.randint(gap_key, (seq_total, SEQ_LEN), 1, 4)
    gap_sizes = jnp.where(single[:, None], 3, gap_sizes)
    reach_pos = jnp.cumsum(gap_sizes, axis=1) - gap_sizes
    base_pos = lax.cummax(jnp.where(opening, reach_pos, 0), axis=1)
    return (segment_ids.astype(jnp.int32), (reach_pos - base_pos).astype(jnp.int32))


def draw_segments(key, part):
    return document_table(key)[0]


def draw_positions(key, part):
    return document_table(key)[1]


def strengthened(drawn, stream_key, source, target, parts, factor):
    owner, partner = [(jnp.arange(drawn.shape[dim]) // (drawn.shape[dim] // parts)).reshape([-1 if axis == dim else 1 for axis in range(drawn.ndim)]) for dim in (source, target)]
    chosen = jax.random.permutation(stream_key, parts)[partner]
    strong = (owner == chosen) | (owner == (partner + parts // 2) % parts)
    return jnp.where(strong, factor * drawn, drawn)


def steps_of(key, dims, pieces, smallest, high):
    gain, own = 1.0, jax.random.fold_in(key, 6)
    for axis_at, shards_of in pieces:
        steps = jnp.exp(jax.random.uniform(jax.random.fold_in(own, axis_at), (shards_of,), jnp.float32, smallest / len(pieces), high / len(pieces)))
        gain = gain * jnp.repeat(steps, dims[axis_at] // shards_of).reshape([-1 if axis == axis_at else 1 for axis in range(len(dims))])
    return gain


def noise(rng, extent, width, limit, shards=(), kind=jnp.bfloat16):
    level = steps_of(rng, extent, shards, -0.22, 0.18) if shards else 1.0
    drawn = jax.random.normal(rng, extent, jnp.float32) * width * level
    return jnp.minimum(jnp.maximum(drawn, -limit), limit).astype(kind)


def bell_draw_with(own_key, dims, scale, most, cuts, heavy, dtype=jnp.bfloat16):
    values = scale * jax.random.normal(own_key, dims, jnp.float32)
    if cuts:
        values = values * steps_of(own_key, dims, cuts, -0.22, 0.18)
    return jnp.clip(strengthened(values, jax.random.fold_in(own_key, 3), *heavy), -most, most).astype(dtype)


def setup_inputs(seed: int = 0) -> dict:
    seeds = jax.random.split(jax.random.key(seed), 18)
    tokens = noise(seeds[0], (ALL_SEQS, SEQ_LEN, D), 1.0, 6.0, ((0, 4), (1, 8)))
    segments = draw_segments(jax.random.fold_in(seeds[17], 71), 0)
    positions = draw_positions(jax.random.fold_in(seeds[17], 71), 0)
    gain_attn = jnp.clip(1.0 + 0.18 * jax.random.normal(seeds[3], (D,), jnp.float32), 0.099609375, 1.8984375).astype(jnp.bfloat16)
    shift_attn = noise(seeds[4], (D,), 0.3, 4.0, ((0, 32),))
    gain_mlp = jnp.clip(1.0 + 0.18 * jax.random.normal(seeds[5], (D,), jnp.float32), 0.099609375, 1.8984375).astype(jnp.bfloat16)
    shift_mlp = noise(seeds[6], (D,), 0.3, 4.0, ((0, 32),))
    qkv_weight = noise(seeds[7], (D, 3 * D), D ** -0.5, 0.21875, ((0, 32),))
    query_bias = noise(seeds[8], (D,), 0.3, 4.0, ((0, 32),))
    key_bias = noise(seeds[9], (D,), 1.0, 6.0, ((0, 32),))
    value_bias = noise(seeds[10], (D,), 0.1, 1.5, ((0, 32),))
    dense_weight = noise(seeds[11], (D, D), (D // 16) ** -0.5, 0.875, ((0, 32),))
    expand_weight = noise(seeds[12], (D, FF), D ** -0.5, 0.21875, ((0, 32),))
    expand_bias = noise(seeds[13], (FF,), 0.3, 4.0, ((0, 32),))
    contract_weight = noise(seeds[14], (FF, D), FF ** -0.5, 0.109375, ((0, 32),))
    output_bias = noise(seeds[15], (D,), 0.3, 4.0, ((0, 32),))
    cotangent = bell_draw_with(seeds[16], (ALL_SEQS, SEQ_LEN, D), 1.0, 6.0, ((0, 4), (1, 8)), (1, 2, 8, 2.0))
    return dict(tokens=tokens, segments=segments, positions=positions, gain_attn=gain_attn, shift_attn=shift_attn, gain_mlp=gain_mlp, shift_mlp=shift_mlp, qkv_weight=qkv_weight, query_bias=query_bias, key_bias=key_bias, value_bias=value_bias, dense_weight=dense_weight, expand_weight=expand_weight, expand_bias=expand_bias, contract_weight=contract_weight, output_bias=output_bias, cotangent=cotangent)


NEG_BIG = -1e+30
EPSILON = 1e-05
HIGHEST = lax.Precision.HIGHEST

@jax.custom_vjp
def low(v):
    return lax.optimization_barrier(v.astype(jnp.bfloat16)).astype(jnp.float32)

@jax.custom_vjp
def low_back(v):
    return v

def low_keep(v):
    return (low(v), None)

def low_pass(kept, grad):
    return (grad,)

def back_keep(v):
    return (v, None)

def back_low(kept, grad):
    return (low(grad),)
low.defvjp(low_keep, low_pass)
low_back.defvjp(back_keep, back_low)

def normalize(values, gain_vec, shift_vec):
    centre = values - lax.optimization_barrier(jnp.mean(values, axis=-1, keepdims=True))
    spread = lax.optimization_barrier(jnp.mean(centre * centre, axis=-1, keepdims=True))
    return centre * lax.rsqrt(spread + EPSILON) * gain_vec + shift_vec

def angles(positions):
    ladder = jnp.arange(ROT_DIMS // 2).astype(jnp.float32)
    inverse = jnp.exp(ladder * (-2.0 * math.log(10000.0) / ROT_DIMS))
    phase_angle = positions.astype(jnp.float32)[..., None] * inverse
    return (jnp.cos(phase_angle)[..., None, :], jnp.sin(phase_angle)[..., None, :])

def rotate(field_in, cosine, sine_part):
    half_dims = ROT_DIMS // 2
    lower_half = field_in[..., :half_dims]
    upper_half = field_in[..., half_dims:ROT_DIMS]
    remainder = field_in[..., ROT_DIMS:]
    return jnp.concatenate([lower_half * cosine - upper_half * sine_part, upper_half * cosine + lower_half * sine_part, remainder], axis=-1)

def project(left_side, right_side):
    return jnp.einsum('gld,df->glf', left_side, right_side, precision=HIGHEST)

def attention(query_rows, key_rows, value_rows, segment):
    groups = query_rows.shape[0]
    block_rows = min(512, SEQ_LEN)
    block_count = SEQ_LEN // block_rows
    key_index = jnp.arange(SEQ_LEN)
    score_scale = 1.0 / math.sqrt(HEAD_DIM)

    def one_block(inputs):
        query_blk, segment_blk, index_blk = inputs
        scores = jnp.einsum('gqhd,gkhd->gqhk', query_blk, key_rows, precision=HIGHEST) * score_scale
        scores = low_back(scores)
        allowed = (key_index[None, None, :] <= index_blk[None, :, None]) & (segment[:, None, :] == segment_blk[:, :, None])
        scores = jnp.where(allowed[:, :, None, :], scores, NEG_BIG)
        largest = lax.optimization_barrier(jnp.max(scores, axis=-1, keepdims=True))
        weights = jnp.exp(scores - largest)
        prob_rows = weights / lax.optimization_barrier(jnp.sum(weights, axis=-1, keepdims=True))
        return jnp.einsum('gqhk,gkhd->gqhd', low(prob_rows), value_rows, precision=HIGHEST)
    query_blocks = query_rows.reshape(groups, block_count, block_rows, HEADS, HEAD_DIM).transpose(1, 0, 2, 3, 4)
    segment_blocks = segment.reshape(groups, block_count, block_rows).transpose(1, 0, 2)
    index_blocks = key_index.reshape(block_count, block_rows)
    mixed_rows = lax.map(jax.checkpoint(one_block), (query_blocks, segment_blocks, index_blocks))
    return mixed_rows.transpose(1, 0, 2, 3, 4).reshape(groups, SEQ_LEN, HEADS, HEAD_DIM)

def layer_forward(tokens, params, segment, position):
    gain_attn, shift_attn, gain_mlp, shift_mlp, qkv_weight, query_bias, key_bias, value_bias, dense_weight, expand_weight, expand_bias, contract_weight, output_bias = params
    groups = tokens.shape[0]
    attn_in = low(normalize(tokens, gain_attn, shift_attn))
    mlp_in = low(normalize(tokens, gain_mlp, shift_mlp))
    packed = project(attn_in, qkv_weight)
    query_raw = low_back(packed[..., :D] + query_bias)
    key_raw = low_back(packed[..., D:2 * D] + key_bias)
    value_rows = low(low_back(packed[..., 2 * D:] + value_bias))
    cosine, sine_part = angles(position)
    heads_shape = (groups, SEQ_LEN, HEADS, HEAD_DIM)
    query_rows = low(rotate(query_raw.reshape(heads_shape), cosine, sine_part))
    key_rows = low(rotate(key_raw.reshape(heads_shape), cosine, sine_part))
    mixed_rows = attention(query_rows, key_rows, value_rows.reshape(heads_shape), segment)
    mixed_rows = low(low_back(mixed_rows.reshape(groups, SEQ_LEN, D)))
    hidden_pre = low_back(project(mlp_in, expand_weight) + expand_bias)
    hidden = low(jax.nn.gelu(hidden_pre, approximate=False))
    return tokens + project(mixed_rows, dense_weight) + project(hidden, contract_weight) + output_bias

def reference(tokens, segments, positions, gain_attn, shift_attn, gain_mlp, shift_mlp, qkv_weight, query_bias, key_bias, value_bias, dense_weight, expand_weight, expand_bias, contract_weight, output_bias, cotangent):
    params = tuple((member.astype(jnp.float32) for member in (gain_attn, shift_attn, gain_mlp, shift_mlp, qkv_weight, query_bias, key_bias, value_bias, dense_weight, expand_weight, expand_bias, contract_weight, output_bias)))
    group_size = math.gcd(ALL_SEQS, max(1, 4096 // SEQ_LEN))
    steps_count = ALL_SEQS // group_size

    def regroup(array):
        return array.reshape((steps_count, group_size) + array.shape[1:])

    def one_group(totals, inputs):
        tok_blk, seg_blk, pos_blk, cot_blk = inputs

        def forward(values, weights):
            return layer_forward(values, weights, seg_blk, pos_blk)
        result, pullback = jax.vjp(forward, tok_blk.astype(jnp.float32), params)
        d_tokens, d_params = pullback(cot_blk.astype(jnp.float32))
        totals = tuple((running + addend for running, addend in zip(totals, d_params)))
        return (totals, (result.astype(jnp.bfloat16), d_tokens.astype(jnp.bfloat16)))
    zero_grads = tuple((jnp.zeros(member.shape, jnp.float32) for member in params))
    totals, (output, input_grad) = lax.scan(one_group, zero_grads, (regroup(tokens), regroup(segments), regroup(positions), regroup(cotangent)))
    full_shape = (ALL_SEQS, SEQ_LEN, D)
    return (output.reshape(full_shape), input_grad.reshape(full_shape), totals[0], totals[1], totals[2], totals[3], totals[4], totals[5], totals[6], totals[7], totals[8], totals[9], totals[10], totals[11], totals[12])
```

```python
import math

import jax
import jax.numpy as jnp
from jax import lax
from jax.experimental import pallas as pl
from jax.experimental.pallas import tpu as pltpu
from jax.sharding import Mesh, PartitionSpec as P

HEAD_DIM = 64
ROT_DIMS = 16


NEG_BIG = -1e30
EPSILON = 1e-05


def from_behind(value, axis, by):
    size = lax.axis_size(axis)
    pairs = [(i, i + by) for i in range(size) if 0 <= i + by < size]
    return lax.ppermute(value, axis, pairs)


def shifted(value, axis, by):
    size = lax.axis_size(axis)
    return lax.ppermute(value, axis, [(i, (i + by) % size) for i in range(size)])


def normalize(values, gain_vec, shift_vec):
    centre = values - jnp.mean(values, axis=-1, keepdims=True)
    spread = jnp.mean(centre * centre, axis=-1, keepdims=True)
    return centre * lax.rsqrt(spread + EPSILON) * gain_vec + shift_vec


def angles(positions):
    ladder = jnp.arange(ROT_DIMS // 2).astype(jnp.float32)
    inverse = jnp.exp(ladder * (-2.0 * math.log(10000.0) / ROT_DIMS))
    phase_angle = positions.astype(jnp.float32)[..., None] * inverse
    return (jnp.cos(phase_angle)[..., None, :], jnp.sin(phase_angle)[..., None, :])


def rotate(field_in, cosine, sine_part):
    half_dims = ROT_DIMS // 2
    lower_half = field_in[..., :half_dims]
    upper_half = field_in[..., half_dims:ROT_DIMS]
    remainder = field_in[..., ROT_DIMS:]
    return jnp.concatenate(
        [
            lower_half * cosine - upper_half * sine_part,
            upper_half * cosine + lower_half * sine_part,
            remainder,
        ],
        axis=-1,
    )


def exact_gelu(pre_act):
    return jax.nn.gelu(pre_act, approximate=False)


def contract_last(left_side, right_side):
    return lax.dot_general(
        left_side, right_side, (((1,), (1,)), ((), ())), preferred_element_type=jnp.float32
    )


def visible(query_seg, query_start, key_seg, key_start):
    query_index = query_start + jnp.arange(query_seg.shape[1])
    key_index = key_start + jnp.arange(key_seg.shape[1])
    allowed = (key_index[None, None, :] <= query_index[None, :, None]) & (
        key_seg[:, None, :] == query_seg[:, :, None]
    )
    return allowed[:, :, None, :]


def pair_grads(query_side, stats_side, query_start, key_side, key_start):
    query_rows, d_mixed, query_seg = query_side
    log_total, delta_rows = stats_side
    key_rows, value_rows, key_seg = key_side
    score_scale = 1.0 / math.sqrt(HEAD_DIM)
    allowed = visible(query_seg, query_start, key_seg, key_start)
    scores = (
        jnp.einsum("bqhd,bkhd->bqhk", query_rows, key_rows, preferred_element_type=jnp.float32)
        * score_scale
    )
    prob_rows = jnp.where(
        allowed, jnp.exp(jnp.where(allowed, scores - log_total[..., None], NEG_BIG)), 0.0
    )
    d_prob = jnp.einsum("bqhd,bkhd->bqhk", d_mixed, value_rows, preferred_element_type=jnp.float32)
    d_scores = (prob_rows * (d_prob - delta_rows[..., None])).astype(jnp.bfloat16)
    d_query = (
        jnp.einsum("bqhk,bkhd->bqhd", d_scores, key_rows, preferred_element_type=jnp.float32)
        * score_scale
    )
    d_key = (
        jnp.einsum("bqhk,bqhd->bkhd", d_scores, query_rows, preferred_element_type=jnp.float32)
        * score_scale
    )
    d_value = jnp.einsum(
        "bqhk,bqhd->bkhd",
        prob_rows.astype(jnp.bfloat16),
        d_mixed,
        preferred_element_type=jnp.float32,
    )
    return (d_query, d_key, d_value)


def per_device(
    tokens,
    segments,
    positions,
    gain_attn,
    shift_attn,
    gain_mlp,
    shift_mlp,
    qkv_weight,
    query_bias,
    key_bias,
    value_bias,
    dense_weight,
    expand_weight,
    expand_bias,
    contract_weight,
    output_bias,
    cotangent,
):
    shards = (
        gain_attn,
        shift_attn,
        gain_mlp,
        shift_mlp,
        qkv_weight,
        query_bias,
        key_bias,
        value_bias,
        dense_weight,
        expand_weight,
        expand_bias,
        contract_weight,
        output_bias,
    )
    gathered = (
        lax.all_gather(shards[0], ("dp", "ctx"), axis=0, tiled=True),
        lax.all_gather(shards[1], ("dp", "ctx"), axis=0, tiled=True),
        lax.all_gather(shards[2], ("dp", "ctx"), axis=0, tiled=True),
        lax.all_gather(shards[3], ("dp", "ctx"), axis=0, tiled=True),
        lax.all_gather(shards[4], ("dp", "ctx"), axis=0, tiled=True),
        lax.all_gather(shards[5], ("dp", "ctx"), axis=0, tiled=True),
        lax.all_gather(shards[6], ("dp", "ctx"), axis=0, tiled=True),
        lax.all_gather(shards[7], ("dp", "ctx"), axis=0, tiled=True),
        lax.all_gather(shards[8], ("dp", "ctx"), axis=0, tiled=True),
        lax.all_gather(shards[9], ("dp", "ctx"), axis=0, tiled=True),
        lax.all_gather(shards[10], ("dp", "ctx"), axis=0, tiled=True),
        lax.all_gather(shards[11], ("dp", "ctx"), axis=0, tiled=True),
        lax.all_gather(shards[12], ("dp", "ctx"), axis=0, tiled=True),
    )
    seq_count, tok_count, model_width = tokens.shape
    row_count = seq_count * tok_count
    head_count = model_width // HEAD_DIM
    heads_shape = (seq_count, tok_count, head_count, HEAD_DIM)
    flat_shape = (seq_count, tok_count, model_width)
    full_gain_attn = gathered[0].astype(jnp.float32)
    full_shift_attn = gathered[1].astype(jnp.float32)
    full_gain_mlp = gathered[2].astype(jnp.float32)
    full_shift_mlp = gathered[3].astype(jnp.float32)
    full_query_bias = gathered[5].astype(jnp.float32)
    full_key_bias = gathered[6].astype(jnp.float32)
    full_value_bias = gathered[7].astype(jnp.float32)
    full_expand_bias = gathered[10].astype(jnp.float32)
    full_output_bias = gathered[12].astype(jnp.float32)
    flat_in = tokens.reshape(row_count, model_width).astype(jnp.float32)

    def both_norms(values, gain_one, shift_one, gain_two, shift_two):
        return (normalize(values, gain_one, shift_one), normalize(values, gain_two, shift_two))

    (norm_attn, norm_mlp), norm_pull = jax.vjp(
        both_norms, flat_in, full_gain_attn, full_shift_attn, full_gain_mlp, full_shift_mlp
    )
    attn_in = norm_attn.astype(jnp.bfloat16)
    mlp_in = norm_mlp.astype(jnp.bfloat16)
    packed = jnp.dot(attn_in, gathered[4], preferred_element_type=jnp.float32)
    query_raw = (packed[:, :model_width] + full_query_bias).reshape(heads_shape)
    key_raw = (packed[:, model_width : 2 * model_width] + full_key_bias).reshape(heads_shape)
    value_rows = (
        (packed[:, 2 * model_width :] + full_value_bias).astype(jnp.bfloat16).reshape(heads_shape)
    )
    cosine, sine_part = angles(positions)

    def turn_heads(field_in):
        return rotate(field_in, cosine, sine_part)

    query_turned, query_pull = jax.vjp(turn_heads, query_raw)
    key_turned, key_pull = jax.vjp(turn_heads, key_raw)
    query_rows = query_turned.astype(jnp.bfloat16)
    key_rows = key_turned.astype(jnp.bfloat16)
    key_flat = key_rows.reshape(flat_shape)
    value_flat = value_rows.reshape(flat_shape)
    ctx_count = lax.axis_size("ctx")
    ctx_index = lax.axis_index("ctx")
    here_start = ctx_index * tok_count
    score_scale = 1.0 / math.sqrt(HEAD_DIM)
    start_max = jnp.full((seq_count, tok_count, head_count), NEG_BIG, jnp.float32)
    key_blk = lax.all_gather(key_flat, "ctx", axis=1, tiled=True)
    value_blk = lax.all_gather(value_flat, "ctx", axis=1, tiled=True)
    seg_blk = lax.all_gather(segments, "ctx", axis=1, tiled=True)
    block_len = key_blk.shape[1]
    key_blk = key_blk.reshape(seq_count, block_len, head_count, HEAD_DIM)
    value_blk = value_blk.reshape(seq_count, block_len, head_count, HEAD_DIM)
    allowed = visible(segments, here_start, seg_blk, jnp.int32(0))
    scores = (
        jnp.einsum("bqhd,bkhd->bqhk", query_rows, key_blk, preferred_element_type=jnp.float32)
        * score_scale
    )
    scores = jnp.where(allowed, scores, NEG_BIG)
    new_max = jnp.maximum(start_max, jnp.max(scores, axis=-1))
    weights = jnp.where(allowed, jnp.exp(scores - new_max[..., None]), 0.0)
    new_sum = jnp.sum(weights, axis=-1)
    new_acc = jnp.einsum(
        "bqhk,bkhd->bqhd",
        weights.astype(jnp.bfloat16),
        value_blk,
        preferred_element_type=jnp.float32,
    )
    log_total = new_max + jnp.log(new_sum)
    mixed_full = new_acc / new_sum[..., None]
    mixed_rows = mixed_full.astype(jnp.bfloat16).reshape(row_count, model_width)
    hidden_pre = jnp.dot(mlp_in, gathered[9], preferred_element_type=jnp.float32) + full_expand_bias
    hidden_act, gelu_pull = jax.vjp(exact_gelu, hidden_pre)
    hidden_rows = hidden_act.astype(jnp.bfloat16)
    result = (
        flat_in
        + jnp.dot(mixed_rows, gathered[8], preferred_element_type=jnp.float32)
        + jnp.dot(hidden_rows, gathered[11], preferred_element_type=jnp.float32)
        + full_output_bias
    )
    output = result.astype(jnp.bfloat16).reshape(flat_shape)
    regathered = (
        lax.all_gather(shards[0], ("dp", "ctx"), axis=0, tiled=True),
        lax.all_gather(shards[1], ("dp", "ctx"), axis=0, tiled=True),
        lax.all_gather(shards[2], ("dp", "ctx"), axis=0, tiled=True),
        lax.all_gather(shards[3], ("dp", "ctx"), axis=0, tiled=True),
        lax.all_gather(shards[4], ("dp", "ctx"), axis=0, tiled=True),
        lax.all_gather(shards[5], ("dp", "ctx"), axis=0, tiled=True),
        lax.all_gather(shards[6], ("dp", "ctx"), axis=0, tiled=True),
        lax.all_gather(shards[7], ("dp", "ctx"), axis=0, tiled=True),
        lax.all_gather(shards[8], ("dp", "ctx"), axis=0, tiled=True),
        lax.all_gather(shards[9], ("dp", "ctx"), axis=0, tiled=True),
        lax.all_gather(shards[10], ("dp", "ctx"), axis=0, tiled=True),
        lax.all_gather(shards[11], ("dp", "ctx"), axis=0, tiled=True),
        lax.all_gather(shards[12], ("dp", "ctx"), axis=0, tiled=True),
    )
    back_qkv = regathered[4]
    back_dense = regathered[8]
    back_expand = regathered[9]
    back_contract = regathered[11]
    grad_rows = cotangent.reshape(row_count, model_width)
    grad_full = grad_rows.astype(jnp.float32)
    d_output_bias = jnp.sum(grad_full, axis=0)
    d_contract = jnp.einsum("rf,rd->fd", hidden_rows, grad_rows, preferred_element_type=jnp.float32)
    d_hidden = contract_last(grad_rows, back_contract)
    d_hidden_pre = gelu_pull(d_hidden)[0].astype(jnp.bfloat16)
    d_expand_bias = jnp.sum(d_hidden_pre.astype(jnp.float32), axis=0)
    d_expand = jnp.einsum("rd,rf->df", mlp_in, d_hidden_pre, preferred_element_type=jnp.float32)
    d_norm_mlp = contract_last(d_hidden_pre, back_expand)
    d_dense = jnp.einsum("ri,rd->id", mixed_rows, grad_rows, preferred_element_type=jnp.float32)
    d_mixed = contract_last(grad_rows, back_dense).astype(jnp.bfloat16).reshape(heads_shape)
    delta_rows = jnp.sum(d_mixed.astype(jnp.float32) * mixed_full, axis=-1)
    query_side = (query_rows, d_mixed, segments)
    stats_side = (log_total, delta_rows)

    def carry_step(step_num, loop_state):
        key_block, grad_block, d_query_acc = loop_state
        owner_dev = (ctx_index - step_num) % ctx_count
        key_side = (
            key_block[0].reshape(heads_shape),
            key_block[1].reshape(heads_shape),
            key_block[2],
        )
        d_query_part, d_key_part, d_value_part = pair_grads(
            query_side, stats_side, here_start, key_side, owner_dev * tok_count
        )
        grad_block = (
            grad_block[0] + d_key_part.reshape(flat_shape),
            grad_block[1] + d_value_part.reshape(flat_shape),
        )
        key_block = from_behind((key_block[0], key_block[1], key_block[2]), "ctx", 1)
        grad_block = (
            shifted(grad_block[0].astype(jnp.bfloat16), "ctx", 1).astype(jnp.float32),
            shifted(grad_block[1].astype(jnp.bfloat16), "ctx", 1).astype(jnp.float32),
        )
        return (key_block, grad_block, d_query_acc + d_query_part)

    zero_flat = jnp.zeros(flat_shape, jnp.float32)
    final_state = lax.fori_loop(
        0,
        ctx_count,
        carry_step,
        (
            (key_flat, value_flat, segments),
            (zero_flat, zero_flat),
            jnp.zeros(heads_shape, jnp.float32),
        ),
    )
    d_query_sum = final_state[2]
    d_key_sum = final_state[1][0].reshape(heads_shape)
    d_value_sum = final_state[1][1].reshape(heads_shape)
    d_query_raw = query_pull(d_query_sum)[0].astype(jnp.bfloat16).reshape(row_count, model_width)
    d_key_raw = key_pull(d_key_sum)[0].astype(jnp.bfloat16).reshape(row_count, model_width)
    d_value_low = d_value_sum.astype(jnp.bfloat16).reshape(row_count, model_width)
    d_query_bias = jnp.sum(d_query_raw.astype(jnp.float32), axis=0)
    d_key_bias = jnp.sum(d_key_raw.astype(jnp.float32), axis=0)
    d_value_bias = jnp.sum(d_value_low.astype(jnp.float32), axis=0)
    d_packed = jnp.concatenate([d_query_raw, d_key_raw, d_value_low], axis=1)
    d_qkv = jnp.einsum("rd,rp->dp", attn_in, d_packed, preferred_element_type=jnp.float32)
    d_norm_attn = contract_last(d_packed, back_qkv)
    d_flat, d_gain_attn, d_shift_attn, d_gain_mlp, d_shift_mlp = norm_pull(
        (d_norm_attn, d_norm_mlp)
    )
    input_grad = (grad_full + d_flat).astype(jnp.bfloat16).reshape(flat_shape)
    owned_grads = (
        lax.psum_scatter(d_gain_attn, ("dp", "ctx"), scatter_dimension=0, tiled=True),
        lax.psum_scatter(d_shift_attn, ("dp", "ctx"), scatter_dimension=0, tiled=True),
        lax.psum_scatter(d_gain_mlp, ("dp", "ctx"), scatter_dimension=0, tiled=True),
        lax.psum_scatter(d_shift_mlp, ("dp", "ctx"), scatter_dimension=0, tiled=True),
        lax.psum_scatter(d_qkv, ("dp", "ctx"), scatter_dimension=0, tiled=True),
        lax.psum_scatter(d_query_bias, ("dp", "ctx"), scatter_dimension=0, tiled=True),
        lax.psum_scatter(d_key_bias, ("dp", "ctx"), scatter_dimension=0, tiled=True),
        lax.psum_scatter(d_value_bias, ("dp", "ctx"), scatter_dimension=0, tiled=True),
        lax.psum_scatter(d_dense, ("dp", "ctx"), scatter_dimension=0, tiled=True),
        lax.psum_scatter(d_expand, ("dp", "ctx"), scatter_dimension=0, tiled=True),
        lax.psum_scatter(d_expand_bias, ("dp", "ctx"), scatter_dimension=0, tiled=True),
        lax.psum_scatter(d_contract, ("dp", "ctx"), scatter_dimension=0, tiled=True),
        lax.psum_scatter(d_output_bias, ("dp", "ctx"), scatter_dimension=0, tiled=True),
    )
    return (
        output,
        input_grad,
        owned_grads[0],
        owned_grads[1],
        owned_grads[2],
        owned_grads[3],
        owned_grads[4],
        owned_grads[5],
        owned_grads[6],
        owned_grads[7],
        owned_grads[8],
        owned_grads[9],
        owned_grads[10],
        owned_grads[11],
        owned_grads[12],
    )


LANES = 128
BLK = 256
BF = jnp.bfloat16
F32 = jnp.float32
SWAP = [(0, 1), (1, 0)]
CTX_AXES = ("y", "x", "core")
ALL_AXES = ("dp", "y", "x", "core")


def dot_nn(a, b):
    return lax.dot_general(a, b, (((1,), (0,)), ((), ())), preferred_element_type=F32)


def dot_nt(a, b):
    return lax.dot_general(a, b, (((1,), (1,)), ((), ())), preferred_element_type=F32)


def dot_tn(a, b):
    return lax.dot_general(a, b, (((0,), (0,)), ((), ())), preferred_element_type=F32)


def whole(shape):
    return pl.BlockSpec(shape, lambda *ids: (0,) * len(shape))


def pre_body(x_ref, vec_ref, w_ref, b_ref, cs_ref, s1_ref, s2_ref, eq_ref, ek_ref,
             attn_ref, mlp_ref, q_ref, k_ref, v_ref):
    x = x_ref[...].astype(F32)
    centre = x - jnp.mean(x, axis=1, keepdims=True)
    spread = jnp.mean(centre * centre, axis=1, keepdims=True)
    xhat = centre * lax.rsqrt(spread + EPSILON)
    attn_in = (xhat * vec_ref[0:1, :] + vec_ref[1:2, :]).astype(BF)
    attn_ref[...] = attn_in
    mlp_ref[...] = (xhat * vec_ref[2:3, :] + vec_ref[3:4, :]).astype(BF)
    packed = dot_nn(attn_in, w_ref[...]) + b_ref[...]
    heads = w_ref.shape[1] // (3 * LANES)
    wide = heads * LANES
    cs, s1, s2 = cs_ref[...], s1_ref[...], s2_ref[...]
    half = ROT_DIMS // 2

    def turn(u):
        return u * cs + pltpu.roll(u, LANES - half, 1) * s1 + pltpu.roll(u, half, 1) * s2

    for h in range(heads):
        cols = slice(h * LANES, (h + 1) * LANES)
        q = turn(packed[:, h * LANES : (h + 1) * LANES])
        q_ref[:, cols] = (q.astype(BF).astype(F32) * (1.0 / math.sqrt(HEAD_DIM)) + eq_ref[...]).astype(BF)
        k = turn(packed[:, wide + h * LANES : wide + (h + 1) * LANES])
        k_ref[:, cols] = (k + ek_ref[...]).astype(BF)
        v_ref[:, cols] = packed[:, 2 * wide + h * LANES : 2 * wide + (h + 1) * LANES].astype(BF)


def pre_call(x, vecs, w_pad, b_pad, tables):
    rows, width = x.shape
    cols = w_pad.shape[1]
    third = cols // 3
    row_block = lambda n: pl.BlockSpec((BLK, n), lambda i: (i, 0))
    return pl.pallas_call(
        pre_body,
        grid=(rows // BLK,),
        in_specs=[row_block(width), whole(vecs.shape), whole(w_pad.shape), whole(b_pad.shape)]
        + [row_block(LANES)] * 5,
        out_specs=[row_block(width)] * 2 + [row_block(third)] * 3,
        out_shape=[jax.ShapeDtypeStruct((rows, width), BF)] * 2
        + [jax.ShapeDtypeStruct((rows, third), BF)] * 3,
        compiler_params=pltpu.CompilerParams(vmem_limit_bytes=40 << 20),
        cost_estimate=pl.CostEstimate(
            flops=2 * rows * width * cols, bytes_accessed=rows * (width * 6 + cols * 2 + LANES * 20), transcendentals=0
        ),
        name="norm_qkv",
    )(x, vecs, w_pad, b_pad, *tables)


def piece(ref, place, j):
    return ref[pl.ds(pl.multiple_of((place ^ j) * BLK, BLK), BLK), :]


def causal(transposed):
    rows = lax.broadcasted_iota(jnp.int32, (BLK, BLK), 0)
    cols = lax.broadcasted_iota(jnp.int32, (BLK, BLK), 1)
    return cols >= rows if transposed else rows >= cols


def row_form(column):
    return jnp.transpose(jnp.broadcast_to(column, (BLK, LANES)))[0:1, :]


def attn_body(place_ref, q_ref, k_ref, v_ref, mixed_ref, full_ref, lse_ref):
    place = place_ref[0]
    for i in range(q_ref.shape[0] // BLK):
        q = piece(q_ref, place, i)
        scores = [dot_nt(q, piece(k_ref, place, j)) for j in range(i + 1)]
        scores[i] = jnp.where(causal(False), scores[i], NEG_BIG)
        top = scores[0]
        for s in scores[1:]:
            top = jnp.maximum(top, s)
        top = jnp.max(top, axis=1, keepdims=True)
        acc = None
        total = None
        for j in range(i + 1):
            p = jnp.exp(scores[j] - top)
            total = p if total is None else total + p
            part = dot_nn(p.astype(BF), piece(v_ref, place, j))
            acc = part if acc is None else acc + part
        total = jnp.sum(total, axis=1, keepdims=True)
        mixed = acc / total
        here = pl.ds(pl.multiple_of((place ^ i) * BLK, BLK), BLK)
        full_ref[here, :] = mixed
        mixed_ref[here, :] = mixed.astype(BF)
        lse_ref[0, i : i + 1, :] = row_form(top + jnp.log(total))


def attn_call(place, q, k, v):
    rows, cols = q.shape
    heads = cols // LANES
    col = pl.BlockSpec((rows, LANES), lambda h, p: (0, h))
    stats = pl.BlockSpec((1, rows // BLK, BLK), lambda h, p: (h, 0, 0))
    return pl.pallas_call(
        attn_body,
        grid_spec=pltpu.PrefetchScalarGridSpec(
            num_scalar_prefetch=1, grid=(heads,), in_specs=[col] * 3, out_specs=[col, col, stats]
        ),
        out_shape=[
            jax.ShapeDtypeStruct((rows, cols), BF),
            jax.ShapeDtypeStruct((rows, cols), F32),
            jax.ShapeDtypeStruct((heads, rows // BLK, BLK), F32),
        ],
        compiler_params=pltpu.CompilerParams(vmem_limit_bytes=48 << 20),
        cost_estimate=pl.CostEstimate(
            flops=heads * rows * rows * 2 * LANES * 4, bytes_accessed=rows * cols * 12, transcendentals=heads * rows * rows // 2
        ),
        name="attention",
    )(place, q, k, v)


def attn_back_body(place_ref, q_ref, k_ref, v_ref, do_ref, full_ref, lse_ref, cs_ref, s1_ref, s2_ref,
                   dq_ref, dk_ref, dv_ref, dk_acc, dv_acc):
    place = place_ref[0]
    blocks = q_ref.shape[0] // BLK
    half = ROT_DIMS // 2
    keep = lax.broadcasted_iota(jnp.int32, (BLK, LANES), 1) < HEAD_DIM

    def unturn(g, here):
        g = jnp.where(keep, g, 0.0)
        return (
            g * cs_ref[here, :]
            - pltpu.roll(g, LANES - half, 1) * s1_ref[here, :]
            - pltpu.roll(g, half, 1) * s2_ref[here, :]
        ).astype(BF)

    for i in reversed(range(blocks)):
        here = pl.ds(pl.multiple_of((place ^ i) * BLK, BLK), BLK)
        q = q_ref[here, :]
        do = do_ref[here, :]
        delta = row_form(jnp.sum(do.astype(F32) * full_ref[here, :], axis=1, keepdims=True))
        lse = lse_ref[0, i : i + 1, :]
        dq = None
        for j in range(i + 1):
            k = piece(k_ref, place, j)
            scores = dot_nt(k, q)
            if j == i:
                scores = jnp.where(causal(True), scores, NEG_BIG)
            p = jnp.exp(scores - lse)
            dp = dot_nt(piece(v_ref, place, j), do)
            ds = (p * (dp - delta)).astype(BF)
            dv = dot_nn(p.astype(BF), do)
            dk = dot_nn(ds, q)
            if i == blocks - 1:
                dv_acc[j] = dv
                dk_acc[j] = dk
            else:
                dv_acc[j] += dv
                dk_acc[j] += dk
            part = dot_tn(ds, k)
            dq = part if dq is None else dq + part
        dq_ref[here, :] = unturn(dq * (1.0 / math.sqrt(HEAD_DIM)), here)
        dk_ref[here, :] = unturn(dk_acc[i], here)
        dv_ref[here, :] = dv_acc[i].astype(BF)


def attn_back_call(place, q, k, v, do, full, lse, tables):
    rows, cols = q.shape
    heads = cols // LANES
    col = pl.BlockSpec((rows, LANES), lambda h, p: (0, h))
    one = pl.BlockSpec((rows, LANES), lambda h, p: (0, 0))
    stats = pl.BlockSpec((1, rows // BLK, BLK), lambda h, p: (h, 0, 0))
    return pl.pallas_call(
        attn_back_body,
        grid_spec=pltpu.PrefetchScalarGridSpec(
            num_scalar_prefetch=1,
            grid=(heads,),
            in_specs=[col] * 5 + [stats] + [one] * 3,
            out_specs=[col] * 3,
            scratch_shapes=[pltpu.VMEM((rows // BLK, BLK, LANES), F32)] * 2,
        ),
        out_shape=[jax.ShapeDtypeStruct((rows, cols), BF)] * 3,
        compiler_params=pltpu.CompilerParams(vmem_limit_bytes=48 << 20),
        cost_estimate=pl.CostEstimate(
            flops=heads * rows * rows * 5 * LANES * 4, bytes_accessed=rows * cols * 18, transcendentals=heads * rows * rows // 2
        ),
        name="attention_back",
    )(place, q, k, v, do, full, lse, *tables)


def swap(value, axis):
    return lax.ppermute(value, axis, SWAP)


def gather_tokens(array, core):
    own = lax.dynamic_index_in_dim(array, core, 0, keepdims=False)
    other = lax.dynamic_index_in_dim(array, 1 - core, 0, keepdims=False)
    own_x, own_y = swap(own, "x"), swap(own, "y")
    mate = swap(other, "core")
    mate_y, mate_x = swap(mate, "y"), swap(mate, "x")
    own_xy = swap(own_x, "y")
    mate_xy = swap(mate_y, "x")
    return jnp.concatenate([own, mate, own_x, mate_x, own_y, mate_y, own_xy, mate_xy], axis=0)


def scatter_tokens(array, core):
    part = array.reshape((8, -1) + array.shape[1:])
    add = lambda a, b: a.astype(F32) + b.astype(F32)
    low = lambda a: a.astype(BF)
    mate1, mate3 = swap(part[3], "x"), swap(part[7], "x")
    own2, own3 = swap(part[4], "y"), swap(part[6], "y")
    mate_here, mate_far = add(part[1], mate1), low(add(part[5], mate3))
    own_here, own_far = add(part[0], own2), low(add(part[2], own3))
    mate_sum = low(add(mate_here, swap(mate_far, "y")))
    mate_got = swap(mate_sum, "core").astype(F32)
    own_sum = add(own_here, swap(own_far, "x"))
    return jnp.stack([jnp.where(core == 0, own_sum, mate_got), jnp.where(core == 0, mate_got, own_sum)])


def pick(first, second, core):
    return jnp.where(core == 0, first, second)


def halves_sum(halves, core):
    first, second = halves
    got = swap(pick(second, first, core).astype(BF), "core")
    return (pick(first, second, core) + got.astype(F32)).astype(BF)


def split_device(tokens, segments, positions, gain_attn, shift_attn, gain_mlp, shift_mlp, qkv_weight,
                 query_bias, key_bias, value_bias, dense_weight, expand_weight, expand_bias,
                 contract_weight, output_bias, cotangent):
    seqs, toks, width = tokens.shape
    rows = 8 * toks
    share = qkv_weight.shape[0]
    hidden_share = contract_weight.shape[0]
    n_dp = lax.axis_size("dp")
    heads = width // HEAD_DIM // 4
    band = heads * HEAD_DIM
    core = lax.axis_index("core")
    chip = lax.axis_index("y") * 2 + lax.axis_index("x")
    place = chip * 2 + core
    dp_here = lax.axis_index("dp")
    hop = [((z * 4 + t), (t * 4 + z)) for z in range(4) for t in range(4)]

    qkv_cols = qkv_weight.reshape(share, 3, 4, band).transpose(2, 0, 1, 3).reshape(4, share, 2, 3 * band // 2)
    qkv_cols = qkv_cols.transpose(0, 2, 1, 3).reshape(8, share, 3 * band // 2)
    exp_cols = expand_weight.reshape(share, n_dp, 8, hidden_share).transpose(2, 0, 1, 3)
    exp_cols = exp_cols.reshape(8, share, n_dp * hidden_share)
    cols = lax.all_to_all(jnp.concatenate([qkv_cols, exp_cols], axis=2), CTX_AXES, 0, 0, tiled=True)
    cols = cols.reshape(8 * share, -1)
    qkv_half = lax.all_gather(cols[:, : 3 * band // 2], "dp", axis=0, tiled=True)
    qkv_mate = swap(qkv_half, "core")
    qkv_here = jnp.concatenate([pick(qkv_half, qkv_mate, core), pick(qkv_mate, qkv_half, core)], axis=1)
    w_pad = jnp.pad(qkv_here.reshape(width, 3 * heads, HEAD_DIM), ((0, 0), (0, 0), (0, LANES - HEAD_DIM)))
    w_pad = w_pad.reshape(width, 3 * heads * LANES)

    small = jnp.concatenate([gain_attn, shift_attn, gain_mlp, shift_mlp, query_bias, key_bias, value_bias,
                             output_bias, expand_bias])
    small = lax.all_gather(small, ALL_AXES, axis=0, tiled=False).astype(F32)
    vectors = [small[:, n * share : (n + 1) * share].reshape(width) for n in range(8)]
    vecs = jnp.stack(vectors[:4])
    out_bias = vectors[7]
    biases = jnp.stack([lax.dynamic_slice(v, (chip * band,), (band,)) for v in vectors[4:7]])
    b_pad = jnp.pad(biases.reshape(3 * heads, HEAD_DIM), ((0, 0), (0, LANES - HEAD_DIM))).reshape(1, -1)
    exp_bias = small[:, 8 * share :].reshape(n_dp, 4, 2, hidden_share)
    exp_bias = lax.dynamic_index_in_dim(exp_bias, chip, 1, keepdims=False).transpose(1, 0, 2).reshape(1, -1)

    marks = lax.all_gather(jnp.stack([segments, positions]), CTX_AXES, axis=0, tiled=False)
    marks = lax.dynamic_index_in_dim(marks, core, 2, keepdims=False)
    marks = jnp.take(marks, place ^ jnp.arange(8), axis=0)
    seg, pos = marks[:, 0].reshape(rows, 1), marks[:, 1].reshape(rows, 1)
    lane = jnp.arange(LANES)[None, :]
    half = ROT_DIMS // 2
    inverse = jnp.exp((lane % half).astype(F32) * (-2.0 * math.log(10000.0) / ROT_DIMS))
    angle = pos.astype(F32) * inverse
    cosine, sine = jnp.cos(angle), jnp.sin(angle)
    table_c = jnp.where(lane < ROT_DIMS, cosine, jnp.where(lane < HEAD_DIM, 1.0, 0.0))
    table_1 = jnp.where(lane < half, -sine, 0.0)
    table_2 = jnp.where((lane >= half) & (lane < ROT_DIMS), sine, 0.0)
    docs = 16
    in_doc = (lane >= HEAD_DIM) & (lane < HEAD_DIM + docs)
    same = in_doc & (lane - HEAD_DIM == seg)
    mark_q = jnp.where(same, 1.0, 0.0)
    mark_k = jnp.where(in_doc & ~same, NEG_BIG, 0.0)

    x_rows = gather_tokens(tokens, core)
    exp_half = lax.all_gather(cols[:, 3 * band // 2 :], "dp", axis=0, tiled=True)
    dense_moved = lax.ppermute(dense_weight, ("dp", "y", "x"), hop)
    low_rows = lax.all_gather(jnp.concatenate([contract_weight, dense_moved], axis=0), "dp", axis=0, tiled=False)
    dy_rows = gather_tokens(cotangent, core)

    attn_in, mlp_in, q, k, v = pre_call(x_rows, vecs, w_pad, b_pad, (table_c, table_1, table_2, mark_q, mark_k))
    place_arr = place.reshape(1).astype(jnp.int32)
    mixed, mixed_full, lse = attn_call(place_arr, q, k, v)

    exp_mate = swap(exp_half, "core")
    w_exp = jnp.concatenate([pick(exp_half, exp_mate, core), pick(exp_mate, exp_half, core)], axis=1)
    low_mate = swap(low_rows, "core")
    low_both = jnp.stack([pick(low_rows, low_mate, core), pick(low_mate, low_rows, core)])
    w_con = low_both[:, :, :hidden_share].reshape(2 * n_dp * hidden_share, width)
    w_den = low_both[:, :, hidden_share:].transpose(1, 0, 2, 3).reshape(heads, HEAD_DIM, width)
    w_den = jnp.pad(w_den, ((0, 0), (0, LANES - HEAD_DIM), (0, 0))).reshape(heads * LANES, width)

    hidden_pre = dot_nn(mlp_in, w_exp) + exp_bias
    hidden = exact_gelu(hidden_pre).astype(BF)
    out_part = (dot_nn(mixed, w_den) + dot_nn(hidden, w_con)).astype(BF)
    out_sum = scatter_tokens(out_part, core)
    output = (tokens.astype(F32) + out_sum + out_bias).astype(BF)

    d_hidden = dot_nt(dy_rows, w_con)
    _, gelu_pull = jax.vjp(exact_gelu, hidden_pre)
    d_hidden_pre = gelu_pull(d_hidden)[0].astype(BF)
    d_mixed = dot_nt(dy_rows, w_den).astype(BF)
    d_con = dot_tn(hidden, dy_rows)
    d_exp = dot_tn(mlp_in, d_hidden_pre)
    d_den = dot_tn(mixed, dy_rows)
    half_rows = n_dp * hidden_share
    con_sum = halves_sum((d_con[:half_rows], d_con[half_rows:]), core).reshape(n_dp, hidden_share, width)
    d_den = d_den.reshape(heads, LANES, width)[:, :HEAD_DIM].reshape(4, 2, share, width)
    den_sum = halves_sum((d_den[:, 0], d_den[:, 1]), core)
    exp_sum = halves_sum((d_exp[:, :half_rows], d_exp[:, half_rows:]), core)
    low_sum = lax.psum_scatter(jnp.concatenate([con_sum, den_sum], axis=1), "dp", scatter_dimension=0, tiled=False)
    grad_contract = low_sum[:hidden_share].astype(F32)
    grad_dense = lax.ppermute(low_sum[hidden_share:], ("dp", "y", "x"), hop).astype(F32)
    exp_own = lax.psum_scatter(exp_sum, "dp", scatter_dimension=0, tiled=True)
    exp_own = lax.all_to_all(exp_own.reshape(8, share, half_rows), CTX_AXES, 0, 0, tiled=True)
    grad_expand = exp_own.reshape(8, share, n_dp, hidden_share).transpose(1, 2, 0, 3).reshape(share, -1).astype(F32)

    dq, dk, dv = attn_back_call(place_arr, q, k, v, d_mixed, mixed_full, lse, (table_c, table_1, table_2))
    d_packed = jnp.concatenate([dq, dk, dv], axis=1)
    e_attn = dot_nt(d_packed, w_pad)
    e_mlp = dot_nt(d_hidden_pre, w_exp)
    xf = x_rows.astype(F32)
    centre = xf - jnp.mean(xf, axis=1, keepdims=True)
    xhat = centre * lax.rsqrt(jnp.mean(centre * centre, axis=1, keepdims=True) + EPSILON)
    d_gain_attn = jnp.sum(e_attn * xhat, axis=0)
    d_shift_attn = jnp.sum(e_attn, axis=0)
    d_gain_mlp = jnp.sum(e_mlp * xhat, axis=0)
    d_shift_mlp = jnp.sum(e_mlp, axis=0)
    pull = (e_attn * vecs[0] + e_mlp * vecs[2]).astype(BF)
    ge = scatter_tokens(pull, core)
    own = tokens.astype(F32)
    own_c = own - jnp.mean(own, axis=2, keepdims=True)
    own_r = lax.rsqrt(jnp.mean(own_c * own_c, axis=2, keepdims=True) + EPSILON)
    own_h = own_c * own_r
    back = own_r * (ge - jnp.mean(ge, axis=2, keepdims=True) - own_h * jnp.mean(ge * own_h, axis=2, keepdims=True))
    input_grad = (cotangent.astype(F32) + back).astype(BF)

    d_qkv = dot_tn(attn_in, d_packed).reshape(width, 3 * heads, LANES)[:, :, :HEAD_DIM].reshape(width, 3 * band)
    qkv_sum = halves_sum((d_qkv[:, : 3 * band // 2], d_qkv[:, 3 * band // 2 :]), core)
    qkv_own = lax.psum_scatter(qkv_sum, "dp", scatter_dimension=0, tiled=True)
    qkv_own = lax.all_to_all(qkv_own.reshape(8, share, 3 * band // 2), CTX_AXES, 0, 0, tiled=True)
    grad_qkv = qkv_own.reshape(4, 2, share, 3 * band // 2).transpose(0, 2, 1, 3).reshape(4, share, 3, band)
    grad_qkv = grad_qkv.transpose(1, 2, 0, 3).reshape(share, -1).astype(F32)

    d_bias = jnp.sum(d_packed.astype(F32), axis=0).reshape(3, heads, LANES)[:, :, :HEAD_DIM].reshape(3, band)
    d_exp_bias = jnp.sum(d_hidden_pre.astype(F32), axis=0).reshape(2, n_dp, hidden_share).transpose(1, 0, 2)
    d_out_bias = jnp.sum(cotangent.astype(F32), axis=(0, 1))
    lines = [v.reshape(-1, share) for v in (d_gain_attn, d_shift_attn, d_gain_mlp, d_shift_mlp)]
    for n in range(3):
        line = lax.dynamic_update_slice(jnp.zeros((width,), F32), d_bias[n], (chip * band,))
        lines.append(line.reshape(-1, share))
    lines.append(d_out_bias.reshape(-1, share))
    line = jnp.zeros((n_dp, 4, 2, hidden_share), F32)
    line = lax.dynamic_update_slice(line, d_exp_bias[:, None], (0, chip, 0, 0))
    lines.append(line.reshape(-1, hidden_share))
    small_grads = lax.all_to_all(jnp.concatenate(lines, axis=1), ALL_AXES, 0, 0, tiled=True)
    small_grads = jnp.sum(small_grads, axis=0)
    part = [small_grads[n * share : (n + 1) * share] for n in range(8)]
    return (output, input_grad, part[0], part[1], part[2], part[3], grad_qkv, part[4], part[5], part[6],
            grad_dense, grad_expand, small_grads[8 * share :], grad_contract, part[7])


def general_plan(mesh):
    placed = (
        P("dp", "ctx", None),
        P("dp", "ctx"),
        P("dp", "ctx"),
        P(("dp", "ctx")),
        P(("dp", "ctx")),
        P(("dp", "ctx")),
        P(("dp", "ctx")),
        P(("dp", "ctx"), None),
        P(("dp", "ctx")),
        P(("dp", "ctx")),
        P(("dp", "ctx")),
        P(("dp", "ctx"), None),
        P(("dp", "ctx"), None),
        P(("dp", "ctx")),
        P(("dp", "ctx"), None),
        P(("dp", "ctx")),
        P("dp", "ctx", None),
    )
    return jax.shard_map(
        per_device,
        mesh=mesh,
        in_specs=placed,
        out_specs=(
            P("dp", "ctx", None),
            P("dp", "ctx", None),
            P(("dp", "ctx")),
            P(("dp", "ctx")),
            P(("dp", "ctx")),
            P(("dp", "ctx")),
            P(("dp", "ctx"), None),
            P(("dp", "ctx")),
            P(("dp", "ctx")),
            P(("dp", "ctx")),
            P(("dp", "ctx"), None),
            P(("dp", "ctx"), None),
            P(("dp", "ctx")),
            P(("dp", "ctx"), None),
            P(("dp", "ctx")),
        ),
        check_vma=False,
    )


def split_plan(mesh):
    fine = Mesh(mesh.devices.reshape(mesh.shape["dp"], 2, 2, 2), ALL_AXES)
    tok = P("dp", CTX_AXES, None)
    mark = P("dp", CTX_AXES)
    vec = P(ALL_AXES)
    mat = P(ALL_AXES, None)
    return jax.shard_map(
        split_device,
        mesh=fine,
        in_specs=(tok, mark, mark, vec, vec, vec, vec, mat, vec, vec, vec, mat, mat, vec, mat, vec, tok),
        out_specs=(tok, tok, vec, vec, vec, vec, mat, vec, vec, vec, mat, mat, vec, mat, vec),
        check_vma=False,
    )


def solution(mesh):
    if mesh.shape["ctx"] == 8 and mesh.shape["dp"] == 4:
        return split_plan(mesh)
    return general_plan(mesh)
```

```python
import math

import jax
import jax.numpy as jnp
from jax import lax
from jax.experimental import pallas as pl
from jax.experimental.pallas import tpu as pltpu
from jax.sharding import Mesh, PartitionSpec as P

HEAD_DIM = 64
ROT_DIMS = 16


NEG_BIG = -1e30
EPSILON = 1e-05


def from_behind(value, axis, by):
    size = lax.axis_size(axis)
    pairs = [(i, i + by) for i in range(size) if 0 <= i + by < size]
    return lax.ppermute(value, axis, pairs)


def shifted(value, axis, by):
    size = lax.axis_size(axis)
    return lax.ppermute(value, axis, [(i, (i + by) % size) for i in range(size)])


def normalize(values, gain_vec, shift_vec):
    centre = values - jnp.mean(values, axis=-1, keepdims=True)
    spread = jnp.mean(centre * centre, axis=-1, keepdims=True)
    return centre * lax.rsqrt(spread + EPSILON) * gain_vec + shift_vec


def angles(positions):
    ladder = jnp.arange(ROT_DIMS // 2).astype(jnp.float32)
    inverse = jnp.exp(ladder * (-2.0 * math.log(10000.0) / ROT_DIMS))
    phase_angle = positions.astype(jnp.float32)[..., None] * inverse
    return (jnp.cos(phase_angle)[..., None, :], jnp.sin(phase_angle)[..., None, :])


def rotate(field_in, cosine, sine_part):
    half_dims = ROT_DIMS // 2
    lower_half = field_in[..., :half_dims]
    upper_half = field_in[..., half_dims:ROT_DIMS]
    remainder = field_in[..., ROT_DIMS:]
    return jnp.concatenate(
        [
            lower_half * cosine - upper_half * sine_part,
            upper_half * cosine + lower_half * sine_part,
            remainder,
        ],
        axis=-1,
    )


def exact_gelu(pre_act):
    return jax.nn.gelu(pre_act, approximate=False)


def contract_last(left_side, right_side):
    return lax.dot_general(
        left_side, right_side, (((1,), (1,)), ((), ())), preferred_element_type=jnp.float32
    )


def visible(query_seg, query_start, key_seg, key_start):
    query_index = query_start + jnp.arange(query_seg.shape[1])
    key_index = key_start + jnp.arange(key_seg.shape[1])
    allowed = (key_index[None, None, :] <= query_index[None, :, None]) & (
        key_seg[:, None, :] == query_seg[:, :, None]
    )
    return allowed[:, :, None, :]


def pair_grads(query_side, stats_side, query_start, key_side, key_start):
    query_rows, d_mixed, query_seg = query_side
    log_total, delta_rows = stats_side
    key_rows, value_rows, key_seg = key_side
    score_scale = 1.0 / math.sqrt(HEAD_DIM)
    allowed = visible(query_seg, query_start, key_seg, key_start)
    scores = (
        jnp.einsum("bqhd,bkhd->bqhk", query_rows, key_rows, preferred_element_type=jnp.float32)
        * score_scale
    )
    prob_rows = jnp.where(
        allowed, jnp.exp(jnp.where(allowed, scores - log_total[..., None], NEG_BIG)), 0.0
    )
    d_prob = jnp.einsum("bqhd,bkhd->bqhk", d_mixed, value_rows, preferred_element_type=jnp.float32)
    d_scores = (prob_rows * (d_prob - delta_rows[..., None])).astype(jnp.bfloat16)
    d_query = (
        jnp.einsum("bqhk,bkhd->bqhd", d_scores, key_rows, preferred_element_type=jnp.float32)
        * score_scale
    )
    d_key = (
        jnp.einsum("bqhk,bqhd->bkhd", d_scores, query_rows, preferred_element_type=jnp.float32)
        * score_scale
    )
    d_value = jnp.einsum(
        "bqhk,bqhd->bkhd",
        prob_rows.astype(jnp.bfloat16),
        d_mixed,
        preferred_element_type=jnp.float32,
    )
    return (d_query, d_key, d_value)


def per_device(
    tokens,
    segments,
    positions,
    gain_attn,
    shift_attn,
    gain_mlp,
    shift_mlp,
    qkv_weight,
    query_bias,
    key_bias,
    value_bias,
    dense_weight,
    expand_weight,
    expand_bias,
    contract_weight,
    output_bias,
    cotangent,
):
    shards = (
        gain_attn,
        shift_attn,
        gain_mlp,
        shift_mlp,
        qkv_weight,
        query_bias,
        key_bias,
        value_bias,
        dense_weight,
        expand_weight,
        expand_bias,
        contract_weight,
        output_bias,
    )
    gathered = (
        lax.all_gather(shards[0], ("dp", "ctx"), axis=0, tiled=True),
        lax.all_gather(shards[1], ("dp", "ctx"), axis=0, tiled=True),
        lax.all_gather(shards[2], ("dp", "ctx"), axis=0, tiled=True),
        lax.all_gather(shards[3], ("dp", "ctx"), axis=0, tiled=True),
        lax.all_gather(shards[4], ("dp", "ctx"), axis=0, tiled=True),
        lax.all_gather(shards[5], ("dp", "ctx"), axis=0, tiled=True),
        lax.all_gather(shards[6], ("dp", "ctx"), axis=0, tiled=True),
        lax.all_gather(shards[7], ("dp", "ctx"), axis=0, tiled=True),
        lax.all_gather(shards[8], ("dp", "ctx"), axis=0, tiled=True),
        lax.all_gather(shards[9], ("dp", "ctx"), axis=0, tiled=True),
        lax.all_gather(shards[10], ("dp", "ctx"), axis=0, tiled=True),
        lax.all_gather(shards[11], ("dp", "ctx"), axis=0, tiled=True),
        lax.all_gather(shards[12], ("dp", "ctx"), axis=0, tiled=True),
    )
    seq_count, tok_count, model_width = tokens.shape
    row_count = seq_count * tok_count
    head_count = model_width // HEAD_DIM
    heads_shape = (seq_count, tok_count, head_count, HEAD_DIM)
    flat_shape = (seq_count, tok_count, model_width)
    full_gain_attn = gathered[0].astype(jnp.float32)
    full_shift_attn = gathered[1].astype(jnp.float32)
    full_gain_mlp = gathered[2].astype(jnp.float32)
    full_shift_mlp = gathered[3].astype(jnp.float32)
    full_query_bias = gathered[5].astype(jnp.float32)
    full_key_bias = gathered[6].astype(jnp.float32)
    full_value_bias = gathered[7].astype(jnp.float32)
    full_expand_bias = gathered[10].astype(jnp.float32)
    full_output_bias = gathered[12].astype(jnp.float32)
    flat_in = tokens.reshape(row_count, model_width).astype(jnp.float32)

    def both_norms(values, gain_one, shift_one, gain_two, shift_two):
        return (normalize(values, gain_one, shift_one), normalize(values, gain_two, shift_two))

    (norm_attn, norm_mlp), norm_pull = jax.vjp(
        both_norms, flat_in, full_gain_attn, full_shift_attn, full_gain_mlp, full_shift_mlp
    )
    attn_in = norm_attn.astype(jnp.bfloat16)
    mlp_in = norm_mlp.astype(jnp.bfloat16)
    packed = jnp.dot(attn_in, gathered[4], preferred_element_type=jnp.float32)
    query_raw = (packed[:, :model_width] + full_query_bias).reshape(heads_shape)
    key_raw = (packed[:, model_width : 2 * model_width] + full_key_bias).reshape(heads_shape)
    value_rows = (
        (packed[:, 2 * model_width :] + full_value_bias).astype(jnp.bfloat16).reshape(heads_shape)
    )
    cosine, sine_part = angles(positions)

    def turn_heads(field_in):
        return rotate(field_in, cosine, sine_part)

    query_turned, query_pull = jax.vjp(turn_heads, query_raw)
    key_turned, key_pull = jax.vjp(turn_heads, key_raw)
    query_rows = query_turned.astype(jnp.bfloat16)
    key_rows = key_turned.astype(jnp.bfloat16)
    key_flat = key_rows.reshape(flat_shape)
    value_flat = value_rows.reshape(flat_shape)
    ctx_count = lax.axis_size("ctx")
    ctx_index = lax.axis_index("ctx")
    here_start = ctx_index * tok_count
    score_scale = 1.0 / math.sqrt(HEAD_DIM)
    start_max = jnp.full((seq_count, tok_count, head_count), NEG_BIG, jnp.float32)
    key_blk = lax.all_gather(key_flat, "ctx", axis=1, tiled=True)
    value_blk = lax.all_gather(value_flat, "ctx", axis=1, tiled=True)
    seg_blk = lax.all_gather(segments, "ctx", axis=1, tiled=True)
    block_len = key_blk.shape[1]
    key_blk = key_blk.reshape(seq_count, block_len, head_count, HEAD_DIM)
    value_blk = value_blk.reshape(seq_count, block_len, head_count, HEAD_DIM)
    allowed = visible(segments, here_start, seg_blk, jnp.int32(0))
    scores = (
        jnp.einsum("bqhd,bkhd->bqhk", query_rows, key_blk, preferred_element_type=jnp.float32)
        * score_scale
    )
    scores = jnp.where(allowed, scores, NEG_BIG)
    new_max = jnp.maximum(start_max, jnp.max(scores, axis=-1))
    weights = jnp.where(allowed, jnp.exp(scores - new_max[..., None]), 0.0)
    new_sum = jnp.sum(weights, axis=-1)
    new_acc = jnp.einsum(
        "bqhk,bkhd->bqhd",
        weights.astype(jnp.bfloat16),
        value_blk,
        preferred_element_type=jnp.float32,
    )
    log_total = new_max + jnp.log(new_sum)
    mixed_full = new_acc / new_sum[..., None]
    mixed_rows = mixed_full.astype(jnp.bfloat16).reshape(row_count, model_width)
    hidden_pre = jnp.dot(mlp_in, gathered[9], preferred_element_type=jnp.float32) + full_expand_bias
    hidden_act, gelu_pull = jax.vjp(exact_gelu, hidden_pre)
    hidden_rows = hidden_act.astype(jnp.bfloat16)
    result = (
        flat_in
        + jnp.dot(mixed_rows, gathered[8], preferred_element_type=jnp.float32)
        + jnp.dot(hidden_rows, gathered[11], preferred_element_type=jnp.float32)
        + full_output_bias
    )
    output = result.astype(jnp.bfloat16).reshape(flat_shape)
    regathered = (
        lax.all_gather(shards[0], ("dp", "ctx"), axis=0, tiled=True),
        lax.all_gather(shards[1], ("dp", "ctx"), axis=0, tiled=True),
        lax.all_gather(shards[2], ("dp", "ctx"), axis=0, tiled=True),
        lax.all_gather(shards[3], ("dp", "ctx"), axis=0, tiled=True),
        lax.all_gather(shards[4], ("dp", "ctx"), axis=0, tiled=True),
        lax.all_gather(shards[5], ("dp", "ctx"), axis=0, tiled=True),
        lax.all_gather(shards[6], ("dp", "ctx"), axis=0, tiled=True),
        lax.all_gather(shards[7], ("dp", "ctx"), axis=0, tiled=True),
        lax.all_gather(shards[8], ("dp", "ctx"), axis=0, tiled=True),
        lax.all_gather(shards[9], ("dp", "ctx"), axis=0, tiled=True),
        lax.all_gather(shards[10], ("dp", "ctx"), axis=0, tiled=True),
        lax.all_gather(shards[11], ("dp", "ctx"), axis=0, tiled=True),
        lax.all_gather(shards[12], ("dp", "ctx"), axis=0, tiled=True),
    )
    back_qkv = regathered[4]
    back_dense = regathered[8]
    back_expand = regathered[9]
    back_contract = regathered[11]
    grad_rows = cotangent.reshape(row_count, model_width)
    grad_full = grad_rows.astype(jnp.float32)
    d_output_bias = jnp.sum(grad_full, axis=0)
    d_contract = jnp.einsum("rf,rd->fd", hidden_rows, grad_rows, preferred_element_type=jnp.float32)
    d_hidden = contract_last(grad_rows, back_contract)
    d_hidden_pre = gelu_pull(d_hidden)[0].astype(jnp.bfloat16)
    d_expand_bias = jnp.sum(d_hidden_pre.astype(jnp.float32), axis=0)
    d_expand = jnp.einsum("rd,rf->df", mlp_in, d_hidden_pre, preferred_element_type=jnp.float32)
    d_norm_mlp = contract_last(d_hidden_pre, back_expand)
    d_dense = jnp.einsum("ri,rd->id", mixed_rows, grad_rows, preferred_element_type=jnp.float32)
    d_mixed = contract_last(grad_rows, back_dense).astype(jnp.bfloat16).reshape(heads_shape)
    delta_rows = jnp.sum(d_mixed.astype(jnp.float32) * mixed_full, axis=-1)
    query_side = (query_rows, d_mixed, segments)
    stats_side = (log_total, delta_rows)

    def carry_step(step_num, loop_state):
        key_block, grad_block, d_query_acc = loop_state
        owner_dev = (ctx_index - step_num) % ctx_count
        key_side = (
            key_block[0].reshape(heads_shape),
            key_block[1].reshape(heads_shape),
            key_block[2],
        )
        d_query_part, d_key_part, d_value_part = pair_grads(
            query_side, stats_side, here_start, key_side, owner_dev * tok_count
        )
        grad_block = (
            grad_block[0] + d_key_part.reshape(flat_shape),
            grad_block[1] + d_value_part.reshape(flat_shape),
        )
        key_block = from_behind((key_block[0], key_block[1], key_block[2]), "ctx", 1)
        grad_block = (
            shifted(grad_block[0].astype(jnp.bfloat16), "ctx", 1).astype(jnp.float32),
            shifted(grad_block[1].astype(jnp.bfloat16), "ctx", 1).astype(jnp.float32),
        )
        return (key_block, grad_block, d_query_acc + d_query_part)

    zero_flat = jnp.zeros(flat_shape, jnp.float32)
    final_state = lax.fori_loop(
        0,
        ctx_count,
        carry_step,
        (
            (key_flat, value_flat, segments),
            (zero_flat, zero_flat),
            jnp.zeros(heads_shape, jnp.float32),
        ),
    )
    d_query_sum = final_state[2]
    d_key_sum = final_state[1][0].reshape(heads_shape)
    d_value_sum = final_state[1][1].reshape(heads_shape)
    d_query_raw = query_pull(d_query_sum)[0].astype(jnp.bfloat16).reshape(row_count, model_width)
    d_key_raw = key_pull(d_key_sum)[0].astype(jnp.bfloat16).reshape(row_count, model_width)
    d_value_low = d_value_sum.astype(jnp.bfloat16).reshape(row_count, model_width)
    d_query_bias = jnp.sum(d_query_raw.astype(jnp.float32), axis=0)
    d_key_bias = jnp.sum(d_key_raw.astype(jnp.float32), axis=0)
    d_value_bias = jnp.sum(d_value_low.astype(jnp.float32), axis=0)
    d_packed = jnp.concatenate([d_query_raw, d_key_raw, d_value_low], axis=1)
    d_qkv = jnp.einsum("rd,rp->dp", attn_in, d_packed, preferred_element_type=jnp.float32)
    d_norm_attn = contract_last(d_packed, back_qkv)
    d_flat, d_gain_attn, d_shift_attn, d_gain_mlp, d_shift_mlp = norm_pull(
        (d_norm_attn, d_norm_mlp)
    )
    input_grad = (grad_full + d_flat).astype(jnp.bfloat16).reshape(flat_shape)
    owned_grads = (
        lax.psum_scatter(d_gain_attn, ("dp", "ctx"), scatter_dimension=0, tiled=True),
        lax.psum_scatter(d_shift_attn, ("dp", "ctx"), scatter_dimension=0, tiled=True),
        lax.psum_scatter(d_gain_mlp, ("dp", "ctx"), scatter_dimension=0, tiled=True),
        lax.psum_scatter(d_shift_mlp, ("dp", "ctx"), scatter_dimension=0, tiled=True),
        lax.psum_scatter(d_qkv, ("dp", "ctx"), scatter_dimension=0, tiled=True),
        lax.psum_scatter(d_query_bias, ("dp", "ctx"), scatter_dimension=0, tiled=True),
        lax.psum_scatter(d_key_bias, ("dp", "ctx"), scatter_dimension=0, tiled=True),
        lax.psum_scatter(d_value_bias, ("dp", "ctx"), scatter_dimension=0, tiled=True),
        lax.psum_scatter(d_dense, ("dp", "ctx"), scatter_dimension=0, tiled=True),
        lax.psum_scatter(d_expand, ("dp", "ctx"), scatter_dimension=0, tiled=True),
        lax.psum_scatter(d_expand_bias, ("dp", "ctx"), scatter_dimension=0, tiled=True),
        lax.psum_scatter(d_contract, ("dp", "ctx"), scatter_dimension=0, tiled=True),
        lax.psum_scatter(d_output_bias, ("dp", "ctx"), scatter_dimension=0, tiled=True),
    )
    return (
        output,
        input_grad,
        owned_grads[0],
        owned_grads[1],
        owned_grads[2],
        owned_grads[3],
        owned_grads[4],
        owned_grads[5],
        owned_grads[6],
        owned_grads[7],
        owned_grads[8],
        owned_grads[9],
        owned_grads[10],
        owned_grads[11],
        owned_grads[12],
    )


LANES = 128
BLK = 256
ROWS = 512
BF = jnp.bfloat16
F32 = jnp.float32
SWAP = [(0, 1), (1, 0)]
CTX_AXES = ("y", "x", "core")
ALL_AXES = ("dp", "y", "x", "core")


def dot_nn(a, b):
    return lax.dot_general(a, b, (((1,), (0,)), ((), ())), preferred_element_type=F32)


def dot_nt(a, b):
    return lax.dot_general(a, b, (((1,), (1,)), ((), ())), preferred_element_type=F32)


def dot_tn(a, b):
    return lax.dot_general(a, b, (((0,), (0,)), ((), ())), preferred_element_type=F32)


def whole(shape):
    return pl.BlockSpec(shape, lambda *ids: (0,) * len(shape))


def pre_body(x_ref, vec_ref, w_ref, b_ref, cs_ref, s1_ref, s2_ref, eq_ref, ek_ref,
             attn_ref, mlp_ref, q_ref, k_ref, v_ref):
    x = x_ref[...].astype(F32)
    centre = x - jnp.mean(x, axis=1, keepdims=True)
    spread = jnp.mean(centre * centre, axis=1, keepdims=True)
    xhat = centre * lax.rsqrt(spread + EPSILON)
    attn_in = (xhat * vec_ref[0:1, :] + vec_ref[1:2, :]).astype(BF)
    attn_ref[...] = attn_in
    mlp_ref[...] = (xhat * vec_ref[2:3, :] + vec_ref[3:4, :]).astype(BF)
    packed = dot_nn(attn_in, w_ref[...]) + b_ref[...]
    heads = w_ref.shape[1] // (3 * LANES)
    wide = heads * LANES
    cs, s1, s2 = cs_ref[...], s1_ref[...], s2_ref[...]
    half = ROT_DIMS // 2

    def turn(u):
        return u * cs + pltpu.roll(u, LANES - half, 1) * s1 + pltpu.roll(u, half, 1) * s2

    for h in range(heads):
        cols = slice(h * LANES, (h + 1) * LANES)
        q = turn(packed[:, h * LANES : (h + 1) * LANES])
        q_ref[:, cols] = (q.astype(BF).astype(F32) * (1.0 / math.sqrt(HEAD_DIM)) + eq_ref[...]).astype(BF)
        k = turn(packed[:, wide + h * LANES : wide + (h + 1) * LANES])
        k_ref[:, cols] = (k + ek_ref[...]).astype(BF)
        v_ref[:, cols] = packed[:, 2 * wide + h * LANES : 2 * wide + (h + 1) * LANES].astype(BF)


def pre_call(x, vecs, w_pad, b_pad, tables):
    rows, width = x.shape
    cols = w_pad.shape[1]
    third = cols // 3
    row_block = lambda n: pl.BlockSpec((ROWS, n), lambda i: (i, 0))
    return pl.pallas_call(
        pre_body,
        grid=(rows // ROWS,),
        in_specs=[row_block(width), whole(vecs.shape), whole(w_pad.shape), whole(b_pad.shape)]
        + [row_block(LANES)] * 5,
        out_specs=[row_block(width)] * 2 + [row_block(third)] * 3,
        out_shape=[jax.ShapeDtypeStruct((rows, width), BF)] * 2
        + [jax.ShapeDtypeStruct((rows, third), BF)] * 3,
        compiler_params=pltpu.CompilerParams(vmem_limit_bytes=56 << 20),
        cost_estimate=pl.CostEstimate(
            flops=2 * rows * width * cols, bytes_accessed=rows * (width * 6 + cols * 2 + LANES * 20), transcendentals=0
        ),
        name="norm_qkv",
    )(x, vecs, w_pad, b_pad, *tables)


def piece(ref, j):
    return ref[j * BLK : (j + 1) * BLK, :]


def causal(transposed):
    rows = lax.broadcasted_iota(jnp.int32, (BLK, BLK), 0)
    cols = lax.broadcasted_iota(jnp.int32, (BLK, BLK), 1)
    return cols >= rows if transposed else rows >= cols


def row_form(column):
    return jnp.transpose(jnp.broadcast_to(column, (BLK, LANES)))[0:1, :]


def attn_body(q_ref, k_ref, v_ref, mixed_ref, full_ref, lse_ref):
    for i in range(q_ref.shape[0] // BLK):
        q = piece(q_ref, i)
        scores = [dot_nt(q, piece(k_ref, j)) for j in range(i + 1)]
        scores[i] = jnp.where(causal(False), scores[i], NEG_BIG)
        top = scores[0]
        for s in scores[1:]:
            top = jnp.maximum(top, s)
        top = jnp.max(top, axis=1, keepdims=True)
        acc = None
        total = None
        for j in range(i + 1):
            p = jnp.exp(scores[j] - top)
            total = p if total is None else total + p
            part = dot_nn(p.astype(BF), piece(v_ref, j))
            acc = part if acc is None else acc + part
        total = jnp.sum(total, axis=1, keepdims=True)
        mixed = acc / total
        here = slice(i * BLK, (i + 1) * BLK)
        full_ref[here, :] = mixed
        mixed_ref[here, :] = mixed.astype(BF)
        lse_ref[0, i : i + 1, :] = row_form(top + jnp.log(total))


def attn_call(q, k, v):
    rows, cols = q.shape
    heads = cols // LANES
    col = pl.BlockSpec((rows, LANES), lambda h: (0, h))
    stats = pl.BlockSpec((1, rows // BLK, BLK), lambda h: (h, 0, 0))
    return pl.pallas_call(
        attn_body,
        grid=(heads,),
        in_specs=[col] * 3,
        out_specs=[col, col, stats],
        out_shape=[
            jax.ShapeDtypeStruct((rows, cols), BF),
            jax.ShapeDtypeStruct((rows, cols), F32),
            jax.ShapeDtypeStruct((heads, rows // BLK, BLK), F32),
        ],
        compiler_params=pltpu.CompilerParams(vmem_limit_bytes=48 << 20),
        cost_estimate=pl.CostEstimate(
            flops=heads * rows * rows * 2 * LANES * 4, bytes_accessed=rows * cols * 12, transcendentals=heads * rows * rows // 2
        ),
        name="attention",
    )(q, k, v)


def attn_back_body(q_ref, k_ref, v_ref, do_ref, full_ref, lse_ref, cs_ref, s1_ref, s2_ref,
                   dq_ref, dk_ref, dv_ref, dk_acc, dv_acc):
    blocks = q_ref.shape[0] // BLK
    half = ROT_DIMS // 2
    keep = lax.broadcasted_iota(jnp.int32, (BLK, LANES), 1) < HEAD_DIM

    def unturn(g, here):
        g = jnp.where(keep, g, 0.0)
        return (
            g * cs_ref[here, :]
            - pltpu.roll(g, LANES - half, 1) * s1_ref[here, :]
            - pltpu.roll(g, half, 1) * s2_ref[here, :]
        ).astype(BF)

    for i in reversed(range(blocks)):
        here = slice(i * BLK, (i + 1) * BLK)
        q = q_ref[here, :]
        do = do_ref[here, :]
        delta = row_form(jnp.sum(do.astype(F32) * full_ref[here, :], axis=1, keepdims=True))
        lse = lse_ref[0, i : i + 1, :]
        dq = None
        for j in range(i + 1):
            k = piece(k_ref, j)
            scores = dot_nt(k, q)
            if j == i:
                scores = jnp.where(causal(True), scores, NEG_BIG)
            p = jnp.exp(scores - lse)
            dp = dot_nt(piece(v_ref, j), do)
            ds = (p * (dp - delta)).astype(BF)
            dv = dot_nn(p.astype(BF), do)
            dk = dot_nn(ds, q)
            if i == blocks - 1:
                dv_acc[j] = dv
                dk_acc[j] = dk
            else:
                dv_acc[j] += dv
                dk_acc[j] += dk
            part = dot_tn(ds, k)
            dq = part if dq is None else dq + part
        dq_ref[here, :] = unturn(dq * (1.0 / math.sqrt(HEAD_DIM)), here)
        dk_ref[here, :] = unturn(dk_acc[i], here)
        dv_ref[here, :] = dv_acc[i].astype(BF)


def attn_back_call(q, k, v, do, full, lse, tables):
    rows, cols = q.shape
    heads = cols // LANES
    col = pl.BlockSpec((rows, LANES), lambda h: (0, h))
    one = pl.BlockSpec((rows, LANES), lambda h: (0, 0))
    stats = pl.BlockSpec((1, rows // BLK, BLK), lambda h: (h, 0, 0))
    return pl.pallas_call(
        attn_back_body,
        grid=(heads,),
        in_specs=[col] * 5 + [stats] + [one] * 3,
        out_specs=[col] * 3,
        scratch_shapes=[pltpu.VMEM((rows // BLK, BLK, LANES), F32)] * 2,
        out_shape=[jax.ShapeDtypeStruct((rows, cols), BF)] * 3,
        compiler_params=pltpu.CompilerParams(vmem_limit_bytes=48 << 20),
        cost_estimate=pl.CostEstimate(
            flops=heads * rows * rows * 5 * LANES * 4, bytes_accessed=rows * cols * 18, transcendentals=heads * rows * rows // 2
        ),
        name="attention_back",
    )(q, k, v, do, full, lse, *tables)


def beside(one_ref, two_ref, axis):
    return jnp.concatenate([one_ref[...], two_ref[...]], axis=axis)


def mlp_body(m_ref, mixed_ref, we1_ref, we2_ref, be_ref, wd_ref, wc1_ref, wc2_ref, hid_ref, slope_ref, out_ref):
    pre = dot_nn(m_ref[...], beside(we1_ref, we2_ref, 1)) + be_ref[...]
    share = 0.5 * (1.0 + lax.erf(pre * math.sqrt(0.5)))
    hidden = (pre * share).astype(BF)
    hid_ref[...] = hidden
    slope_ref[...] = (share + pre * (jnp.exp(-0.5 * pre * pre) * (1.0 / math.sqrt(2.0 * math.pi)))).astype(BF)
    out_ref[...] = (dot_nn(mixed_ref[...], wd_ref[...]) + dot_nn(hidden, beside(wc1_ref, wc2_ref, 0))).astype(BF)


def mlp_call(mlp_in, mixed, w_exps, b_exp, w_den, w_cons):
    rows, width = mlp_in.shape
    hid = b_exp.shape[1]
    weights = (*w_exps, b_exp, w_den, *w_cons)
    row_block = lambda n: pl.BlockSpec((ROWS, n), lambda i: (i, 0))
    return pl.pallas_call(
        mlp_body,
        grid=(rows // ROWS,),
        in_specs=[row_block(width), row_block(mixed.shape[1])] + [whole(w.shape) for w in weights],
        out_specs=[row_block(hid), row_block(hid), row_block(width)],
        out_shape=[jax.ShapeDtypeStruct((rows, n), BF) for n in (hid, hid, width)],
        compiler_params=pltpu.CompilerParams(vmem_limit_bytes=56 << 20),
        cost_estimate=pl.CostEstimate(
            flops=6 * rows * width * hid, bytes_accessed=rows * (width * 4 + hid * 6), transcendentals=rows * hid * 2
        ),
        name="mlp_forward",
    )(mlp_in, mixed, *weights)


def first_or_add(ref, value, step):
    @pl.when(step == 0)
    def _():
        ref[...] = value

    @pl.when(step > 0)
    def _():
        ref[...] += value


def xhat_of(x):
    centre = x - jnp.mean(x, axis=1, keepdims=True)
    return centre * lax.rsqrt(jnp.mean(centre * centre, axis=1, keepdims=True) + EPSILON)


def mlp_back_body(dy_ref, hid_ref, slope_ref, m_ref, mixed_ref, x_ref, vec_ref, we1_ref, we2_ref, wd_ref, wc1_ref, wc2_ref,
                  dmix_ref, pull_ref, cnear_ref, cfar_ref, enear_ref, efar_ref, dden_ref, stat_ref, dbias_ref,
                  dcon_ref, dexp_ref):
    step = pl.program_id(0)
    dy = dy_ref[...]
    dmix_ref[...] = dot_nt(dy, wd_ref[...]).astype(BF)
    dpre = (dot_nt(dy, beside(wc1_ref, wc2_ref, 0)) * slope_ref[...].astype(F32)).astype(BF)
    first_or_add(dcon_ref, dot_tn(hid_ref[...], dy), step)
    first_or_add(dden_ref, dot_tn(mixed_ref[...], dy), step)
    first_or_add(dexp_ref, dot_tn(m_ref[...], dpre), step)
    e = dot_nt(dpre, beside(we1_ref, we2_ref, 1))
    pull_ref[...] = (e * vec_ref[2:3, :]).astype(BF)
    xhat = xhat_of(x_ref[...].astype(F32))
    first_or_add(stat_ref, jnp.concatenate([jnp.sum(e * xhat, axis=0, keepdims=True), jnp.sum(e, axis=0, keepdims=True)]), step)
    first_or_add(dbias_ref, jnp.sum(dpre.astype(F32), axis=0, keepdims=True), step)

    @pl.when(step == pl.num_programs(0) - 1)
    def _():
        part = dcon_ref.shape[0] // 2
        cnear_ref[...] = dcon_ref[:part, :]
        cfar_ref[...] = dcon_ref[part:, :].astype(BF)
        enear_ref[...] = dexp_ref[:, :part]
        efar_ref[...] = dexp_ref[:, part:].astype(BF)


def mlp_back_call(dy, hidden, slope, mlp_in, mixed, x, vecs, w_exps, w_den, w_cons):
    rows, width = dy.shape
    hid, mix = hidden.shape[1], mixed.shape[1]
    row_block = lambda n: pl.BlockSpec((ROWS, n), lambda i: (i, 0))
    con, exp = (hid // 2, width), (width, hid // 2)
    full = [(con, F32), (con, BF), (exp, F32), (exp, BF), ((mix, width), F32), ((2, width), F32), ((1, hid), F32)]
    weights = (vecs, *w_exps, w_den, *w_cons)
    return pl.pallas_call(
        mlp_back_body,
        grid=(rows // ROWS,),
        in_specs=[row_block(n) for n in (width, hid, hid, width, mix, width)] + [whole(w.shape) for w in weights],
        out_specs=[row_block(mix), row_block(width)] + [whole(f) for f, _ in full],
        out_shape=[jax.ShapeDtypeStruct((rows, mix), BF), jax.ShapeDtypeStruct((rows, width), BF)]
        + [jax.ShapeDtypeStruct(f, t) for f, t in full],
        scratch_shapes=[pltpu.VMEM((hid, width), F32), pltpu.VMEM((width, hid), F32)],
        compiler_params=pltpu.CompilerParams(vmem_limit_bytes=56 << 20),
        cost_estimate=pl.CostEstimate(
            flops=30 * rows * width * hid, bytes_accessed=rows * (width * 8 + hid * 6) + 8 * width * hid, transcendentals=0
        ),
        name="mlp_back",
    )(dy, hidden, slope, mlp_in, mixed, x, *weights)


def last_body(dq_ref, dk_ref, dv_ref, x_ref, mpull_ref, vec_ref, w_ref, pull_ref, stat_ref, dbias_ref):
    step = pl.program_id(0)
    packed = jnp.concatenate([dq_ref[...], dk_ref[...], dv_ref[...]], axis=1)
    e = dot_nt(packed, w_ref[...])
    pull_ref[...] = (e * vec_ref[0:1, :] + mpull_ref[...].astype(F32)).astype(BF)
    xhat = xhat_of(x_ref[...].astype(F32))
    first_or_add(stat_ref, jnp.concatenate([jnp.sum(e * xhat, axis=0, keepdims=True), jnp.sum(e, axis=0, keepdims=True)]), step)
    first_or_add(dbias_ref, jnp.sum(packed.astype(F32), axis=0, keepdims=True), step)


def last_call(dq, dk, dv, x, mpull, vecs, w_pad):
    rows, width = x.shape
    third, cols = dq.shape[1], w_pad.shape[1]
    row_block = lambda n: pl.BlockSpec((ROWS, n), lambda i: (i, 0))
    full = [(2, width), (1, cols)]
    return pl.pallas_call(
        last_body,
        grid=(rows // ROWS,),
        in_specs=[row_block(n) for n in (third, third, third, width, width)] + [whole(vecs.shape), whole(w_pad.shape)],
        out_specs=[row_block(width)] + [whole(f) for f in full],
        out_shape=[jax.ShapeDtypeStruct((rows, width), BF)] + [jax.ShapeDtypeStruct(f, F32) for f in full],
        compiler_params=pltpu.CompilerParams(vmem_limit_bytes=56 << 20),
        cost_estimate=pl.CostEstimate(
            flops=2 * rows * width * cols, bytes_accessed=rows * (width * 6 + cols * 2) + 2 * width * cols, transcendentals=0
        ),
        name="input_pull",
    )(dq, dk, dv, x, mpull, vecs, w_pad)


def qkv_grad_body(attn_ref, dq_ref, dk_ref, dv_ref, one_ref, two_ref):
    attn_in = attn_ref[...]
    parts = []
    for ref in (dq_ref, dk_ref, dv_ref):
        grad = dot_tn(attn_in, ref[...])
        parts += [grad[:, h * LANES : h * LANES + HEAD_DIM] for h in range(grad.shape[1] // LANES)]
    grad = jnp.concatenate(parts, axis=1)
    half = one_ref.shape[1]
    one_ref[...] = grad[:, :half].astype(BF)
    two_ref[...] = grad[:, half:].astype(BF)


def qkv_grad_call(attn_in, dq, dk, dv):
    rows, width = attn_in.shape
    cols = 3 * dq.shape[1] * HEAD_DIM // LANES
    out = pl.BlockSpec((BLK, cols // 2), lambda i: (i, 0))
    return pl.pallas_call(
        qkv_grad_body,
        grid=(width // BLK,),
        in_specs=[pl.BlockSpec((rows, BLK), lambda i: (0, i))] + [whole(dq.shape)] * 3,
        out_specs=[out, out],
        out_shape=[jax.ShapeDtypeStruct((width, cols // 2), BF)] * 2,
        compiler_params=pltpu.CompilerParams(vmem_limit_bytes=56 << 20),
        cost_estimate=pl.CostEstimate(flops=4 * rows * width * cols, bytes_accessed=rows * width * 8, transcendentals=0),
        name="qkv_grad",
    )(attn_in, dq, dk, dv)


def tie(value, *others):
    return lax.optimization_barrier((value,) + others)[0]


def swap(value, axis):
    return lax.ppermute(value, axis, SWAP)


def exchange(value, axes):
    return lax.all_to_all(value, axes, 0, 0, tiled=True)


def gather_tokens(array):
    got = exchange(jnp.tile(array, (4, 1, 1)), CTX_AXES)
    return got.reshape(-1, array.shape[2])


def scatter_tokens(array):
    got = exchange(array.reshape((8, -1) + array.shape[1:]), CTX_AXES)
    return jnp.sum(got.reshape((4, 2) + got.shape[1:]).astype(F32), axis=0)


def by_xor(pieces, here):
    count = len(pieces)
    bit = 1
    while bit < count:
        flip = (here // bit) % 2 == 1
        pieces = [jnp.where(flip, pieces[k ^ bit], pieces[k]) for k in range(count)]
        bit *= 2
    return pieces


def along_dp(value, k):
    return lax.ppermute(value, "dp", [(z, z ^ k) for z in range(4)])


def gather_dp(value, after=None):
    pieces = [value] + [along_dp(value, k) for k in (1, 2, 3)]
    if after is not None:
        pieces = list(lax.optimization_barrier((*pieces, after))[:4])
    return jnp.stack(by_xor(pieces, lax.axis_index("dp")))


def exchange_ctx(value, here):
    pieces = by_xor([value[k] for k in range(8)], here)
    got = [pieces[0]]
    for k in range(1, 8):
        got.append(lax.ppermute(pieces[k], CTX_AXES, [(i, i ^ k) for i in range(8)]))
    return jnp.stack(by_xor(got, here))


def scatter_dp(value):
    pieces = by_xor([value[k] for k in range(4)], lax.axis_index("dp"))
    got = [along_dp(pieces[k], k).astype(F32) for k in (1, 2, 3)]
    return (pieces[0].astype(F32) + got[0] + got[1] + got[2]).astype(BF)


def pick(first, second, core):
    return jnp.where(core == 0, first, second)


def halves_sum(halves, core):
    first, second = halves
    got = swap(pick(second, first, core).astype(BF), "core")
    return (pick(first, second, core) + got.astype(F32)).astype(BF)


def split_device(tokens, segments, positions, gain_attn, shift_attn, gain_mlp, shift_mlp, qkv_weight,
                 query_bias, key_bias, value_bias, dense_weight, expand_weight, expand_bias,
                 contract_weight, output_bias, cotangent):
    seqs, toks, width = tokens.shape
    rows = 8 * toks
    share = qkv_weight.shape[0]
    hidden_share = contract_weight.shape[0]
    n_dp = lax.axis_size("dp")
    heads = width // HEAD_DIM // 4
    band = heads * HEAD_DIM
    core = lax.axis_index("core")
    chip = lax.axis_index("y") * 2 + lax.axis_index("x")
    hop = [((z * 4 + t), (t * 4 + z)) for z in range(4) for t in range(4)]

    third = 3 * band // 2
    qkv_cols = qkv_weight.reshape(share, 3, 4, band).transpose(2, 0, 1, 3).reshape(4, share, 2, third)
    qkv_cols = qkv_cols.transpose(0, 2, 1, 3).reshape(8, share, third)
    exp_cols = expand_weight.reshape(share, n_dp, 8, hidden_share).transpose(2, 0, 1, 3)
    exp_cols = exp_cols.reshape(8, share, n_dp * hidden_share)
    wide = third + n_dp * hidden_share
    small = jnp.concatenate([gain_attn, shift_attn, gain_mlp, shift_mlp, query_bias, key_bias, value_bias,
                             output_bias, expand_bias])
    small_n = small.shape[0]
    row_of = lambda v: jnp.pad(v, ((0, 0), (0, wide - v.shape[1])))
    extra = jnp.stack([
        row_of(jnp.broadcast_to(small[None], (2, small_n))),
        row_of(jnp.concatenate([positions // 64, positions % 64], axis=1).astype(BF)),
        row_of(segments.astype(BF)),
    ], axis=1)
    extra = jnp.tile(extra, (4, 1, 1))
    cols = lax.all_to_all(
        jnp.concatenate([jnp.concatenate([qkv_cols, exp_cols], axis=2), extra], axis=1), CTX_AXES, 0, 0, tiled=True
    )
    x_rows = gather_tokens(tokens)
    dy_rows = gather_tokens(tie(cotangent, x_rows))
    weights = cols[:, :share].reshape(8 * share, wide)
    payload = jnp.concatenate([weights[:, :third], cols[:, share, :third]], axis=0)
    qkv_got = gather_dp(payload)
    exp_mine = weights[:, third:]
    dense_moved = lax.ppermute(dense_weight, ("dp", "y", "x"), hop)
    low_mine = jnp.concatenate([contract_weight, dense_moved], axis=0)

    qkv_half = qkv_got[:, : 8 * share].reshape(width, third)
    qkv_mate = swap(qkv_half, "core")
    qkv_here = jnp.concatenate([pick(qkv_half, qkv_mate, core), pick(qkv_mate, qkv_half, core)], axis=1)
    w_pad = jnp.pad(qkv_here.reshape(width, 3 * heads, HEAD_DIM), ((0, 0), (0, 0), (0, LANES - HEAD_DIM)))
    w_pad = w_pad.reshape(width, 3 * heads * LANES)
    small = qkv_got[:, 8 * share :].reshape(n_dp * 8, third)[:, :small_n].astype(F32)
    vectors = [small[:, n * share : (n + 1) * share].reshape(width) for n in range(8)]
    vecs = jnp.stack(vectors[:4])
    out_bias = vectors[7]
    biases = jnp.stack([lax.dynamic_slice(v, (chip * band,), (band,)) for v in vectors[4:7]])
    b_pad = jnp.pad(biases.reshape(3 * heads, HEAD_DIM), ((0, 0), (0, LANES - HEAD_DIM))).reshape(1, -1)
    exp_bias = small[:, 8 * share :].reshape(n_dp, 4, 2, hidden_share)
    exp_bias = lax.dynamic_index_in_dim(exp_bias, chip, 1, keepdims=False).transpose(1, 0, 2).reshape(2, -1)
    exp_bias = jnp.stack([pick(exp_bias[0], exp_bias[1], core), pick(exp_bias[1], exp_bias[0], core)]).reshape(1, -1)

    marks = cols[:, share + 1 :].astype(F32)
    pos = (marks[:, 0, :toks] * 64.0 + marks[:, 0, toks : 2 * toks]).reshape(rows, 1)
    seg = marks[:, 1, :toks].reshape(rows, 1).astype(jnp.int32)
    lane = jnp.arange(LANES)[None, :]
    half = ROT_DIMS // 2
    inverse = jnp.exp((lane % half).astype(F32) * (-2.0 * math.log(10000.0) / ROT_DIMS))
    angle = pos * inverse
    cosine, sine = jnp.cos(angle), jnp.sin(angle)
    table_c = jnp.where(lane < ROT_DIMS, cosine, jnp.where(lane < HEAD_DIM, 1.0, 0.0))
    table_1 = jnp.where(lane < half, -sine, 0.0)
    table_2 = jnp.where((lane >= half) & (lane < ROT_DIMS), sine, 0.0)
    docs = 16
    in_doc = (lane >= HEAD_DIM) & (lane < HEAD_DIM + docs)
    same = in_doc & (lane - HEAD_DIM == seg)
    mark_q = jnp.where(same, 1.0, 0.0)
    mark_k = jnp.where(in_doc & ~same, NEG_BIG, 0.0)

    attn_in, mlp_in, q, k, v = pre_call(x_rows, vecs, w_pad, b_pad, (table_c, table_1, table_2, mark_q, mark_k))
    exp_got = gather_dp(tie(exp_mine, qkv_got), q).reshape(width, -1)
    low_got = gather_dp(tie(low_mine, qkv_got), q)
    mixed, mixed_full, lse = attn_call(q, k, v)

    half_rows = n_dp * hidden_share
    exp_mate, low_mate, _ = lax.optimization_barrier((swap(exp_got, "core"), swap(low_got, "core"), mixed))
    w_exps = (exp_got, exp_mate)
    w_cons = tuple(w[:, :hidden_share].reshape(half_rows, width) for w in (low_got, low_mate))
    den, den_mate = low_got[:, hidden_share:], low_mate[:, hidden_share:]
    w_den = jnp.stack([pick(den, den_mate, core), pick(den_mate, den, core)], axis=1).reshape(heads, HEAD_DIM, width)
    w_den = jnp.pad(w_den, ((0, 0), (0, LANES - HEAD_DIM), (0, 0))).reshape(heads * LANES, width)

    hidden, slope, out_part = mlp_call(mlp_in, mixed, w_exps, exp_bias, w_den, w_cons)
    out_sum = scatter_tokens(out_part)
    output = (tokens.astype(F32) + out_sum + out_bias).astype(BF)

    d_mixed, mlp_pull, con_near, con_far, exp_near, exp_far, d_den, mlp_stat, d_exp_bias = mlp_back_call(
        dy_rows, hidden, slope, mlp_in, mixed, x_rows, vecs, w_exps, w_den, w_cons
    )
    near_and = lambda near, far: (near + swap(far, "core").astype(F32)).astype(BF)
    con_sum = near_and(con_near, con_far).reshape(n_dp, hidden_share, width)
    exp_sum = near_and(exp_near, exp_far).reshape(n_dp, 8 * share, half_rows)
    d_den = d_den.reshape(heads, LANES, width)[:, :HEAD_DIM].reshape(4, 2, share, width)
    den_sum = halves_sum((d_den[:, 0], d_den[:, 1]), core)
    low_sum = jnp.concatenate([con_sum, den_sum], axis=1)
    d_mixed, exp_sum, low_sum = lax.optimization_barrier((d_mixed, exp_sum, low_sum))
    exp_own = scatter_dp(exp_sum)
    low_sum = scatter_dp(low_sum)
    grad_contract = low_sum[:hidden_share].astype(F32)
    grad_dense = lax.ppermute(low_sum[hidden_share:], ("dp", "y", "x"), hop).astype(F32)

    dq, dk, dv = attn_back_call(q, k, v, d_mixed, mixed_full, lse, (table_c, table_1, table_2))
    dq = tie(dq, output, low_sum, exp_own)
    pull, attn_stat, d_bias = last_call(dq, dk, dv, x_rows, mlp_pull, vecs, w_pad)
    d_bias = d_bias.reshape(3, heads, LANES)[:, :, :HEAD_DIM].reshape(3, band)
    d_exp_bias = d_exp_bias.reshape(2, n_dp, hidden_share)
    d_exp_bias = jnp.stack([pick(d_exp_bias[0], d_exp_bias[1], core), pick(d_exp_bias[1], d_exp_bias[0], core)], axis=1)
    d_out_bias = jnp.sum(cotangent.astype(F32), axis=(0, 1))
    lines = [v.reshape(-1, share) for v in (attn_stat[0], attn_stat[1], mlp_stat[0], mlp_stat[1])]
    for n in range(3):
        line = lax.dynamic_update_slice(jnp.zeros((width,), F32), d_bias[n], (chip * band,))
        lines.append(line.reshape(-1, share))
    lines.append(d_out_bias.reshape(-1, share))
    line = jnp.zeros((n_dp, 4, 2, hidden_share), F32)
    line = lax.dynamic_update_slice(line, d_exp_bias[:, None], (0, chip, 0, 0))
    lines.append(line.reshape(-1, hidden_share))
    lines = jnp.pad(jnp.concatenate(lines, axis=1), ((0, 0), (0, 2 * third - small_n))).reshape(n_dp, 8, 2 * third)
    pulled = exchange(pull.reshape(8, toks, width), CTX_AXES)
    qkv_halves = qkv_grad_call(tie(attn_in, pull), dq, dk, dv)
    spread = small_n // 2
    qkv_halves = [
        jnp.concatenate(
            [
                half_grad.reshape(n_dp, 8 * share, third),
                jnp.pad(lines[:, :, n * spread : (n + 1) * spread], ((0, 0), (0, 0), (0, third - spread))).astype(BF),
            ],
            axis=1,
        )
        for n, half_grad in enumerate(qkv_halves)
    ]
    qkv_near, qkv_far = pick(qkv_halves[0], qkv_halves[1], core), pick(qkv_halves[1], qkv_halves[0], core)
    qkv_sum = near_and(qkv_near.astype(F32), qkv_far)
    qkv_own = scatter_dp(qkv_sum)
    own_cols = jnp.concatenate([qkv_own[: 8 * share], exp_own], axis=1).reshape(8, share, wide)
    own_small = row_of(qkv_own[8 * share :])[:, None]
    owned = exchange_ctx(jnp.concatenate([own_cols, own_small], axis=1), chip * 2 + core)
    grad_expand = owned[:, :share, third:].reshape(8, share, n_dp, hidden_share).transpose(1, 2, 0, 3)
    grad_expand = grad_expand.reshape(share, -1).astype(F32)
    owned = owned.reshape(4, 2, share + 1, wide)
    grad_qkv = owned[:, :, :share, :third].transpose(0, 2, 1, 3).reshape(4, share, 3, band)
    grad_qkv = grad_qkv.transpose(1, 2, 0, 3).reshape(share, -1).astype(F32)
    small_grads = jnp.sum(owned[:, :, share, :spread].astype(F32), axis=0).reshape(small_n)
    pulled = tie(pulled, small_grads, grad_qkv, grad_expand)
    ge = jnp.sum(pulled.reshape(4, 2, toks, width).astype(F32), axis=0)
    own = tokens.astype(F32)
    own_c = own - jnp.mean(own, axis=2, keepdims=True)
    own_r = lax.rsqrt(jnp.mean(own_c * own_c, axis=2, keepdims=True) + EPSILON)
    own_h = own_c * own_r
    back = own_r * (ge - jnp.mean(ge, axis=2, keepdims=True) - own_h * jnp.mean(ge * own_h, axis=2, keepdims=True))
    input_grad = (cotangent.astype(F32) + back).astype(BF)
    part = [small_grads[n * share : (n + 1) * share] for n in range(8)]
    return (output, input_grad, part[0], part[1], part[2], part[3], grad_qkv, part[4], part[5], part[6],
            grad_dense, grad_expand, small_grads[8 * share :], grad_contract, part[7])


def general_plan(mesh):
    placed = (
        P("dp", "ctx", None),
        P("dp", "ctx"),
        P("dp", "ctx"),
        P(("dp", "ctx")),
        P(("dp", "ctx")),
        P(("dp", "ctx")),
        P(("dp", "ctx")),
        P(("dp", "ctx"), None),
        P(("dp", "ctx")),
        P(("dp", "ctx")),
        P(("dp", "ctx")),
        P(("dp", "ctx"), None),
        P(("dp", "ctx"), None),
        P(("dp", "ctx")),
        P(("dp", "ctx"), None),
        P(("dp", "ctx")),
        P("dp", "ctx", None),
    )
    return jax.shard_map(
        per_device,
        mesh=mesh,
        in_specs=placed,
        out_specs=(
            P("dp", "ctx", None),
            P("dp", "ctx", None),
            P(("dp", "ctx")),
            P(("dp", "ctx")),
            P(("dp", "ctx")),
            P(("dp", "ctx")),
            P(("dp", "ctx"), None),
            P(("dp", "ctx")),
            P(("dp", "ctx")),
            P(("dp", "ctx")),
            P(("dp", "ctx"), None),
            P(("dp", "ctx"), None),
            P(("dp", "ctx")),
            P(("dp", "ctx"), None),
            P(("dp", "ctx")),
        ),
        check_vma=False,
    )


def split_plan(mesh):
    fine = Mesh(mesh.devices.reshape(mesh.shape["dp"], 2, 2, 2), ALL_AXES)
    tok = P("dp", CTX_AXES, None)
    mark = P("dp", CTX_AXES)
    vec = P(ALL_AXES)
    mat = P(ALL_AXES, None)
    return jax.shard_map(
        split_device,
        mesh=fine,
        in_specs=(tok, mark, mark, vec, vec, vec, vec, mat, vec, vec, vec, mat, mat, vec, mat, vec, tok),
        out_specs=(tok, tok, vec, vec, vec, vec, mat, vec, vec, vec, mat, mat, vec, mat, vec),
        check_vma=False,
    )


def solution(mesh):
    if mesh.shape["ctx"] == 8 and mesh.shape["dp"] == 4:
        return split_plan(mesh)
    return general_plan(mesh)
```

```python
import math

import jax
import jax.numpy as jnp
from jax import lax
from jax.experimental import pallas as pl
from jax.experimental.pallas import tpu as pltpu
from jax.sharding import Mesh, PartitionSpec as P

HEAD_DIM = 64
ROT_DIMS = 16


NEG_BIG = -1e30
EPSILON = 1e-05


def from_behind(value, axis, by):
    size = lax.axis_size(axis)
    pairs = [(i, i + by) for i in range(size) if 0 <= i + by < size]
    return lax.ppermute(value, axis, pairs)


def shifted(value, axis, by):
    size = lax.axis_size(axis)
    return lax.ppermute(value, axis, [(i, (i + by) % size) for i in range(size)])


def normalize(values, gain_vec, shift_vec):
    centre = values - jnp.mean(values, axis=-1, keepdims=True)
    spread = jnp.mean(centre * centre, axis=-1, keepdims=True)
    return centre * lax.rsqrt(spread + EPSILON) * gain_vec + shift_vec


def angles(positions):
    ladder = jnp.arange(ROT_DIMS // 2).astype(jnp.float32)
    inverse = jnp.exp(ladder * (-2.0 * math.log(10000.0) / ROT_DIMS))
    phase_angle = positions.astype(jnp.float32)[..., None] * inverse
    return (jnp.cos(phase_angle)[..., None, :], jnp.sin(phase_angle)[..., None, :])


def rotate(field_in, cosine, sine_part):
    half_dims = ROT_DIMS // 2
    lower_half = field_in[..., :half_dims]
    upper_half = field_in[..., half_dims:ROT_DIMS]
    remainder = field_in[..., ROT_DIMS:]
    return jnp.concatenate(
        [
            lower_half * cosine - upper_half * sine_part,
            upper_half * cosine + lower_half * sine_part,
            remainder,
        ],
        axis=-1,
    )


def exact_gelu(pre_act):
    return jax.nn.gelu(pre_act, approximate=False)


def contract_last(left_side, right_side):
    return lax.dot_general(
        left_side, right_side, (((1,), (1,)), ((), ())), preferred_element_type=jnp.float32
    )


def visible(query_seg, query_start, key_seg, key_start):
    query_index = query_start + jnp.arange(query_seg.shape[1])
    key_index = key_start + jnp.arange(key_seg.shape[1])
    allowed = (key_index[None, None, :] <= query_index[None, :, None]) & (
        key_seg[:, None, :] == query_seg[:, :, None]
    )
    return allowed[:, :, None, :]


def pair_grads(query_side, stats_side, query_start, key_side, key_start):
    query_rows, d_mixed, query_seg = query_side
    log_total, delta_rows = stats_side
    key_rows, value_rows, key_seg = key_side
    score_scale = 1.0 / math.sqrt(HEAD_DIM)
    allowed = visible(query_seg, query_start, key_seg, key_start)
    scores = (
        jnp.einsum("bqhd,bkhd->bqhk", query_rows, key_rows, preferred_element_type=jnp.float32)
        * score_scale
    )
    prob_rows = jnp.where(
        allowed, jnp.exp(jnp.where(allowed, scores - log_total[..., None], NEG_BIG)), 0.0
    )
    d_prob = jnp.einsum("bqhd,bkhd->bqhk", d_mixed, value_rows, preferred_element_type=jnp.float32)
    d_scores = (prob_rows * (d_prob - delta_rows[..., None])).astype(jnp.bfloat16)
    d_query = (
        jnp.einsum("bqhk,bkhd->bqhd", d_scores, key_rows, preferred_element_type=jnp.float32)
        * score_scale
    )
    d_key = (
        jnp.einsum("bqhk,bqhd->bkhd", d_scores, query_rows, preferred_element_type=jnp.float32)
        * score_scale
    )
    d_value = jnp.einsum(
        "bqhk,bqhd->bkhd",
        prob_rows.astype(jnp.bfloat16),
        d_mixed,
        preferred_element_type=jnp.float32,
    )
    return (d_query, d_key, d_value)


def per_device(
    tokens,
    segments,
    positions,
    gain_attn,
    shift_attn,
    gain_mlp,
    shift_mlp,
    qkv_weight,
    query_bias,
    key_bias,
    value_bias,
    dense_weight,
    expand_weight,
    expand_bias,
    contract_weight,
    output_bias,
    cotangent,
):
    shards = (
        gain_attn,
        shift_attn,
        gain_mlp,
        shift_mlp,
        qkv_weight,
        query_bias,
        key_bias,
        value_bias,
        dense_weight,
        expand_weight,
        expand_bias,
        contract_weight,
        output_bias,
    )
    gathered = (
        lax.all_gather(shards[0], ("dp", "ctx"), axis=0, tiled=True),
        lax.all_gather(shards[1], ("dp", "ctx"), axis=0, tiled=True),
        lax.all_gather(shards[2], ("dp", "ctx"), axis=0, tiled=True),
        lax.all_gather(shards[3], ("dp", "ctx"), axis=0, tiled=True),
        lax.all_gather(shards[4], ("dp", "ctx"), axis=0, tiled=True),
        lax.all_gather(shards[5], ("dp", "ctx"), axis=0, tiled=True),
        lax.all_gather(shards[6], ("dp", "ctx"), axis=0, tiled=True),
        lax.all_gather(shards[7], ("dp", "ctx"), axis=0, tiled=True),
        lax.all_gather(shards[8], ("dp", "ctx"), axis=0, tiled=True),
        lax.all_gather(shards[9], ("dp", "ctx"), axis=0, tiled=True),
        lax.all_gather(shards[10], ("dp", "ctx"), axis=0, tiled=True),
        lax.all_gather(shards[11], ("dp", "ctx"), axis=0, tiled=True),
        lax.all_gather(shards[12], ("dp", "ctx"), axis=0, tiled=True),
    )
    seq_count, tok_count, model_width = tokens.shape
    row_count = seq_count * tok_count
    head_count = model_width // HEAD_DIM
    heads_shape = (seq_count, tok_count, head_count, HEAD_DIM)
    flat_shape = (seq_count, tok_count, model_width)
    full_gain_attn = gathered[0].astype(jnp.float32)
    full_shift_attn = gathered[1].astype(jnp.float32)
    full_gain_mlp = gathered[2].astype(jnp.float32)
    full_shift_mlp = gathered[3].astype(jnp.float32)
    full_query_bias = gathered[5].astype(jnp.float32)
    full_key_bias = gathered[6].astype(jnp.float32)
    full_value_bias = gathered[7].astype(jnp.float32)
    full_expand_bias = gathered[10].astype(jnp.float32)
    full_output_bias = gathered[12].astype(jnp.float32)
    flat_in = tokens.reshape(row_count, model_width).astype(jnp.float32)

    def both_norms(values, gain_one, shift_one, gain_two, shift_two):
        return (normalize(values, gain_one, shift_one), normalize(values, gain_two, shift_two))

    (norm_attn, norm_mlp), norm_pull = jax.vjp(
        both_norms, flat_in, full_gain_attn, full_shift_attn, full_gain_mlp, full_shift_mlp
    )
    attn_in = norm_attn.astype(jnp.bfloat16)
    mlp_in = norm_mlp.astype(jnp.bfloat16)
    packed = jnp.dot(attn_in, gathered[4], preferred_element_type=jnp.float32)
    query_raw = (packed[:, :model_width] + full_query_bias).reshape(heads_shape)
    key_raw = (packed[:, model_width : 2 * model_width] + full_key_bias).reshape(heads_shape)
    value_rows = (
        (packed[:, 2 * model_width :] + full_value_bias).astype(jnp.bfloat16).reshape(heads_shape)
    )
    cosine, sine_part = angles(positions)

    def turn_heads(field_in):
        return rotate(field_in, cosine, sine_part)

    query_turned, query_pull = jax.vjp(turn_heads, query_raw)
    key_turned, key_pull = jax.vjp(turn_heads, key_raw)
    query_rows = query_turned.astype(jnp.bfloat16)
    key_rows = key_turned.astype(jnp.bfloat16)
    key_flat = key_rows.reshape(flat_shape)
    value_flat = value_rows.reshape(flat_shape)
    ctx_count = lax.axis_size("ctx")
    ctx_index = lax.axis_index("ctx")
    here_start = ctx_index * tok_count
    score_scale = 1.0 / math.sqrt(HEAD_DIM)
    start_max = jnp.full((seq_count, tok_count, head_count), NEG_BIG, jnp.float32)
    key_blk = lax.all_gather(key_flat, "ctx", axis=1, tiled=True)
    value_blk = lax.all_gather(value_flat, "ctx", axis=1, tiled=True)
    seg_blk = lax.all_gather(segments, "ctx", axis=1, tiled=True)
    block_len = key_blk.shape[1]
    key_blk = key_blk.reshape(seq_count, block_len, head_count, HEAD_DIM)
    value_blk = value_blk.reshape(seq_count, block_len, head_count, HEAD_DIM)
    allowed = visible(segments, here_start, seg_blk, jnp.int32(0))
    scores = (
        jnp.einsum("bqhd,bkhd->bqhk", query_rows, key_blk, preferred_element_type=jnp.float32)
        * score_scale
    )
    scores = jnp.where(allowed, scores, NEG_BIG)
    new_max = jnp.maximum(start_max, jnp.max(scores, axis=-1))
    weights = jnp.where(allowed, jnp.exp(scores - new_max[..., None]), 0.0)
    new_sum = jnp.sum(weights, axis=-1)
    new_acc = jnp.einsum(
        "bqhk,bkhd->bqhd",
        weights.astype(jnp.bfloat16),
        value_blk,
        preferred_element_type=jnp.float32,
    )
    log_total = new_max + jnp.log(new_sum)
    mixed_full = new_acc / new_sum[..., None]
    mixed_rows = mixed_full.astype(jnp.bfloat16).reshape(row_count, model_width)
    hidden_pre = jnp.dot(mlp_in, gathered[9], preferred_element_type=jnp.float32) + full_expand_bias
    hidden_act, gelu_pull = jax.vjp(exact_gelu, hidden_pre)
    hidden_rows = hidden_act.astype(jnp.bfloat16)
    result = (
        flat_in
        + jnp.dot(mixed_rows, gathered[8], preferred_element_type=jnp.float32)
        + jnp.dot(hidden_rows, gathered[11], preferred_element_type=jnp.float32)
        + full_output_bias
    )
    output = result.astype(jnp.bfloat16).reshape(flat_shape)
    regathered = (
        lax.all_gather(shards[0], ("dp", "ctx"), axis=0, tiled=True),
        lax.all_gather(shards[1], ("dp", "ctx"), axis=0, tiled=True),
        lax.all_gather(shards[2], ("dp", "ctx"), axis=0, tiled=True),
        lax.all_gather(shards[3], ("dp", "ctx"), axis=0, tiled=True),
        lax.all_gather(shards[4], ("dp", "ctx"), axis=0, tiled=True),
        lax.all_gather(shards[5], ("dp", "ctx"), axis=0, tiled=True),
        lax.all_gather(shards[6], ("dp", "ctx"), axis=0, tiled=True),
        lax.all_gather(shards[7], ("dp", "ctx"), axis=0, tiled=True),
        lax.all_gather(shards[8], ("dp", "ctx"), axis=0, tiled=True),
        lax.all_gather(shards[9], ("dp", "ctx"), axis=0, tiled=True),
        lax.all_gather(shards[10], ("dp", "ctx"), axis=0, tiled=True),
        lax.all_gather(shards[11], ("dp", "ctx"), axis=0, tiled=True),
        lax.all_gather(shards[12], ("dp", "ctx"), axis=0, tiled=True),
    )
    back_qkv = regathered[4]
    back_dense = regathered[8]
    back_expand = regathered[9]
    back_contract = regathered[11]
    grad_rows = cotangent.reshape(row_count, model_width)
    grad_full = grad_rows.astype(jnp.float32)
    d_output_bias = jnp.sum(grad_full, axis=0)
    d_contract = jnp.einsum("rf,rd->fd", hidden_rows, grad_rows, preferred_element_type=jnp.float32)
    d_hidden = contract_last(grad_rows, back_contract)
    d_hidden_pre = gelu_pull(d_hidden)[0].astype(jnp.bfloat16)
    d_expand_bias = jnp.sum(d_hidden_pre.astype(jnp.float32), axis=0)
    d_expand = jnp.einsum("rd,rf->df", mlp_in, d_hidden_pre, preferred_element_type=jnp.float32)
    d_norm_mlp = contract_last(d_hidden_pre, back_expand)
    d_dense = jnp.einsum("ri,rd->id", mixed_rows, grad_rows, preferred_element_type=jnp.float32)
    d_mixed = contract_last(grad_rows, back_dense).astype(jnp.bfloat16).reshape(heads_shape)
    delta_rows = jnp.sum(d_mixed.astype(jnp.float32) * mixed_full, axis=-1)
    query_side = (query_rows, d_mixed, segments)
    stats_side = (log_total, delta_rows)

    def carry_step(step_num, loop_state):
        key_block, grad_block, d_query_acc = loop_state
        owner_dev = (ctx_index - step_num) % ctx_count
        key_side = (
            key_block[0].reshape(heads_shape),
            key_block[1].reshape(heads_shape),
            key_block[2],
        )
        d_query_part, d_key_part, d_value_part = pair_grads(
            query_side, stats_side, here_start, key_side, owner_dev * tok_count
        )
        grad_block = (
            grad_block[0] + d_key_part.reshape(flat_shape),
            grad_block[1] + d_value_part.reshape(flat_shape),
        )
        key_block = from_behind((key_block[0], key_block[1], key_block[2]), "ctx", 1)
        grad_block = (
            shifted(grad_block[0].astype(jnp.bfloat16), "ctx", 1).astype(jnp.float32),
            shifted(grad_block[1].astype(jnp.bfloat16), "ctx", 1).astype(jnp.float32),
        )
        return (key_block, grad_block, d_query_acc + d_query_part)

    zero_flat = jnp.zeros(flat_shape, jnp.float32)
    final_state = lax.fori_loop(
        0,
        ctx_count,
        carry_step,
        (
            (key_flat, value_flat, segments),
            (zero_flat, zero_flat),
            jnp.zeros(heads_shape, jnp.float32),
        ),
    )
    d_query_sum = final_state[2]
    d_key_sum = final_state[1][0].reshape(heads_shape)
    d_value_sum = final_state[1][1].reshape(heads_shape)
    d_query_raw = query_pull(d_query_sum)[0].astype(jnp.bfloat16).reshape(row_count, model_width)
    d_key_raw = key_pull(d_key_sum)[0].astype(jnp.bfloat16).reshape(row_count, model_width)
    d_value_low = d_value_sum.astype(jnp.bfloat16).reshape(row_count, model_width)
    d_query_bias = jnp.sum(d_query_raw.astype(jnp.float32), axis=0)
    d_key_bias = jnp.sum(d_key_raw.astype(jnp.float32), axis=0)
    d_value_bias = jnp.sum(d_value_low.astype(jnp.float32), axis=0)
    d_packed = jnp.concatenate([d_query_raw, d_key_raw, d_value_low], axis=1)
    d_qkv = jnp.einsum("rd,rp->dp", attn_in, d_packed, preferred_element_type=jnp.float32)
    d_norm_attn = contract_last(d_packed, back_qkv)
    d_flat, d_gain_attn, d_shift_attn, d_gain_mlp, d_shift_mlp = norm_pull(
        (d_norm_attn, d_norm_mlp)
    )
    input_grad = (grad_full + d_flat).astype(jnp.bfloat16).reshape(flat_shape)
    owned_grads = (
        lax.psum_scatter(d_gain_attn, ("dp", "ctx"), scatter_dimension=0, tiled=True),
        lax.psum_scatter(d_shift_attn, ("dp", "ctx"), scatter_dimension=0, tiled=True),
        lax.psum_scatter(d_gain_mlp, ("dp", "ctx"), scatter_dimension=0, tiled=True),
        lax.psum_scatter(d_shift_mlp, ("dp", "ctx"), scatter_dimension=0, tiled=True),
        lax.psum_scatter(d_qkv, ("dp", "ctx"), scatter_dimension=0, tiled=True),
        lax.psum_scatter(d_query_bias, ("dp", "ctx"), scatter_dimension=0, tiled=True),
        lax.psum_scatter(d_key_bias, ("dp", "ctx"), scatter_dimension=0, tiled=True),
        lax.psum_scatter(d_value_bias, ("dp", "ctx"), scatter_dimension=0, tiled=True),
        lax.psum_scatter(d_dense, ("dp", "ctx"), scatter_dimension=0, tiled=True),
        lax.psum_scatter(d_expand, ("dp", "ctx"), scatter_dimension=0, tiled=True),
        lax.psum_scatter(d_expand_bias, ("dp", "ctx"), scatter_dimension=0, tiled=True),
        lax.psum_scatter(d_contract, ("dp", "ctx"), scatter_dimension=0, tiled=True),
        lax.psum_scatter(d_output_bias, ("dp", "ctx"), scatter_dimension=0, tiled=True),
    )
    return (
        output,
        input_grad,
        owned_grads[0],
        owned_grads[1],
        owned_grads[2],
        owned_grads[3],
        owned_grads[4],
        owned_grads[5],
        owned_grads[6],
        owned_grads[7],
        owned_grads[8],
        owned_grads[9],
        owned_grads[10],
        owned_grads[11],
        owned_grads[12],
    )


LANES = 128
BLK = 256
ATT_ROWS = 512
ROWS = 512
BACK_ROWS = 1024
BF = jnp.bfloat16
F32 = jnp.float32
SWAP = [(0, 1), (1, 0)]
CTX_AXES = ("y", "x", "core")
ALL_AXES = ("dp", "y", "x", "core")


def dot_nn(a, b):
    return lax.dot_general(a, b, (((1,), (0,)), ((), ())), preferred_element_type=F32)


def dot_nt(a, b):
    return lax.dot_general(a, b, (((1,), (1,)), ((), ())), preferred_element_type=F32)


def dot_tn(a, b):
    return lax.dot_general(a, b, (((0,), (0,)), ((), ())), preferred_element_type=F32)


def whole(shape):
    return pl.BlockSpec(shape, lambda *ids: (0,) * len(shape))


def pre_body(x_ref, vec_ref, w_ref, b_ref, cs_ref, s1_ref, s2_ref, eq_ref, ek_ref,
             attn_ref, mlp_ref, q_ref, k_ref, v_ref):
    x = x_ref[...].astype(F32)
    centre = x - jnp.mean(x, axis=1, keepdims=True)
    spread = jnp.mean(centre * centre, axis=1, keepdims=True)
    xhat = centre * lax.rsqrt(spread + EPSILON)
    attn_in = (xhat * vec_ref[0:1, :] + vec_ref[1:2, :]).astype(BF)
    attn_ref[...] = xhat.astype(BF)
    mlp_ref[...] = (xhat * vec_ref[2:3, :] + vec_ref[3:4, :]).astype(BF)
    packed = dot_nn(attn_in, w_ref[...]) + b_ref[...]
    heads = w_ref.shape[1] // (3 * LANES)
    wide = heads * LANES
    cs, s1, s2 = cs_ref[...], s1_ref[...], s2_ref[...]
    half = ROT_DIMS // 2

    def turn(u):
        return u * cs + pltpu.roll(u, LANES - half, 1) * s1 + pltpu.roll(u, half, 1) * s2

    for h in range(heads):
        cols = slice(h * LANES, (h + 1) * LANES)
        q = turn(packed[:, h * LANES : (h + 1) * LANES])
        q_ref[:, cols] = (q.astype(BF).astype(F32) * (1.0 / math.sqrt(HEAD_DIM)) + eq_ref[...]).astype(BF)
        k = turn(packed[:, wide + h * LANES : wide + (h + 1) * LANES])
        k_ref[:, cols] = (k + ek_ref[...]).astype(BF)
        v_ref[:, cols] = packed[:, 2 * wide + h * LANES : 2 * wide + (h + 1) * LANES].astype(BF)


def pre_call(x, vecs, w_pad, b_pad, tables):
    rows, width = x.shape
    cols = w_pad.shape[1]
    third = cols // 3
    row_block = lambda n: pl.BlockSpec((ROWS, n), lambda i: (i, 0))
    return pl.pallas_call(
        pre_body,
        grid=(rows // ROWS,),
        in_specs=[row_block(width), whole(vecs.shape), whole(w_pad.shape), whole(b_pad.shape)]
        + [row_block(LANES)] * 5,
        out_specs=[row_block(width)] * 2 + [row_block(third)] * 3,
        out_shape=[jax.ShapeDtypeStruct((rows, width), BF)] * 2
        + [jax.ShapeDtypeStruct((rows, third), BF)] * 3,
        compiler_params=pltpu.CompilerParams(vmem_limit_bytes=56 << 20),
        cost_estimate=pl.CostEstimate(
            flops=2 * rows * width * cols, bytes_accessed=rows * (width * 6 + cols * 2 + LANES * 20), transcendentals=0
        ),
        name="norm_qkv",
    )(x, vecs, w_pad, b_pad, *tables)


def piece(ref, j):
    return ref[j * ATT_ROWS : (j + 1) * ATT_ROWS, :]


def causal(transposed):
    rows = lax.broadcasted_iota(jnp.int32, (ATT_ROWS, ATT_ROWS), 0)
    cols = lax.broadcasted_iota(jnp.int32, (ATT_ROWS, ATT_ROWS), 1)
    return cols >= rows if transposed else rows >= cols


def row_form(column):
    return jnp.transpose(jnp.broadcast_to(column, (ATT_ROWS, LANES)))[0:1, :]


def attn_body(q_ref, k_ref, v_ref, mixed_ref, full_ref, lse_ref):
    for i in range(q_ref.shape[0] // ATT_ROWS):
        q = piece(q_ref, i)
        scores = [dot_nt(q, piece(k_ref, j)) for j in range(i + 1)]
        scores[i] = jnp.where(causal(False), scores[i], NEG_BIG)
        top = scores[0]
        for s in scores[1:]:
            top = jnp.maximum(top, s)
        top = jnp.max(top, axis=1, keepdims=True)
        acc = None
        total = None
        for j in range(i + 1):
            p = jnp.exp(scores[j] - top)
            total = p if total is None else total + p
            part = dot_nn(p.astype(BF), piece(v_ref, j))
            acc = part if acc is None else acc + part
        total = jnp.sum(total, axis=1, keepdims=True)
        mixed = acc / total
        here = slice(i * ATT_ROWS, (i + 1) * ATT_ROWS)
        full_ref[here, :] = mixed
        mixed_ref[here, :] = mixed.astype(BF)
        lse_ref[0, i : i + 1, :] = row_form(top + jnp.log(total))


def attn_call(q, k, v):
    rows, cols = q.shape
    heads = cols // LANES
    col = pl.BlockSpec((rows, LANES), lambda h: (0, h))
    stats = pl.BlockSpec((1, rows // ATT_ROWS, ATT_ROWS), lambda h: (h, 0, 0))
    return pl.pallas_call(
        attn_body,
        grid=(heads,),
        in_specs=[col] * 3,
        out_specs=[col, col, stats],
        out_shape=[
            jax.ShapeDtypeStruct((rows, cols), BF),
            jax.ShapeDtypeStruct((rows, cols), F32),
            jax.ShapeDtypeStruct((heads, rows // ATT_ROWS, ATT_ROWS), F32),
        ],
        compiler_params=pltpu.CompilerParams(vmem_limit_bytes=48 << 20),
        cost_estimate=pl.CostEstimate(
            flops=heads * rows * rows * 2 * LANES * 4, bytes_accessed=rows * cols * 12, transcendentals=heads * rows * rows // 2
        ),
        name="attention",
    )(q, k, v)


def attn_back_body(q_ref, k_ref, v_ref, do_ref, full_ref, lse_ref, cs_ref, s1_ref, s2_ref,
                   dq_ref, dk_ref, dv_ref, dk_acc, dv_acc, kt_ref):
    blocks = q_ref.shape[0] // ATT_ROWS
    half = ROT_DIMS // 2
    keep = lax.broadcasted_iota(jnp.int32, (ATT_ROWS, LANES), 1) < HEAD_DIM

    def unturn(g, here):
        g = jnp.where(keep, g, 0.0)
        return (
            g * cs_ref[here, :]
            - pltpu.roll(g, LANES - half, 1) * s1_ref[here, :]
            - pltpu.roll(g, half, 1) * s2_ref[here, :]
        ).astype(BF)

    for j in range(blocks):
        kt_ref[j] = jnp.transpose(piece(k_ref, j).astype(F32)).astype(BF)
    for i in reversed(range(blocks)):
        here = slice(i * ATT_ROWS, (i + 1) * ATT_ROWS)
        q = q_ref[here, :]
        do = do_ref[here, :]
        delta = row_form(jnp.sum(do.astype(F32) * full_ref[here, :], axis=1, keepdims=True))
        lse = lse_ref[0, i : i + 1, :]
        dq = None
        for j in range(i + 1):
            k = piece(k_ref, j)
            scores = dot_nt(k, q)
            if j == i:
                scores = jnp.where(causal(True), scores, NEG_BIG)
            p = jnp.exp(scores - lse)
            dp = dot_nt(piece(v_ref, j), do)
            ds = (p * (dp - delta)).astype(BF)
            dv = dot_nn(p.astype(BF), do)
            dk = dot_nn(ds, q)
            if i == blocks - 1:
                dv_acc[j] = dv
                dk_acc[j] = dk
            else:
                dv_acc[j] += dv
                dk_acc[j] += dk
            part = dot_nn(kt_ref[j], ds)
            dq = part if dq is None else dq + part
        dq_ref[here, :] = unturn(jnp.transpose(dq) * (1.0 / math.sqrt(HEAD_DIM)), here)
        dk_ref[here, :] = unturn(dk_acc[i], here)
        dv_ref[here, :] = dv_acc[i].astype(BF)


def attn_back_call(q, k, v, do, full, lse, tables):
    rows, cols = q.shape
    heads = cols // LANES
    col = pl.BlockSpec((rows, LANES), lambda h: (0, h))
    one = pl.BlockSpec((rows, LANES), lambda h: (0, 0))
    stats = pl.BlockSpec((1, rows // ATT_ROWS, ATT_ROWS), lambda h: (h, 0, 0))
    return pl.pallas_call(
        attn_back_body,
        grid=(heads,),
        in_specs=[col] * 5 + [stats] + [one] * 3,
        out_specs=[col] * 3,
        scratch_shapes=[pltpu.VMEM((rows // ATT_ROWS, ATT_ROWS, LANES), F32)] * 2 + [pltpu.VMEM((rows // ATT_ROWS, LANES, ATT_ROWS), BF)],
        out_shape=[jax.ShapeDtypeStruct((rows, cols), BF)] * 3,
        compiler_params=pltpu.CompilerParams(vmem_limit_bytes=48 << 20),
        cost_estimate=pl.CostEstimate(
            flops=heads * rows * rows * 5 * LANES * 4, bytes_accessed=rows * cols * 18, transcendentals=heads * rows * rows // 2
        ),
        name="attention_back",
    )(q, k, v, do, full, lse, *tables)


def beside(one_ref, two_ref, axis):
    return jnp.concatenate([one_ref[...], two_ref[...]], axis=axis)


def mlp_body(m_ref, mixed_ref, we1_ref, we2_ref, be_ref, wd_ref, wc1_ref, wc2_ref, hid_ref, slope_ref, out_ref):
    pre = dot_nn(m_ref[...], beside(we1_ref, we2_ref, 1)) + be_ref[...]
    share = 0.5 * (1.0 + lax.erf(pre * math.sqrt(0.5)))
    hidden = (pre * share).astype(BF)
    hid_ref[...] = hidden
    slope_ref[...] = (share + pre * (jnp.exp(-0.5 * pre * pre) * (1.0 / math.sqrt(2.0 * math.pi)))).astype(BF)
    out_ref[...] = (dot_nn(mixed_ref[...], wd_ref[...]) + dot_nn(hidden, beside(wc1_ref, wc2_ref, 0))).astype(BF)


def mlp_call(mlp_in, mixed, w_exps, b_exp, w_den, w_cons):
    rows, width = mlp_in.shape
    hid = b_exp.shape[1]
    weights = (*w_exps, b_exp, w_den, *w_cons)
    row_block = lambda n: pl.BlockSpec((ROWS, n), lambda i: (i, 0))
    return pl.pallas_call(
        mlp_body,
        grid=(rows // ROWS,),
        in_specs=[row_block(width), row_block(mixed.shape[1])] + [whole(w.shape) for w in weights],
        out_specs=[row_block(hid), row_block(hid), row_block(width)],
        out_shape=[jax.ShapeDtypeStruct((rows, n), BF) for n in (hid, hid, width)],
        compiler_params=pltpu.CompilerParams(vmem_limit_bytes=56 << 20),
        cost_estimate=pl.CostEstimate(
            flops=6 * rows * width * hid, bytes_accessed=rows * (width * 4 + hid * 6), transcendentals=rows * hid * 2
        ),
        name="mlp_forward",
    )(mlp_in, mixed, *weights)


def first_or_add(ref, value, step):
    @pl.when(step == 0)
    def _():
        ref[...] = value

    @pl.when(step > 0)
    def _():
        ref[...] += value


def mlp_back_body(dy_ref, hid_ref, slope_ref, m_ref, mixed_ref, vec_ref, col_ref, we1_ref, we2_ref, wd_ref, wc1_ref, wc2_ref,
                  dmix_ref, pull_ref, cnear_ref, cfar_ref, enear_ref, efar_ref, dden_ref, stat_ref, dbias_ref,
                  dcon_ref, dexp_ref):
    step = pl.program_id(0)
    dy = dy_ref[...]
    dmix_ref[...] = dot_nt(dy, wd_ref[...]).astype(BF)
    dpre = (dot_nt(dy, beside(wc1_ref, wc2_ref, 0)) * slope_ref[...].astype(F32)).astype(BF)
    first_or_add(dcon_ref, dot_tn(hid_ref[...], dy), step)
    first_or_add(dden_ref, dot_tn(mixed_ref[...], dy), step)
    first_or_add(dexp_ref, dot_tn(m_ref[...], dpre), step)
    e = dot_nt(dpre, beside(we1_ref, we2_ref, 1))
    pull_ref[...] = (e * vec_ref[2:3, :]).astype(BF)
    first_or_add(dbias_ref, dot_nn(jnp.ones((8, dpre.shape[0]), BF), dpre)[0:1, :], step)

    @pl.when(step == pl.num_programs(0) - 1)
    def _():
        part = dcon_ref.shape[0] // 2
        cnear_ref[...] = dcon_ref[:part, :]
        cfar_ref[...] = dcon_ref[part:, :].astype(BF)
        plain, bias = dexp_ref[...], dbias_ref[...]
        w_exp = beside(we1_ref, we2_ref, 1).astype(F32)
        grad = plain * col_ref[:, 2:3] + bias * col_ref[:, 3:4]
        enear_ref[...] = grad[:, :part]
        efar_ref[...] = grad[:, part:].astype(BF)
        stat_ref[:, 0:1] = jnp.sum(plain * w_exp, axis=1, keepdims=True)
        stat_ref[:, 1:2] = jnp.sum(bias * w_exp, axis=1, keepdims=True)


def mlp_back_call(dy, hidden, slope, xhat, mixed, vecs, vec_cols, w_exps, w_den, w_cons):
    rows, width = dy.shape
    hid, mix = hidden.shape[1], mixed.shape[1]
    row_block = lambda n: pl.BlockSpec((BACK_ROWS, n), lambda i: (i, 0))
    con, exp = (hid // 2, width), (width, hid // 2)
    full = [(con, F32), (con, BF), (exp, F32), (exp, BF), ((mix, width), F32), ((width, 2), F32), ((1, hid), F32)]
    weights = (vecs, vec_cols, *w_exps, w_den, *w_cons)
    return pl.pallas_call(
        mlp_back_body,
        grid=(rows // BACK_ROWS,),
        in_specs=[row_block(n) for n in (width, hid, hid, width, mix)] + [whole(w.shape) for w in weights],
        out_specs=[row_block(mix), row_block(width)] + [whole(f) for f, _ in full],
        out_shape=[jax.ShapeDtypeStruct((rows, mix), BF), jax.ShapeDtypeStruct((rows, width), BF)]
        + [jax.ShapeDtypeStruct(f, t) for f, t in full],
        scratch_shapes=[pltpu.VMEM((hid, width), F32), pltpu.VMEM((width, hid), F32)],
        compiler_params=pltpu.CompilerParams(vmem_limit_bytes=56 << 20),
        cost_estimate=pl.CostEstimate(
            flops=30 * rows * width * hid, bytes_accessed=rows * (width * 8 + hid * 6) + 8 * width * hid, transcendentals=0
        ),
        name="mlp_back",
    )(dy, hidden, slope, xhat, mixed, *weights)


def last_body(dq_ref, dk_ref, dv_ref, mpull_ref, vec_ref, w_ref, pull_ref):
    packed = jnp.concatenate([dq_ref[...], dk_ref[...], dv_ref[...]], axis=1)
    e = dot_nt(packed, w_ref[...])
    pull_ref[...] = (e * vec_ref[0:1, :] + mpull_ref[...].astype(F32)).astype(BF)


def last_call(dq, dk, dv, mpull, vecs, w_pad):
    rows, width = mpull.shape
    third, cols = dq.shape[1], w_pad.shape[1]
    row_block = lambda n: pl.BlockSpec((ROWS, n), lambda i: (i, 0))
    return pl.pallas_call(
        last_body,
        grid=(rows // ROWS,),
        in_specs=[row_block(n) for n in (third, third, third, width)] + [whole(vecs.shape), whole(w_pad.shape)],
        out_specs=row_block(width),
        out_shape=jax.ShapeDtypeStruct((rows, width), BF),
        compiler_params=pltpu.CompilerParams(vmem_limit_bytes=56 << 20),
        cost_estimate=pl.CostEstimate(
            flops=2 * rows * width * cols, bytes_accessed=rows * (width * 6 + cols * 2) + 2 * width * cols, transcendentals=0
        ),
        name="input_pull",
    )(dq, dk, dv, mpull, vecs, w_pad)


def qkv_grad_body(xhat_ref, dq_ref, dk_ref, dv_ref, w_ref, col_ref, one_ref, two_ref, stat_ref, dbias_ref):
    refs = (dq_ref, dk_ref, dv_ref)
    wide = dq_ref.shape[1]

    @pl.when(pl.program_id(0) == 0)
    def _():
        ones = jnp.ones((8, dq_ref.shape[0]), BF)
        for n, ref in enumerate(refs):
            dbias_ref[:, n * wide : (n + 1) * wide] = dot_nn(ones, ref[...])[0:1, :]

    xhat = xhat_ref[...]
    gain, shift = col_ref[:, 0:1], col_ref[:, 1:2]
    parts = []
    of_gain = of_shift = 0.0
    for n, ref in enumerate(refs):
        plain = dot_tn(xhat, ref[...])
        bias = dbias_ref[:, n * wide : (n + 1) * wide]
        weight = w_ref[:, n * wide : (n + 1) * wide].astype(F32)
        of_gain += jnp.sum(plain * weight, axis=1, keepdims=True)
        of_shift += jnp.sum(bias * weight, axis=1, keepdims=True)
        grad = plain * gain + bias * shift
        parts += [grad[:, h * LANES : h * LANES + HEAD_DIM] for h in range(wide // LANES)]
    stat_ref[:, 0:1] = of_gain
    stat_ref[:, 1:2] = of_shift
    grad = jnp.concatenate(parts, axis=1)
    half = one_ref.shape[1]
    one_ref[...] = grad[:, :half].astype(BF)
    two_ref[...] = grad[:, half:].astype(BF)


def qkv_grad_call(xhat, dq, dk, dv, w_pad, vec_cols):
    rows, width = xhat.shape
    cols = 3 * dq.shape[1] * HEAD_DIM // LANES
    block = lambda n: pl.BlockSpec((BLK, n), lambda i: (i, 0))
    bias = (1, w_pad.shape[1])
    return pl.pallas_call(
        qkv_grad_body,
        grid=(width // BLK,),
        in_specs=[pl.BlockSpec((rows, BLK), lambda i: (0, i))] + [whole(dq.shape)] * 3
        + [block(w_pad.shape[1]), block(vec_cols.shape[1])],
        out_specs=[block(cols // 2), block(cols // 2), block(2), whole(bias)],
        out_shape=[jax.ShapeDtypeStruct((width, cols // 2), BF)] * 2
        + [jax.ShapeDtypeStruct((width, 2), F32), jax.ShapeDtypeStruct(bias, F32)],
        compiler_params=pltpu.CompilerParams(vmem_limit_bytes=56 << 20),
        cost_estimate=pl.CostEstimate(flops=4 * rows * width * cols, bytes_accessed=rows * width * 8, transcendentals=0),
        name="qkv_grad",
    )(xhat, dq, dk, dv, w_pad, vec_cols)


def pack_body(qkv_ref, exp_ref, small_ref, marks_ref, out_ref):
    qkv, exp, small = qkv_ref[...].astype(F32), exp_ref[...].astype(F32), small_ref[...].astype(F32)
    share, wide = qkv.shape[0], out_ref.shape[2]
    band = qkv.shape[1] // 12
    third = 3 * band // 2
    n_dp = 4
    strip = (wide - third) // n_dp
    line = jnp.concatenate([small[n : n + 1] for n in range(small.shape[0])] + [jnp.zeros((1, wide - small.size), F32)], axis=1)
    for c in range(2):
        marks = marks_ref[c]
        toks = marks.shape[1] // 3
        extra = jnp.concatenate(
            [
                line,
                jnp.concatenate([marks[:, : 2 * toks], jnp.zeros((1, wide - 2 * toks), F32)], axis=1),
                jnp.concatenate([marks[:, 2 * toks :], jnp.zeros((1, wide - toks), F32)], axis=1),
                jnp.zeros((5, wide), F32),
            ],
            axis=0,
        )
        for t in range(4):
            mine = jnp.concatenate([qkv[:, (4 * p + t) * band : (4 * p + t + 1) * band] for p in range(3)], axis=1)
            strips = [exp[:, (z * 8 + 2 * t + c) * strip : (z * 8 + 2 * t + c + 1) * strip] for z in range(n_dp)]
            cols = jnp.concatenate([mine[:, c * third : (c + 1) * third]] + strips, axis=1)
            out_ref[2 * t + c] = jnp.concatenate([cols, extra], axis=0).astype(BF)


def pack_call(qkv, exp, small, marks, wide):
    share = qkv.shape[0]
    return pl.pallas_call(
        pack_body,
        out_shape=jax.ShapeDtypeStruct((8, share + 8, wide), BF),
        cost_estimate=pl.CostEstimate(flops=0, bytes_accessed=qkv.size * 8, transcendentals=0),
        name="pack_columns",
    )(qkv, exp, small, marks)


def unpack_body(got_ref, qkv_ref, exp_ref, small_ref):
    share = qkv_ref.shape[0]
    band = qkv_ref.shape[1] // 12
    third = 3 * band // 2
    wide = got_ref.shape[2]
    strip = exp_ref.shape[1] // 32
    got = [got_ref[n].astype(F32) for n in range(8)]
    mine = [jnp.concatenate([got[2 * t][:share, :third], got[2 * t + 1][:share, :third]], axis=1) for t in range(4)]
    qkv_ref[...] = jnp.concatenate([mine[t][:, p * band : (p + 1) * band] for p in range(3) for t in range(4)], axis=1)
    exp_ref[...] = jnp.concatenate(
        [got[n][:share, third + z * strip : third + (z + 1) * strip] for z in range((wide - third) // strip) for n in range(8)],
        axis=1,
    )
    for c in range(2):
        small_ref[c] = (got[c] + got[2 + c] + got[4 + c] + got[6 + c])[share:, :]


def unpack_call(got, share, qkv_n, exp_n):
    extra = got.shape[1] - share
    return pl.pallas_call(
        unpack_body,
        out_shape=[
            jax.ShapeDtypeStruct((share, qkv_n), F32),
            jax.ShapeDtypeStruct((share, exp_n), F32),
            jax.ShapeDtypeStruct((2, extra, got.shape[2]), F32),
        ],
        cost_estimate=pl.CostEstimate(flops=0, bytes_accessed=got.size * 6, transcendentals=0),
        name="unpack_columns",
    )(got)


def tie(value, *others):
    return lax.optimization_barrier((value,) + others)[0]


def swap(value, axis):
    return lax.ppermute(value, axis, SWAP)


def exchange(value, axes):
    return lax.all_to_all(value, axes, 0, 0, tiled=True)


def scatter_tokens(array):
    got = exchange(array.reshape((8, -1) + array.shape[1:]), CTX_AXES)
    return jnp.sum(got.reshape((4, 2) + got.shape[1:]).astype(F32), axis=0)


def by_xor(pieces, here):
    count = len(pieces)
    bit = 1
    while bit < count:
        flip = (here // bit) % 2 == 1
        pieces = [jnp.where(flip, pieces[k ^ bit], pieces[k]) for k in range(count)]
        bit *= 2
    return pieces


def along_dp(value, k):
    return lax.ppermute(value, "dp", [(z, z ^ k) for z in range(4)])


def gather_dp(value, after=None):
    pieces = [value] + [along_dp(value, k) for k in (1, 2, 3)]
    if after is not None:
        pieces = list(lax.optimization_barrier((*pieces, after))[:4])
    return jnp.stack(by_xor(pieces, lax.axis_index("dp")))


def scatter_dp(value):
    pieces = by_xor([value[k] for k in range(4)], lax.axis_index("dp"))
    got = [along_dp(pieces[k], k).astype(F32) for k in (1, 2, 3)]
    return (pieces[0].astype(F32) + got[0] + got[1] + got[2]).astype(BF)


def pick(first, second, core):
    return jnp.where(core == 0, first, second)


def halves_sum(halves, core):
    first, second = halves
    got = swap(pick(second, first, core).astype(BF), "core")
    return (pick(first, second, core) + got.astype(F32)).astype(BF)


def split_device(tokens, segments, positions, gain_attn, shift_attn, gain_mlp, shift_mlp, qkv_weight,
                 query_bias, key_bias, value_bias, dense_weight, expand_weight, expand_bias,
                 contract_weight, output_bias, cotangent):
    seqs, toks, width = tokens.shape
    rows = 8 * toks
    share = qkv_weight.shape[0]
    hidden_share = contract_weight.shape[0]
    n_dp = lax.axis_size("dp")
    heads = width // HEAD_DIM // 4
    band = heads * HEAD_DIM
    core = lax.axis_index("core")
    chip = lax.axis_index("y") * 2 + lax.axis_index("x")
    hop = [((z * 4 + t), (t * 4 + z)) for z in range(4) for t in range(4)]

    third = 3 * band // 2
    wide = third + n_dp * hidden_share
    vectors = (gain_attn, shift_attn, gain_mlp, shift_mlp, query_bias, key_bias, value_bias, output_bias)
    small = jnp.concatenate([v[None] for v in vectors] + [expand_bias.reshape(-1, share)], axis=0)
    small_n = small.size
    marks = jnp.concatenate([positions // 64, positions % 64, segments], axis=1)[:, None].astype(F32)
    cols = exchange(pack_call(qkv_weight, expand_weight, small, marks, wide), CTX_AXES)
    x_rows = exchange(tie(jnp.tile(tokens, (4, 1, 1)), cols), CTX_AXES).reshape(rows, width)
    dy_tiled = jnp.tile(cotangent, (4, 1, 1))
    dy_rows = exchange(tie(dy_tiled, x_rows), CTX_AXES).reshape(rows, width)
    weights = cols[:, :share].reshape(8 * share, wide)
    payload = jnp.concatenate([weights[:, :third], cols[:, share, :third]], axis=0)
    qkv_got = gather_dp(payload)
    exp_mine = weights[:, third:]
    dense_moved = lax.ppermute(dense_weight, ("dp", "y", "x"), hop)
    low_mine = jnp.concatenate([contract_weight, dense_moved], axis=0)

    qkv_half = qkv_got[:, : 8 * share].reshape(width, third)
    qkv_mate = swap(qkv_half, "core")
    qkv_here = jnp.concatenate([pick(qkv_half, qkv_mate, core), pick(qkv_mate, qkv_half, core)], axis=1)
    w_pad = jnp.pad(qkv_here.reshape(width, 3 * heads, HEAD_DIM), ((0, 0), (0, 0), (0, LANES - HEAD_DIM)))
    w_pad = w_pad.reshape(width, 3 * heads * LANES)
    small = qkv_got[:, 8 * share :].reshape(n_dp * 8, third)[:, :small_n].astype(F32)
    vectors = [small[:, n * share : (n + 1) * share].reshape(width) for n in range(8)]
    vecs = jnp.stack(vectors[:4])
    vecs = tie(vecs, dy_tiled)
    vec_cols = vecs.T
    out_bias = vectors[7]
    biases = jnp.stack([lax.dynamic_slice(v, (chip * band,), (band,)) for v in vectors[4:7]])
    b_pad = jnp.pad(biases.reshape(3 * heads, HEAD_DIM), ((0, 0), (0, LANES - HEAD_DIM))).reshape(1, -1)
    exp_bias = small[:, 8 * share :].reshape(n_dp, 4, 2, hidden_share)
    exp_bias = lax.dynamic_index_in_dim(exp_bias, chip, 1, keepdims=False).transpose(1, 0, 2).reshape(2, -1)
    exp_bias = jnp.stack([pick(exp_bias[0], exp_bias[1], core), pick(exp_bias[1], exp_bias[0], core)]).reshape(1, -1)

    marks = cols[:, share + 1 : share + 3].astype(F32)
    pos = (marks[:, 0, :toks] * 64.0 + marks[:, 0, toks : 2 * toks]).reshape(rows, 1)
    seg = marks[:, 1, :toks].reshape(rows, 1).astype(jnp.int32)
    lane = jnp.arange(LANES)[None, :]
    half = ROT_DIMS // 2
    inverse = jnp.exp((lane % half).astype(F32) * (-2.0 * math.log(10000.0) / ROT_DIMS))
    angle = pos * inverse
    cosine, sine = jnp.cos(angle), jnp.sin(angle)
    table_c = jnp.where(lane < ROT_DIMS, cosine, jnp.where(lane < HEAD_DIM, 1.0, 0.0))
    table_1 = jnp.where(lane < half, -sine, 0.0)
    table_2 = jnp.where((lane >= half) & (lane < ROT_DIMS), sine, 0.0)
    docs = 16
    in_doc = (lane >= HEAD_DIM) & (lane < HEAD_DIM + docs)
    same = in_doc & (lane - HEAD_DIM == seg)
    mark_q = jnp.where(same, 1.0, 0.0)
    mark_k = jnp.where(in_doc & ~same, NEG_BIG, 0.0)

    xhat, mlp_in, q, k, v = pre_call(x_rows, vecs, w_pad, b_pad, (table_c, table_1, table_2, mark_q, mark_k))
    exp_got = gather_dp(tie(exp_mine, qkv_got), q).reshape(width, -1)
    low_got = gather_dp(tie(low_mine, qkv_got), q)
    mixed, mixed_full, lse = attn_call(q, k, v)

    half_rows = n_dp * hidden_share
    exp_mate, low_mate, _ = lax.optimization_barrier((swap(exp_got, "core"), swap(low_got, "core"), mixed))
    w_exps = (exp_got, exp_mate)
    w_cons = tuple(w[:, :hidden_share].reshape(half_rows, width) for w in (low_got, low_mate))
    den, den_mate = low_got[:, hidden_share:], low_mate[:, hidden_share:]
    w_den = jnp.stack([pick(den, den_mate, core), pick(den_mate, den, core)], axis=1).reshape(heads, HEAD_DIM, width)
    w_den = jnp.pad(w_den, ((0, 0), (0, LANES - HEAD_DIM), (0, 0))).reshape(heads * LANES, width)

    hidden, slope, out_part = mlp_call(mlp_in, mixed, w_exps, exp_bias, w_den, w_cons)
    out_sum = scatter_tokens(out_part)
    output = (tokens.astype(F32) + out_sum + out_bias).astype(BF)

    d_mixed, mlp_pull, con_near, con_far, exp_near, exp_far, d_den, mlp_stat, d_exp_bias = mlp_back_call(
        dy_rows, hidden, slope, xhat, mixed, vecs, vec_cols, w_exps, w_den, w_cons
    )
    near_and = lambda near, far: (near + swap(far, "core").astype(F32)).astype(BF)
    con_sum = near_and(con_near, con_far).reshape(n_dp, hidden_share, width)
    exp_sum = near_and(exp_near, exp_far).reshape(n_dp, 8 * share, half_rows)
    d_den = d_den.reshape(heads, LANES, width)[:, :HEAD_DIM].reshape(4, 2, share, width)
    den_sum = halves_sum((d_den[:, 0], d_den[:, 1]), core)
    low_sum = jnp.concatenate([con_sum, den_sum], axis=1)
    d_mixed, exp_sum, low_sum = lax.optimization_barrier((d_mixed, exp_sum, low_sum))
    exp_own = scatter_dp(exp_sum)
    low_sum = scatter_dp(low_sum)
    grad_contract = low_sum[:hidden_share].astype(F32)
    grad_dense = lax.ppermute(low_sum[hidden_share:], ("dp", "y", "x"), hop).astype(F32)

    dq, dk, dv = attn_back_call(q, k, v, d_mixed, mixed_full, lse, (table_c, table_1, table_2))
    dq = tie(dq, output, low_sum, exp_own)
    pull = last_call(dq, dk, dv, mlp_pull, vecs, w_pad)
    pulled = exchange(pull.reshape(8, toks, width), CTX_AXES)
    qkv_one, qkv_two, attn_stat, d_bias = qkv_grad_call(tie(xhat, pull), dq, dk, dv, w_pad, vec_cols)
    qkv_halves = (qkv_one, qkv_two)
    d_bias = d_bias.reshape(3, heads, LANES)[:, :, :HEAD_DIM].reshape(3, band)
    d_exp_bias = d_exp_bias.reshape(2, n_dp, hidden_share)
    d_exp_bias = jnp.stack([pick(d_exp_bias[0], d_exp_bias[1], core), pick(d_exp_bias[1], d_exp_bias[0], core)], axis=1)
    d_out_bias = jnp.sum(cotangent.astype(F32), axis=(0, 1))
    lines = [v.reshape(-1, share) for v in (attn_stat[:, 0], attn_stat[:, 1], mlp_stat[:, 0], mlp_stat[:, 1])]
    for n in range(3):
        line = lax.dynamic_update_slice(jnp.zeros((width,), F32), d_bias[n], (chip * band,))
        lines.append(line.reshape(-1, share))
    lines.append(d_out_bias.reshape(-1, share))
    line = jnp.zeros((n_dp, 4, 2, hidden_share), F32)
    line = lax.dynamic_update_slice(line, d_exp_bias[:, None], (0, chip, 0, 0))
    lines.append(line.reshape(-1, hidden_share))
    lines = jnp.pad(jnp.concatenate(lines, axis=1), ((0, 0), (0, 2 * third - small_n))).reshape(n_dp, 8, 2 * third)
    spread = small_n // 2
    qkv_halves = [
        jnp.concatenate(
            [
                half_grad.reshape(n_dp, 8 * share, third),
                jnp.pad(lines[:, :, n * spread : (n + 1) * spread], ((0, 0), (0, 0), (0, third - spread))).astype(BF),
            ],
            axis=1,
        )
        for n, half_grad in enumerate(qkv_halves)
    ]
    qkv_near, qkv_far = pick(qkv_halves[0], qkv_halves[1], core), pick(qkv_halves[1], qkv_halves[0], core)
    qkv_own = scatter_dp(near_and(qkv_near.astype(F32), qkv_far))
    own_cols = jnp.concatenate([qkv_own[: 8 * share], exp_own], axis=1).reshape(8, share, wide)
    own_small = jnp.pad(qkv_own[8 * share :][:, None], ((0, 0), (0, 7), (0, wide - third)))
    owned, pulled = lax.optimization_barrier((jnp.concatenate([own_cols, own_small], axis=1), pulled))
    owned = exchange(owned, CTX_AXES)
    grad_qkv, grad_expand, small_grads = unpack_call(owned, share, qkv_weight.shape[1], expand_weight.shape[1])
    small_grads = small_grads[:, 0, :spread].reshape(small_n)
    ge = jnp.sum(pulled.reshape(4, 2, toks, width).astype(F32), axis=0)
    own = tokens.astype(F32)
    own_c = own - jnp.mean(own, axis=2, keepdims=True)
    own_r = lax.rsqrt(jnp.mean(own_c * own_c, axis=2, keepdims=True) + EPSILON)
    own_h = own_c * own_r
    back = own_r * (ge - jnp.mean(ge, axis=2, keepdims=True) - own_h * jnp.mean(ge * own_h, axis=2, keepdims=True))
    input_grad = (cotangent.astype(F32) + back).astype(BF)
    part = [small_grads[n * share : (n + 1) * share] for n in range(8)]
    return (output, input_grad, part[0], part[1], part[2], part[3], grad_qkv, part[4], part[5], part[6],
            grad_dense, grad_expand, small_grads[8 * share :], grad_contract, part[7])


def general_plan(mesh):
    placed = (
        P("dp", "ctx", None),
        P("dp", "ctx"),
        P("dp", "ctx"),
        P(("dp", "ctx")),
        P(("dp", "ctx")),
        P(("dp", "ctx")),
        P(("dp", "ctx")),
        P(("dp", "ctx"), None),
        P(("dp", "ctx")),
        P(("dp", "ctx")),
        P(("dp", "ctx")),
        P(("dp", "ctx"), None),
        P(("dp", "ctx"), None),
        P(("dp", "ctx")),
        P(("dp", "ctx"), None),
        P(("dp", "ctx")),
        P("dp", "ctx", None),
    )
    return jax.shard_map(
        per_device,
        mesh=mesh,
        in_specs=placed,
        out_specs=(
            P("dp", "ctx", None),
            P("dp", "ctx", None),
            P(("dp", "ctx")),
            P(("dp", "ctx")),
            P(("dp", "ctx")),
            P(("dp", "ctx")),
            P(("dp", "ctx"), None),
            P(("dp", "ctx")),
            P(("dp", "ctx")),
            P(("dp", "ctx")),
            P(("dp", "ctx"), None),
            P(("dp", "ctx"), None),
            P(("dp", "ctx")),
            P(("dp", "ctx"), None),
            P(("dp", "ctx")),
        ),
        check_vma=False,
    )


def split_plan(mesh):
    fine = Mesh(mesh.devices.reshape(mesh.shape["dp"], 2, 2, 2), ALL_AXES)
    tok = P("dp", CTX_AXES, None)
    mark = P("dp", CTX_AXES)
    vec = P(ALL_AXES)
    mat = P(ALL_AXES, None)
    return jax.shard_map(
        split_device,
        mesh=fine,
        in_specs=(tok, mark, mark, vec, vec, vec, vec, mat, vec, vec, vec, mat, mat, vec, mat, vec, tok),
        out_specs=(tok, tok, vec, vec, vec, vec, mat, vec, vec, vec, mat, mat, vec, mat, vec),
        check_vma=False,
    )


def solution(mesh):
    if mesh.shape["ctx"] == 8 and mesh.shape["dp"] == 4:
        return split_plan(mesh)
    return general_plan(mesh)
```

```python
import math

import jax
import jax.numpy as jnp
from jax import lax
from jax.experimental import pallas as pl
from jax.experimental.pallas import tpu as pltpu
from jax.sharding import Mesh, PartitionSpec as P

HEAD_DIM = 64
ROT_DIMS = 16


NEG_BIG = -1e30
EPSILON = 1e-05


def from_behind(value, axis, by):
    size = lax.axis_size(axis)
    pairs = [(i, i + by) for i in range(size) if 0 <= i + by < size]
    return lax.ppermute(value, axis, pairs)


def shifted(value, axis, by):
    size = lax.axis_size(axis)
    return lax.ppermute(value, axis, [(i, (i + by) % size) for i in range(size)])


def normalize(values, gain_vec, shift_vec):
    centre = values - jnp.mean(values, axis=-1, keepdims=True)
    spread = jnp.mean(centre * centre, axis=-1, keepdims=True)
    return centre * lax.rsqrt(spread + EPSILON) * gain_vec + shift_vec


def angles(positions):
    ladder = jnp.arange(ROT_DIMS // 2).astype(jnp.float32)
    inverse = jnp.exp(ladder * (-2.0 * math.log(10000.0) / ROT_DIMS))
    phase_angle = positions.astype(jnp.float32)[..., None] * inverse
    return (jnp.cos(phase_angle)[..., None, :], jnp.sin(phase_angle)[..., None, :])


def rotate(field_in, cosine, sine_part):
    half_dims = ROT_DIMS // 2
    lower_half = field_in[..., :half_dims]
    upper_half = field_in[..., half_dims:ROT_DIMS]
    remainder = field_in[..., ROT_DIMS:]
    return jnp.concatenate(
        [
            lower_half * cosine - upper_half * sine_part,
            upper_half * cosine + lower_half * sine_part,
            remainder,
        ],
        axis=-1,
    )


def exact_gelu(pre_act):
    return jax.nn.gelu(pre_act, approximate=False)


def contract_last(left_side, right_side):
    return lax.dot_general(
        left_side, right_side, (((1,), (1,)), ((), ())), preferred_element_type=jnp.float32
    )


def visible(query_seg, query_start, key_seg, key_start):
    query_index = query_start + jnp.arange(query_seg.shape[1])
    key_index = key_start + jnp.arange(key_seg.shape[1])
    allowed = (key_index[None, None, :] <= query_index[None, :, None]) & (
        key_seg[:, None, :] == query_seg[:, :, None]
    )
    return allowed[:, :, None, :]


def pair_grads(query_side, stats_side, query_start, key_side, key_start):
    query_rows, d_mixed, query_seg = query_side
    log_total, delta_rows = stats_side
    key_rows, value_rows, key_seg = key_side
    score_scale = 1.0 / math.sqrt(HEAD_DIM)
    allowed = visible(query_seg, query_start, key_seg, key_start)
    scores = (
        jnp.einsum("bqhd,bkhd->bqhk", query_rows, key_rows, preferred_element_type=jnp.float32)
        * score_scale
    )
    prob_rows = jnp.where(
        allowed, jnp.exp(jnp.where(allowed, scores - log_total[..., None], NEG_BIG)), 0.0
    )
    d_prob = jnp.einsum("bqhd,bkhd->bqhk", d_mixed, value_rows, preferred_element_type=jnp.float32)
    d_scores = (prob_rows * (d_prob - delta_rows[..., None])).astype(jnp.bfloat16)
    d_query = (
        jnp.einsum("bqhk,bkhd->bqhd", d_scores, key_rows, preferred_element_type=jnp.float32)
        * score_scale
    )
    d_key = (
        jnp.einsum("bqhk,bqhd->bkhd", d_scores, query_rows, preferred_element_type=jnp.float32)
        * score_scale
    )
    d_value = jnp.einsum(
        "bqhk,bqhd->bkhd",
        prob_rows.astype(jnp.bfloat16),
        d_mixed,
        preferred_element_type=jnp.float32,
    )
    return (d_query, d_key, d_value)


def per_device(
    tokens,
    segments,
    positions,
    gain_attn,
    shift_attn,
    gain_mlp,
    shift_mlp,
    qkv_weight,
    query_bias,
    key_bias,
    value_bias,
    dense_weight,
    expand_weight,
    expand_bias,
    contract_weight,
    output_bias,
    cotangent,
):
    shards = (
        gain_attn,
        shift_attn,
        gain_mlp,
        shift_mlp,
        qkv_weight,
        query_bias,
        key_bias,
        value_bias,
        dense_weight,
        expand_weight,
        expand_bias,
        contract_weight,
        output_bias,
    )
    gathered = (
        lax.all_gather(shards[0], ("dp", "ctx"), axis=0, tiled=True),
        lax.all_gather(shards[1], ("dp", "ctx"), axis=0, tiled=True),
        lax.all_gather(shards[2], ("dp", "ctx"), axis=0, tiled=True),
        lax.all_gather(shards[3], ("dp", "ctx"), axis=0, tiled=True),
        lax.all_gather(shards[4], ("dp", "ctx"), axis=0, tiled=True),
        lax.all_gather(shards[5], ("dp", "ctx"), axis=0, tiled=True),
        lax.all_gather(shards[6], ("dp", "ctx"), axis=0, tiled=True),
        lax.all_gather(shards[7], ("dp", "ctx"), axis=0, tiled=True),
        lax.all_gather(shards[8], ("dp", "ctx"), axis=0, tiled=True),
        lax.all_gather(shards[9], ("dp", "ctx"), axis=0, tiled=True),
        lax.all_gather(shards[10], ("dp", "ctx"), axis=0, tiled=True),
        lax.all_gather(shards[11], ("dp", "ctx"), axis=0, tiled=True),
        lax.all_gather(shards[12], ("dp", "ctx"), axis=0, tiled=True),
    )
    seq_count, tok_count, model_width = tokens.shape
    row_count = seq_count * tok_count
    head_count = model_width // HEAD_DIM
    heads_shape = (seq_count, tok_count, head_count, HEAD_DIM)
    flat_shape = (seq_count, tok_count, model_width)
    full_gain_attn = gathered[0].astype(jnp.float32)
    full_shift_attn = gathered[1].astype(jnp.float32)
    full_gain_mlp = gathered[2].astype(jnp.float32)
    full_shift_mlp = gathered[3].astype(jnp.float32)
    full_query_bias = gathered[5].astype(jnp.float32)
    full_key_bias = gathered[6].astype(jnp.float32)
    full_value_bias = gathered[7].astype(jnp.float32)
    full_expand_bias = gathered[10].astype(jnp.float32)
    full_output_bias = gathered[12].astype(jnp.float32)
    flat_in = tokens.reshape(row_count, model_width).astype(jnp.float32)

    def both_norms(values, gain_one, shift_one, gain_two, shift_two):
        return (normalize(values, gain_one, shift_one), normalize(values, gain_two, shift_two))

    (norm_attn, norm_mlp), norm_pull = jax.vjp(
        both_norms, flat_in, full_gain_attn, full_shift_attn, full_gain_mlp, full_shift_mlp
    )
    attn_in = norm_attn.astype(jnp.bfloat16)
    mlp_in = norm_mlp.astype(jnp.bfloat16)
    packed = jnp.dot(attn_in, gathered[4], preferred_element_type=jnp.float32)
    query_raw = (packed[:, :model_width] + full_query_bias).reshape(heads_shape)
    key_raw = (packed[:, model_width : 2 * model_width] + full_key_bias).reshape(heads_shape)
    value_rows = (
        (packed[:, 2 * model_width :] + full_value_bias).astype(jnp.bfloat16).reshape(heads_shape)
    )
    cosine, sine_part = angles(positions)

    def turn_heads(field_in):
        return rotate(field_in, cosine, sine_part)

    query_turned, query_pull = jax.vjp(turn_heads, query_raw)
    key_turned, key_pull = jax.vjp(turn_heads, key_raw)
    query_rows = query_turned.astype(jnp.bfloat16)
    key_rows = key_turned.astype(jnp.bfloat16)
    key_flat = key_rows.reshape(flat_shape)
    value_flat = value_rows.reshape(flat_shape)
    ctx_count = lax.axis_size("ctx")
    ctx_index = lax.axis_index("ctx")
    here_start = ctx_index * tok_count
    score_scale = 1.0 / math.sqrt(HEAD_DIM)
    start_max = jnp.full((seq_count, tok_count, head_count), NEG_BIG, jnp.float32)
    key_blk = lax.all_gather(key_flat, "ctx", axis=1, tiled=True)
    value_blk = lax.all_gather(value_flat, "ctx", axis=1, tiled=True)
    seg_blk = lax.all_gather(segments, "ctx", axis=1, tiled=True)
    block_len = key_blk.shape[1]
    key_blk = key_blk.reshape(seq_count, block_len, head_count, HEAD_DIM)
    value_blk = value_blk.reshape(seq_count, block_len, head_count, HEAD_DIM)
    allowed = visible(segments, here_start, seg_blk, jnp.int32(0))
    scores = (
        jnp.einsum("bqhd,bkhd->bqhk", query_rows, key_blk, preferred_element_type=jnp.float32)
        * score_scale
    )
    scores = jnp.where(allowed, scores, NEG_BIG)
    new_max = jnp.maximum(start_max, jnp.max(scores, axis=-1))
    weights = jnp.where(allowed, jnp.exp(scores - new_max[..., None]), 0.0)
    new_sum = jnp.sum(weights, axis=-1)
    new_acc = jnp.einsum(
        "bqhk,bkhd->bqhd",
        weights.astype(jnp.bfloat16),
        value_blk,
        preferred_element_type=jnp.float32,
    )
    log_total = new_max + jnp.log(new_sum)
    mixed_full = new_acc / new_sum[..., None]
    mixed_rows = mixed_full.astype(jnp.bfloat16).reshape(row_count, model_width)
    hidden_pre = jnp.dot(mlp_in, gathered[9], preferred_element_type=jnp.float32) + full_expand_bias
    hidden_act, gelu_pull = jax.vjp(exact_gelu, hidden_pre)
    hidden_rows = hidden_act.astype(jnp.bfloat16)
    result = (
        flat_in
        + jnp.dot(mixed_rows, gathered[8], preferred_element_type=jnp.float32)
        + jnp.dot(hidden_rows, gathered[11], preferred_element_type=jnp.float32)
        + full_output_bias
    )
    output = result.astype(jnp.bfloat16).reshape(flat_shape)
    regathered = (
        lax.all_gather(shards[0], ("dp", "ctx"), axis=0, tiled=True),
        lax.all_gather(shards[1], ("dp", "ctx"), axis=0, tiled=True),
        lax.all_gather(shards[2], ("dp", "ctx"), axis=0, tiled=True),
        lax.all_gather(shards[3], ("dp", "ctx"), axis=0, tiled=True),
        lax.all_gather(shards[4], ("dp", "ctx"), axis=0, tiled=True),
        lax.all_gather(shards[5], ("dp", "ctx"), axis=0, tiled=True),
        lax.all_gather(shards[6], ("dp", "ctx"), axis=0, tiled=True),
        lax.all_gather(shards[7], ("dp", "ctx"), axis=0, tiled=True),
        lax.all_gather(shards[8], ("dp", "ctx"), axis=0, tiled=True),
        lax.all_gather(shards[9], ("dp", "ctx"), axis=0, tiled=True),
        lax.all_gather(shards[10], ("dp", "ctx"), axis=0, tiled=True),
        lax.all_gather(shards[11], ("dp", "ctx"), axis=0, tiled=True),
        lax.all_gather(shards[12], ("dp", "ctx"), axis=0, tiled=True),
    )
    back_qkv = regathered[4]
    back_dense = regathered[8]
    back_expand = regathered[9]
    back_contract = regathered[11]
    grad_rows = cotangent.reshape(row_count, model_width)
    grad_full = grad_rows.astype(jnp.float32)
    d_output_bias = jnp.sum(grad_full, axis=0)
    d_contract = jnp.einsum("rf,rd->fd", hidden_rows, grad_rows, preferred_element_type=jnp.float32)
    d_hidden = contract_last(grad_rows, back_contract)
    d_hidden_pre = gelu_pull(d_hidden)[0].astype(jnp.bfloat16)
    d_expand_bias = jnp.sum(d_hidden_pre.astype(jnp.float32), axis=0)
    d_expand = jnp.einsum("rd,rf->df", mlp_in, d_hidden_pre, preferred_element_type=jnp.float32)
    d_norm_mlp = contract_last(d_hidden_pre, back_expand)
    d_dense = jnp.einsum("ri,rd->id", mixed_rows, grad_rows, preferred_element_type=jnp.float32)
    d_mixed = contract_last(grad_rows, back_dense).astype(jnp.bfloat16).reshape(heads_shape)
    delta_rows = jnp.sum(d_mixed.astype(jnp.float32) * mixed_full, axis=-1)
    query_side = (query_rows, d_mixed, segments)
    stats_side = (log_total, delta_rows)

    def carry_step(step_num, loop_state):
        key_block, grad_block, d_query_acc = loop_state
        owner_dev = (ctx_index - step_num) % ctx_count
        key_side = (
            key_block[0].reshape(heads_shape),
            key_block[1].reshape(heads_shape),
            key_block[2],
        )
        d_query_part, d_key_part, d_value_part = pair_grads(
            query_side, stats_side, here_start, key_side, owner_dev * tok_count
        )
        grad_block = (
            grad_block[0] + d_key_part.reshape(flat_shape),
            grad_block[1] + d_value_part.reshape(flat_shape),
        )
        key_block = from_behind((key_block[0], key_block[1], key_block[2]), "ctx", 1)
        grad_block = (
            shifted(grad_block[0].astype(jnp.bfloat16), "ctx", 1).astype(jnp.float32),
            shifted(grad_block[1].astype(jnp.bfloat16), "ctx", 1).astype(jnp.float32),
        )
        return (key_block, grad_block, d_query_acc + d_query_part)

    zero_flat = jnp.zeros(flat_shape, jnp.float32)
    final_state = lax.fori_loop(
        0,
        ctx_count,
        carry_step,
        (
            (key_flat, value_flat, segments),
            (zero_flat, zero_flat),
            jnp.zeros(heads_shape, jnp.float32),
        ),
    )
    d_query_sum = final_state[2]
    d_key_sum = final_state[1][0].reshape(heads_shape)
    d_value_sum = final_state[1][1].reshape(heads_shape)
    d_query_raw = query_pull(d_query_sum)[0].astype(jnp.bfloat16).reshape(row_count, model_width)
    d_key_raw = key_pull(d_key_sum)[0].astype(jnp.bfloat16).reshape(row_count, model_width)
    d_value_low = d_value_sum.astype(jnp.bfloat16).reshape(row_count, model_width)
    d_query_bias = jnp.sum(d_query_raw.astype(jnp.float32), axis=0)
    d_key_bias = jnp.sum(d_key_raw.astype(jnp.float32), axis=0)
    d_value_bias = jnp.sum(d_value_low.astype(jnp.float32), axis=0)
    d_packed = jnp.concatenate([d_query_raw, d_key_raw, d_value_low], axis=1)
    d_qkv = jnp.einsum("rd,rp->dp", attn_in, d_packed, preferred_element_type=jnp.float32)
    d_norm_attn = contract_last(d_packed, back_qkv)
    d_flat, d_gain_attn, d_shift_attn, d_gain_mlp, d_shift_mlp = norm_pull(
        (d_norm_attn, d_norm_mlp)
    )
    input_grad = (grad_full + d_flat).astype(jnp.bfloat16).reshape(flat_shape)
    owned_grads = (
        lax.psum_scatter(d_gain_attn, ("dp", "ctx"), scatter_dimension=0, tiled=True),
        lax.psum_scatter(d_shift_attn, ("dp", "ctx"), scatter_dimension=0, tiled=True),
        lax.psum_scatter(d_gain_mlp, ("dp", "ctx"), scatter_dimension=0, tiled=True),
        lax.psum_scatter(d_shift_mlp, ("dp", "ctx"), scatter_dimension=0, tiled=True),
        lax.psum_scatter(d_qkv, ("dp", "ctx"), scatter_dimension=0, tiled=True),
        lax.psum_scatter(d_query_bias, ("dp", "ctx"), scatter_dimension=0, tiled=True),
        lax.psum_scatter(d_key_bias, ("dp", "ctx"), scatter_dimension=0, tiled=True),
        lax.psum_scatter(d_value_bias, ("dp", "ctx"), scatter_dimension=0, tiled=True),
        lax.psum_scatter(d_dense, ("dp", "ctx"), scatter_dimension=0, tiled=True),
        lax.psum_scatter(d_expand, ("dp", "ctx"), scatter_dimension=0, tiled=True),
        lax.psum_scatter(d_expand_bias, ("dp", "ctx"), scatter_dimension=0, tiled=True),
        lax.psum_scatter(d_contract, ("dp", "ctx"), scatter_dimension=0, tiled=True),
        lax.psum_scatter(d_output_bias, ("dp", "ctx"), scatter_dimension=0, tiled=True),
    )
    return (
        output,
        input_grad,
        owned_grads[0],
        owned_grads[1],
        owned_grads[2],
        owned_grads[3],
        owned_grads[4],
        owned_grads[5],
        owned_grads[6],
        owned_grads[7],
        owned_grads[8],
        owned_grads[9],
        owned_grads[10],
        owned_grads[11],
        owned_grads[12],
    )


LANES = 128
BLK = 256
ATT_ROWS = 512
ROWS = 512
BACK_ROWS = 1024
BF = jnp.bfloat16
F32 = jnp.float32
SWAP = [(0, 1), (1, 0)]
CTX_AXES = ("y", "x", "core")
ALL_AXES = ("dp", "y", "x", "core")


def dot_nn(a, b):
    return lax.dot_general(a, b, (((1,), (0,)), ((), ())), preferred_element_type=F32)


def dot_nt(a, b):
    return lax.dot_general(a, b, (((1,), (1,)), ((), ())), preferred_element_type=F32)


def dot_tn(a, b):
    return lax.dot_general(a, b, (((0,), (0,)), ((), ())), preferred_element_type=F32)


def whole(shape):
    return pl.BlockSpec(shape, lambda *ids: (0,) * len(shape))


def pre_body(x_ref, vec_ref, w_ref, b_ref, cs_ref, s1_ref, s2_ref, eq_ref, ek_ref,
             attn_ref, mlp_ref, q_ref, k_ref, v_ref):
    x = x_ref[...].astype(F32)
    centre = x - jnp.mean(x, axis=1, keepdims=True)
    spread = jnp.mean(centre * centre, axis=1, keepdims=True)
    xhat = centre * lax.rsqrt(spread + EPSILON)
    attn_in = (xhat * vec_ref[0:1, :] + vec_ref[1:2, :]).astype(BF)
    attn_ref[...] = xhat.astype(BF)
    mlp_ref[...] = (xhat * vec_ref[2:3, :] + vec_ref[3:4, :]).astype(BF)
    packed = dot_nn(attn_in, w_ref[...]) + b_ref[...]
    heads = w_ref.shape[1] // (3 * LANES)
    wide = heads * LANES
    cs, s1, s2 = cs_ref[...], s1_ref[...], s2_ref[...]
    half = ROT_DIMS // 2

    def turn(u):
        return u * cs + pltpu.roll(u, LANES - half, 1) * s1 + pltpu.roll(u, half, 1) * s2

    for h in range(heads):
        cols = slice(h * LANES, (h + 1) * LANES)
        q = turn(packed[:, h * LANES : (h + 1) * LANES])
        q_ref[:, cols] = (q.astype(BF).astype(F32) * (1.0 / math.sqrt(HEAD_DIM)) + eq_ref[...]).astype(BF)
        k = turn(packed[:, wide + h * LANES : wide + (h + 1) * LANES])
        k_ref[:, cols] = (k + ek_ref[...]).astype(BF)
        v_ref[:, cols] = packed[:, 2 * wide + h * LANES : 2 * wide + (h + 1) * LANES].astype(BF)


def pre_call(x, vecs, w_pad, b_pad, tables):
    rows, width = x.shape
    cols = w_pad.shape[1]
    third = cols // 3
    row_block = lambda n: pl.BlockSpec((ROWS, n), lambda i: (i, 0))
    return pl.pallas_call(
        pre_body,
        grid=(rows // ROWS,),
        in_specs=[row_block(width), whole(vecs.shape), whole(w_pad.shape), whole(b_pad.shape)]
        + [row_block(LANES)] * 5,
        out_specs=[row_block(width)] * 2 + [row_block(third)] * 3,
        out_shape=[jax.ShapeDtypeStruct((rows, width), BF)] * 2
        + [jax.ShapeDtypeStruct((rows, third), BF)] * 3,
        compiler_params=pltpu.CompilerParams(vmem_limit_bytes=56 << 20),
        cost_estimate=pl.CostEstimate(
            flops=2 * rows * width * cols, bytes_accessed=rows * (width * 6 + cols * 2 + LANES * 20), transcendentals=0
        ),
        name="norm_qkv",
    )(x, vecs, w_pad, b_pad, *tables)


def piece(ref, j):
    return ref[j * ATT_ROWS : (j + 1) * ATT_ROWS, :]


def causal(transposed):
    rows = lax.broadcasted_iota(jnp.int32, (ATT_ROWS, ATT_ROWS), 0)
    cols = lax.broadcasted_iota(jnp.int32, (ATT_ROWS, ATT_ROWS), 1)
    return cols >= rows if transposed else rows >= cols


def row_form(column):
    return jnp.transpose(jnp.broadcast_to(column, (ATT_ROWS, LANES)))[0:1, :]


def attn_body(q_ref, k_ref, v_ref, mixed_ref, full_ref, lse_ref):
    for i in range(q_ref.shape[0] // ATT_ROWS):
        q = piece(q_ref, i)
        scores = [dot_nt(q, piece(k_ref, j)) for j in range(i + 1)]
        scores[i] = jnp.where(causal(False), scores[i], NEG_BIG)
        top = scores[0]
        for s in scores[1:]:
            top = jnp.maximum(top, s)
        top = jnp.max(top, axis=1, keepdims=True)
        acc = None
        total = None
        for j in range(i + 1):
            p = jnp.exp(scores[j] - top)
            total = p if total is None else total + p
            part = dot_nn(p.astype(BF), piece(v_ref, j))
            acc = part if acc is None else acc + part
        total = jnp.sum(total, axis=1, keepdims=True)
        mixed = acc / total
        here = slice(i * ATT_ROWS, (i + 1) * ATT_ROWS)
        full_ref[here, :] = mixed
        mixed_ref[here, :] = mixed.astype(BF)
        lse_ref[0, i : i + 1, :] = row_form(top + jnp.log(total))


def attn_call(q, k, v):
    rows, cols = q.shape
    heads = cols // LANES
    col = pl.BlockSpec((rows, LANES), lambda h: (0, h))
    stats = pl.BlockSpec((1, rows // ATT_ROWS, ATT_ROWS), lambda h: (h, 0, 0))
    return pl.pallas_call(
        attn_body,
        grid=(heads,),
        in_specs=[col] * 3,
        out_specs=[col, col, stats],
        out_shape=[
            jax.ShapeDtypeStruct((rows, cols), BF),
            jax.ShapeDtypeStruct((rows, cols), F32),
            jax.ShapeDtypeStruct((heads, rows // ATT_ROWS, ATT_ROWS), F32),
        ],
        compiler_params=pltpu.CompilerParams(vmem_limit_bytes=48 << 20),
        cost_estimate=pl.CostEstimate(
            flops=heads * rows * rows * 2 * LANES * 4, bytes_accessed=rows * cols * 12, transcendentals=heads * rows * rows // 2
        ),
        name="attention",
    )(q, k, v)


def attn_back_body(q_ref, k_ref, v_ref, do_ref, full_ref, lse_ref, cs_ref, s1_ref, s2_ref,
                   dq_ref, dk_ref, dv_ref, dk_acc, dv_acc, kt_ref):
    blocks = q_ref.shape[0] // ATT_ROWS
    half = ROT_DIMS // 2
    keep = lax.broadcasted_iota(jnp.int32, (ATT_ROWS, LANES), 1) < HEAD_DIM

    def unturn(g, here):
        g = jnp.where(keep, g, 0.0)
        return (
            g * cs_ref[here, :]
            - pltpu.roll(g, LANES - half, 1) * s1_ref[here, :]
            - pltpu.roll(g, half, 1) * s2_ref[here, :]
        ).astype(BF)

    for j in range(blocks):
        kt_ref[j] = jnp.transpose(piece(k_ref, j).astype(F32)).astype(BF)
    for i in reversed(range(blocks)):
        here = slice(i * ATT_ROWS, (i + 1) * ATT_ROWS)
        q = q_ref[here, :]
        do = do_ref[here, :]
        delta = row_form(jnp.sum(do.astype(F32) * full_ref[here, :], axis=1, keepdims=True))
        lse = lse_ref[0, i : i + 1, :]
        dq = None
        for j in range(i + 1):
            k = piece(k_ref, j)
            scores = dot_nt(k, q)
            if j == i:
                scores = jnp.where(causal(True), scores, NEG_BIG)
            p = jnp.exp(scores - lse)
            dp = dot_nt(piece(v_ref, j), do)
            ds = (p * (dp - delta)).astype(BF)
            dv = dot_nn(p.astype(BF), do)
            dk = dot_nn(ds, q)
            if i == blocks - 1:
                dv_acc[j] = dv
                dk_acc[j] = dk
            else:
                dv_acc[j] += dv
                dk_acc[j] += dk
            part = dot_nn(kt_ref[j], ds)
            dq = part if dq is None else dq + part
        dq_ref[here, :] = unturn(jnp.transpose(dq) * (1.0 / math.sqrt(HEAD_DIM)), here)
        dk_ref[here, :] = unturn(dk_acc[i], here)
        dv_ref[here, :] = dv_acc[i].astype(BF)


def attn_back_call(q, k, v, do, full, lse, tables):
    rows, cols = q.shape
    heads = cols // LANES
    col = pl.BlockSpec((rows, LANES), lambda h: (0, h))
    one = pl.BlockSpec((rows, LANES), lambda h: (0, 0))
    stats = pl.BlockSpec((1, rows // ATT_ROWS, ATT_ROWS), lambda h: (h, 0, 0))
    return pl.pallas_call(
        attn_back_body,
        grid=(heads,),
        in_specs=[col] * 5 + [stats] + [one] * 3,
        out_specs=[col] * 3,
        scratch_shapes=[pltpu.VMEM((rows // ATT_ROWS, ATT_ROWS, LANES), F32)] * 2 + [pltpu.VMEM((rows // ATT_ROWS, LANES, ATT_ROWS), BF)],
        out_shape=[jax.ShapeDtypeStruct((rows, cols), BF)] * 3,
        compiler_params=pltpu.CompilerParams(vmem_limit_bytes=48 << 20),
        cost_estimate=pl.CostEstimate(
            flops=heads * rows * rows * 5 * LANES * 4, bytes_accessed=rows * cols * 18, transcendentals=heads * rows * rows // 2
        ),
        name="attention_back",
    )(q, k, v, do, full, lse, *tables)


def beside(one_ref, two_ref, axis):
    return jnp.concatenate([one_ref[...], two_ref[...]], axis=axis)


def mlp_body(m_ref, mixed_ref, we1_ref, we2_ref, be_ref, wd_ref, wc1_ref, wc2_ref, hid_ref, slope_ref, out_ref):
    pre = dot_nn(m_ref[...], beside(we1_ref, we2_ref, 1)) + be_ref[...]
    share = 0.5 * (1.0 + lax.erf(pre * math.sqrt(0.5)))
    hidden = (pre * share).astype(BF)
    hid_ref[...] = hidden
    slope_ref[...] = (share + pre * (jnp.exp(-0.5 * pre * pre) * (1.0 / math.sqrt(2.0 * math.pi)))).astype(BF)
    out_ref[...] = (dot_nn(mixed_ref[...], wd_ref[...]) + dot_nn(hidden, beside(wc1_ref, wc2_ref, 0))).astype(BF)


def mlp_call(mlp_in, mixed, w_exps, b_exp, w_den, w_cons):
    rows, width = mlp_in.shape
    hid = b_exp.shape[1]
    weights = (*w_exps, b_exp, w_den, *w_cons)
    row_block = lambda n: pl.BlockSpec((ROWS, n), lambda i: (i, 0))
    return pl.pallas_call(
        mlp_body,
        grid=(rows // ROWS,),
        in_specs=[row_block(width), row_block(mixed.shape[1])] + [whole(w.shape) for w in weights],
        out_specs=[row_block(hid), row_block(hid), row_block(width)],
        out_shape=[jax.ShapeDtypeStruct((rows, n), BF) for n in (hid, hid, width)],
        compiler_params=pltpu.CompilerParams(vmem_limit_bytes=56 << 20),
        cost_estimate=pl.CostEstimate(
            flops=6 * rows * width * hid, bytes_accessed=rows * (width * 4 + hid * 6), transcendentals=rows * hid * 2
        ),
        name="mlp_forward",
    )(mlp_in, mixed, *weights)


def first_or_add(ref, value, step):
    @pl.when(step == 0)
    def _():
        ref[...] = value

    @pl.when(step > 0)
    def _():
        ref[...] += value


def mlp_back_body(dy_ref, hid_ref, slope_ref, m_ref, mixed_ref, vec_ref, col_ref, we1_ref, we2_ref, wd_ref, wc1_ref, wc2_ref,
                  dmix_ref, pull_ref, cnear_ref, cfar_ref, enear_ref, efar_ref, dden_ref, stat_ref, dbias_ref,
                  dcon_ref, dexp_ref):
    step = pl.program_id(0)
    dy = dy_ref[...]
    dmix_ref[...] = dot_nt(dy, wd_ref[...]).astype(BF)
    dpre = (dot_nt(dy, beside(wc1_ref, wc2_ref, 0)) * slope_ref[...].astype(F32)).astype(BF)
    first_or_add(dcon_ref, dot_tn(hid_ref[...], dy), step)
    first_or_add(dden_ref, dot_tn(mixed_ref[...], dy), step)
    first_or_add(dexp_ref, dot_tn(m_ref[...], dpre), step)
    e = dot_nt(dpre, beside(we1_ref, we2_ref, 1))
    pull_ref[...] = (e * vec_ref[2:3, :]).astype(BF)
    first_or_add(dbias_ref, dot_nn(jnp.ones((8, dpre.shape[0]), BF), dpre)[0:1, :], step)

    @pl.when(step == pl.num_programs(0) - 1)
    def _():
        part = dcon_ref.shape[0] // 2
        cnear_ref[...] = dcon_ref[:part, :]
        cfar_ref[...] = dcon_ref[part:, :].astype(BF)
        plain, bias = dexp_ref[...], dbias_ref[...]
        w_exp = beside(we1_ref, we2_ref, 1).astype(F32)
        grad = plain * col_ref[:, 2:3] + bias * col_ref[:, 3:4]
        enear_ref[...] = grad[:, :part]
        efar_ref[...] = grad[:, part:].astype(BF)
        stat_ref[:, 0:1] = jnp.sum(plain * w_exp, axis=1, keepdims=True)
        stat_ref[:, 1:2] = jnp.sum(bias * w_exp, axis=1, keepdims=True)


def mlp_back_call(dy, hidden, slope, xhat, mixed, vecs, vec_cols, w_exps, w_den, w_cons):
    rows, width = dy.shape
    hid, mix = hidden.shape[1], mixed.shape[1]
    row_block = lambda n: pl.BlockSpec((BACK_ROWS, n), lambda i: (i, 0))
    con, exp = (hid // 2, width), (width, hid // 2)
    full = [(con, F32), (con, BF), (exp, F32), (exp, BF), ((mix, width), F32), ((width, 2), F32), ((1, hid), F32)]
    weights = (vecs, vec_cols, *w_exps, w_den, *w_cons)
    return pl.pallas_call(
        mlp_back_body,
        grid=(rows // BACK_ROWS,),
        in_specs=[row_block(n) for n in (width, hid, hid, width, mix)] + [whole(w.shape) for w in weights],
        out_specs=[row_block(mix), row_block(width)] + [whole(f) for f, _ in full],
        out_shape=[jax.ShapeDtypeStruct((rows, mix), BF), jax.ShapeDtypeStruct((rows, width), BF)]
        + [jax.ShapeDtypeStruct(f, t) for f, t in full],
        scratch_shapes=[pltpu.VMEM((hid, width), F32), pltpu.VMEM((width, hid), F32)],
        compiler_params=pltpu.CompilerParams(vmem_limit_bytes=56 << 20),
        cost_estimate=pl.CostEstimate(
            flops=30 * rows * width * hid, bytes_accessed=rows * (width * 8 + hid * 6) + 8 * width * hid, transcendentals=0
        ),
        name="mlp_back",
    )(dy, hidden, slope, xhat, mixed, *weights)


def last_body(dq_ref, dk_ref, dv_ref, mpull_ref, vec_ref, w_ref, pull_ref, packed_ref):
    parts = []
    for ref in (dq_ref, dk_ref, dv_ref):
        wide = ref[...].astype(F32)
        parts += [wide[:, h * LANES : h * LANES + HEAD_DIM] for h in range(wide.shape[1] // LANES)]
    packed = jnp.concatenate(parts, axis=1).astype(BF)
    packed_ref[...] = packed
    e = dot_nt(packed, w_ref[...])
    pull_ref[...] = (e * vec_ref[0:1, :] + mpull_ref[...].astype(F32)).astype(BF)


def last_call(dq, dk, dv, mpull, vecs, w_qkv):
    rows, width = mpull.shape
    third, cols = dq.shape[1], w_qkv.shape[1]
    row_block = lambda n: pl.BlockSpec((ROWS, n), lambda i: (i, 0))
    return pl.pallas_call(
        last_body,
        grid=(rows // ROWS,),
        in_specs=[row_block(n) for n in (third, third, third, width)] + [whole(vecs.shape), whole(w_qkv.shape)],
        out_specs=[row_block(width), row_block(cols)],
        out_shape=[jax.ShapeDtypeStruct((rows, width), BF), jax.ShapeDtypeStruct((rows, cols), BF)],
        compiler_params=pltpu.CompilerParams(vmem_limit_bytes=56 << 20),
        cost_estimate=pl.CostEstimate(
            flops=2 * rows * width * cols, bytes_accessed=rows * (width * 6 + cols * 4) + 2 * width * cols, transcendentals=0
        ),
        name="input_pull",
    )(dq, dk, dv, mpull, vecs, w_qkv)


def qkv_grad_body(core_ref, xhat_ref, packed_ref, w_ref, col_ref, near_ref, far_ref, stat_ref, dbias_ref):
    @pl.when(pl.program_id(0) == 0)
    def _():
        dbias_ref[...] = dot_nn(jnp.ones((8, packed_ref.shape[0]), BF), packed_ref[...])[0:1, :]

    plain = dot_tn(xhat_ref[...], packed_ref[...])
    bias = dbias_ref[...]
    weight = w_ref[...].astype(F32)
    stat_ref[:, 0:1] = jnp.sum(plain * weight, axis=1, keepdims=True)
    stat_ref[:, 1:2] = jnp.sum(bias * weight, axis=1, keepdims=True)
    grad = plain * col_ref[:, 0:1] + bias * col_ref[:, 1:2]
    half = near_ref.shape[2]
    one, two = grad[:, :half], grad[:, half:]
    first = core_ref[0] == 0
    blocks, lines = near_ref.shape[0], near_ref.shape[1]
    rows = grad.shape[0] // blocks
    for ref, value in ((near_ref, jnp.where(first, one, two)), (far_ref, jnp.where(first, two, one))):
        for n in range(blocks):
            ref[n, :rows, :] = value[n * rows : (n + 1) * rows].astype(BF)
            ref[n, rows:, :] = jnp.zeros((lines - rows, half), BF)


def qkv_grad_call(core, xhat, packed, w_qkv, vec_cols, n_dp):
    rows, width = xhat.shape
    cols = packed.shape[1]
    steps = 2
    block = lambda n: pl.BlockSpec((width // steps, n), lambda i: (i, 0))
    out = (n_dp, width // n_dp + 16, cols // 2)
    out_block = pl.BlockSpec((n_dp // steps,) + out[1:], lambda i: (i, 0, 0))
    return pl.pallas_call(
        qkv_grad_body,
        grid=(steps,),
        in_specs=[
            pl.BlockSpec(memory_space=pltpu.SMEM),
            pl.BlockSpec((rows, width // steps), lambda i: (0, i)),
            whole(packed.shape),
            block(cols),
            block(vec_cols.shape[1]),
        ],
        out_specs=[out_block, out_block, block(2), whole((1, cols))],
        out_shape=[jax.ShapeDtypeStruct(out, BF)] * 2
        + [jax.ShapeDtypeStruct((width, 2), F32), jax.ShapeDtypeStruct((1, cols), F32)],
        compiler_params=pltpu.CompilerParams(vmem_limit_bytes=56 << 20),
        cost_estimate=pl.CostEstimate(flops=2 * rows * width * cols, bytes_accessed=rows * width * 4, transcendentals=0),
        name="qkv_grad",
    )(core, xhat, packed, w_qkv, vec_cols)


def pack_body(qkv_ref, exp_ref, small_ref, marks_ref, out_ref):
    qkv, exp, small = qkv_ref[...].astype(F32), exp_ref[...].astype(F32), small_ref[...].astype(F32)
    share, wide = qkv.shape[0], out_ref.shape[2]
    band = qkv.shape[1] // 12
    third = 3 * band // 2
    n_dp = 4
    strip = (wide - third) // n_dp
    line = jnp.concatenate([small[n : n + 1] for n in range(small.shape[0])] + [jnp.zeros((1, wide - small.size), F32)], axis=1)
    for c in range(2):
        marks = marks_ref[c]
        toks = marks.shape[1] // 3
        extra = jnp.concatenate(
            [
                line,
                jnp.concatenate([marks[:, : 2 * toks], jnp.zeros((1, wide - 2 * toks), F32)], axis=1),
                jnp.concatenate([marks[:, 2 * toks :], jnp.zeros((1, wide - toks), F32)], axis=1),
                jnp.zeros((5, wide), F32),
            ],
            axis=0,
        )
        for t in range(4):
            mine = jnp.concatenate([qkv[:, (4 * p + t) * band : (4 * p + t + 1) * band] for p in range(3)], axis=1)
            strips = [exp[:, (z * 8 + 2 * t + c) * strip : (z * 8 + 2 * t + c + 1) * strip] for z in range(n_dp)]
            cols = jnp.concatenate([mine[:, c * third : (c + 1) * third]] + strips, axis=1)
            out_ref[2 * t + c] = jnp.concatenate([cols, extra], axis=0).astype(BF)


def pack_call(qkv, exp, small, marks, wide):
    share = qkv.shape[0]
    return pl.pallas_call(
        pack_body,
        out_shape=jax.ShapeDtypeStruct((8, share + 8, wide), BF),
        cost_estimate=pl.CostEstimate(flops=0, bytes_accessed=qkv.size * 8, transcendentals=0),
        name="pack_columns",
    )(qkv, exp, small, marks)


def unpack_body(got_ref, qkv_ref, exp_ref, small_ref):
    share = qkv_ref.shape[0]
    band = qkv_ref.shape[1] // 12
    third = 3 * band // 2
    wide = got_ref.shape[2]
    strip = exp_ref.shape[1] // 32
    got = [got_ref[n].astype(F32) for n in range(8)]
    mine = [jnp.concatenate([got[2 * t][:share, :third], got[2 * t + 1][:share, :third]], axis=1) for t in range(4)]
    qkv_ref[...] = jnp.concatenate([mine[t][:, p * band : (p + 1) * band] for p in range(3) for t in range(4)], axis=1)
    exp_ref[...] = jnp.concatenate(
        [got[n][:share, third + z * strip : third + (z + 1) * strip] for z in range((wide - third) // strip) for n in range(8)],
        axis=1,
    )
    for c in range(2):
        small_ref[c] = (got[c] + got[2 + c] + got[4 + c] + got[6 + c])[share:, :]


def unpack_call(got, share, qkv_n, exp_n):
    extra = got.shape[1] - share
    return pl.pallas_call(
        unpack_body,
        out_shape=[
            jax.ShapeDtypeStruct((share, qkv_n), F32),
            jax.ShapeDtypeStruct((share, exp_n), F32),
            jax.ShapeDtypeStruct((2, extra, got.shape[2]), F32),
        ],
        cost_estimate=pl.CostEstimate(flops=0, bytes_accessed=got.size * 6, transcendentals=0),
        name="unpack_columns",
    )(got)


def tie(value, *others):
    return lax.optimization_barrier((value,) + others)[0]


def swap(value, axis):
    return lax.ppermute(value, axis, SWAP)


def exchange(value, axes):
    return lax.all_to_all(value, axes, 0, 0, tiled=True)


def scatter_tokens(array):
    got = exchange(array.reshape((8, -1) + array.shape[1:]), CTX_AXES)
    return jnp.sum(got.reshape((4, 2) + got.shape[1:]).astype(F32), axis=0)


def by_xor(pieces, here):
    count = len(pieces)
    bit = 1
    while bit < count:
        flip = (here // bit) % 2 == 1
        pieces = [jnp.where(flip, pieces[k ^ bit], pieces[k]) for k in range(count)]
        bit *= 2
    return pieces


def along_dp(value, k):
    return lax.ppermute(value, "dp", [(z, z ^ k) for z in range(4)])


def gather_dp(value, after=None):
    pieces = [value] + [along_dp(value, k) for k in (1, 2, 3)]
    if after is not None:
        pieces = list(lax.optimization_barrier((*pieces, after))[:4])
    return jnp.stack(by_xor(pieces, lax.axis_index("dp")))


def scatter_dp(value):
    pieces = by_xor([value[k] for k in range(4)], lax.axis_index("dp"))
    got = [along_dp(pieces[k], k).astype(F32) for k in (1, 2, 3)]
    return (pieces[0].astype(F32) + got[0] + got[1] + got[2]).astype(BF)


def pick(first, second, core):
    return jnp.where(core == 0, first, second)


def halves_sum(halves, core):
    first, second = halves
    got = swap(pick(second, first, core).astype(BF), "core")
    return (pick(first, second, core) + got.astype(F32)).astype(BF)


def split_device(tokens, segments, positions, gain_attn, shift_attn, gain_mlp, shift_mlp, qkv_weight,
                 query_bias, key_bias, value_bias, dense_weight, expand_weight, expand_bias,
                 contract_weight, output_bias, cotangent):
    seqs, toks, width = tokens.shape
    rows = 8 * toks
    share = qkv_weight.shape[0]
    hidden_share = contract_weight.shape[0]
    n_dp = lax.axis_size("dp")
    heads = width // HEAD_DIM // 4
    band = heads * HEAD_DIM
    core = lax.axis_index("core")
    chip = lax.axis_index("y") * 2 + lax.axis_index("x")
    hop = [((z * 4 + t), (t * 4 + z)) for z in range(4) for t in range(4)]

    third = 3 * band // 2
    wide = third + n_dp * hidden_share
    vectors = (gain_attn, shift_attn, gain_mlp, shift_mlp, query_bias, key_bias, value_bias, output_bias)
    small = jnp.concatenate([v[None] for v in vectors] + [expand_bias.reshape(-1, share)], axis=0)
    small_n = small.size
    marks = jnp.concatenate([positions // 64, positions % 64, segments], axis=1)[:, None].astype(F32)
    cols = exchange(pack_call(qkv_weight, expand_weight, small, marks, wide), CTX_AXES)
    x_rows = exchange(tie(jnp.tile(tokens, (4, 1, 1)), cols), CTX_AXES).reshape(rows, width)
    dy_tiled = jnp.tile(cotangent, (4, 1, 1))
    dy_rows = exchange(tie(dy_tiled, x_rows), CTX_AXES).reshape(rows, width)
    weights = cols[:, :share].reshape(8 * share, wide)
    payload = jnp.concatenate([weights[:, :third], cols[:, share, :third]], axis=0)
    qkv_got = gather_dp(payload)
    exp_mine = weights[:, third:]
    dense_moved = lax.ppermute(dense_weight, ("dp", "y", "x"), hop)
    low_mine = jnp.concatenate([contract_weight, dense_moved], axis=0)

    qkv_half = qkv_got[:, : 8 * share].reshape(width, third)
    qkv_mate = swap(qkv_half, "core")
    qkv_here = jnp.concatenate([pick(qkv_half, qkv_mate, core), pick(qkv_mate, qkv_half, core)], axis=1)
    w_pad = jnp.pad(qkv_here.reshape(width, 3 * heads, HEAD_DIM), ((0, 0), (0, 0), (0, LANES - HEAD_DIM)))
    w_pad = w_pad.reshape(width, 3 * heads * LANES)
    small = qkv_got[:, 8 * share :].reshape(n_dp * 8, third)[:, :small_n].astype(F32)
    vectors = [small[:, n * share : (n + 1) * share].reshape(width) for n in range(8)]
    vecs = jnp.stack(vectors[:4])
    vecs = tie(vecs, dy_tiled)
    vec_cols = vecs.T
    out_bias = vectors[7]
    biases = jnp.stack([lax.dynamic_slice(v, (chip * band,), (band,)) for v in vectors[4:7]])
    b_pad = jnp.pad(biases.reshape(3 * heads, HEAD_DIM), ((0, 0), (0, LANES - HEAD_DIM))).reshape(1, -1)
    exp_bias = small[:, 8 * share :].reshape(n_dp, 4, 2, hidden_share)
    exp_bias = lax.dynamic_index_in_dim(exp_bias, chip, 1, keepdims=False).transpose(1, 0, 2).reshape(2, -1)
    exp_bias = jnp.stack([pick(exp_bias[0], exp_bias[1], core), pick(exp_bias[1], exp_bias[0], core)]).reshape(1, -1)

    marks = cols[:, share + 1 : share + 3].astype(F32)
    pos = (marks[:, 0, :toks] * 64.0 + marks[:, 0, toks : 2 * toks]).reshape(rows, 1)
    seg = marks[:, 1, :toks].reshape(rows, 1).astype(jnp.int32)
    lane = jnp.arange(LANES)[None, :]
    half = ROT_DIMS // 2
    inverse = jnp.exp((lane % half).astype(F32) * (-2.0 * math.log(10000.0) / ROT_DIMS))
    angle = pos * inverse
    cosine, sine = jnp.cos(angle), jnp.sin(angle)
    table_c = jnp.where(lane < ROT_DIMS, cosine, jnp.where(lane < HEAD_DIM, 1.0, 0.0))
    table_1 = jnp.where(lane < half, -sine, 0.0)
    table_2 = jnp.where((lane >= half) & (lane < ROT_DIMS), sine, 0.0)
    docs = 16
    in_doc = (lane >= HEAD_DIM) & (lane < HEAD_DIM + docs)
    same = in_doc & (lane - HEAD_DIM == seg)
    mark_q = jnp.where(same, 1.0, 0.0)
    mark_k = jnp.where(in_doc & ~same, NEG_BIG, 0.0)

    xhat, mlp_in, q, k, v = pre_call(x_rows, vecs, w_pad, b_pad, (table_c, table_1, table_2, mark_q, mark_k))
    exp_got = gather_dp(tie(exp_mine, qkv_got), q).reshape(width, -1)
    low_got = gather_dp(tie(low_mine, qkv_got), q)
    mixed, mixed_full, lse = attn_call(q, k, v)

    half_rows = n_dp * hidden_share
    exp_mate, low_mate, _ = lax.optimization_barrier((swap(exp_got, "core"), swap(low_got, "core"), mixed))
    w_exps = (exp_got, exp_mate)
    w_cons = tuple(w[:, :hidden_share].reshape(half_rows, width) for w in (low_got, low_mate))
    den, den_mate = low_got[:, hidden_share:], low_mate[:, hidden_share:]
    w_den = jnp.stack([pick(den, den_mate, core), pick(den_mate, den, core)], axis=1).reshape(heads, HEAD_DIM, width)
    w_den = jnp.pad(w_den, ((0, 0), (0, LANES - HEAD_DIM), (0, 0))).reshape(heads * LANES, width)

    hidden, slope, out_part = mlp_call(mlp_in, mixed, w_exps, exp_bias, w_den, w_cons)
    out_sum = scatter_tokens(out_part)
    output = (tokens.astype(F32) + out_sum + out_bias).astype(BF)

    d_mixed, mlp_pull, con_near, con_far, exp_near, exp_far, d_den, mlp_stat, d_exp_bias = mlp_back_call(
        dy_rows, hidden, slope, xhat, mixed, vecs, vec_cols, w_exps, w_den, w_cons
    )
    near_and = lambda near, far: (near + swap(far, "core").astype(F32)).astype(BF)
    con_sum = near_and(con_near, con_far).reshape(n_dp, hidden_share, width)
    exp_sum = near_and(exp_near, exp_far).reshape(n_dp, 8 * share, half_rows)
    d_den = d_den.reshape(heads, LANES, width)[:, :HEAD_DIM].reshape(4, 2, share, width)
    den_sum = halves_sum((d_den[:, 0], d_den[:, 1]), core)
    low_sum = jnp.concatenate([con_sum, den_sum], axis=1)
    d_mixed, exp_sum, low_sum = lax.optimization_barrier((d_mixed, exp_sum, low_sum))
    exp_own = scatter_dp(exp_sum)
    low_sum = scatter_dp(low_sum)
    grad_contract = low_sum[:hidden_share].astype(F32)
    grad_dense = lax.ppermute(low_sum[hidden_share:], ("dp", "y", "x"), hop).astype(F32)

    dq, dk, dv = attn_back_call(q, k, v, d_mixed, mixed_full, lse, (table_c, table_1, table_2))
    dq = tie(dq, output, low_sum, exp_own)
    pull, packed = last_call(dq, dk, dv, mlp_pull, vecs, qkv_here)
    pulled = exchange(pull.reshape(8, toks, width), CTX_AXES)
    core_arr = core.reshape(1).astype(jnp.int32)
    qkv_near, qkv_far, attn_stat, d_bias = qkv_grad_call(core_arr, tie(xhat, pull), packed, qkv_here, vec_cols, n_dp)
    d_bias = d_bias.reshape(3, band)
    d_exp_bias = d_exp_bias.reshape(2, n_dp, hidden_share)
    d_exp_bias = jnp.stack([pick(d_exp_bias[0], d_exp_bias[1], core), pick(d_exp_bias[1], d_exp_bias[0], core)], axis=1)
    d_out_bias = jnp.sum(cotangent.astype(F32), axis=(0, 1))
    lines = [v.reshape(-1, share) for v in (attn_stat[:, 0], attn_stat[:, 1], mlp_stat[:, 0], mlp_stat[:, 1])]
    for n in range(3):
        line = lax.dynamic_update_slice(jnp.zeros((width,), F32), d_bias[n], (chip * band,))
        lines.append(line.reshape(-1, share))
    lines.append(d_out_bias.reshape(-1, share))
    line = jnp.zeros((n_dp, 4, 2, hidden_share), F32)
    line = lax.dynamic_update_slice(line, d_exp_bias[:, None], (0, chip, 0, 0))
    lines.append(line.reshape(-1, hidden_share))
    lines = jnp.pad(jnp.concatenate(lines, axis=1), ((0, 0), (0, 2 * third - small_n))).reshape(n_dp, 8, 2 * third)
    spread = small_n // 2
    line_halves = [
        jnp.pad(lines[:, :, n * spread : (n + 1) * spread], ((0, 0), (0, 8), (0, third - spread))).astype(BF) for n in range(2)
    ]
    qkv_near = lax.dynamic_update_slice(qkv_near, pick(line_halves[0], line_halves[1], core), (0, 8 * share, 0))
    qkv_far = lax.dynamic_update_slice(qkv_far, pick(line_halves[1], line_halves[0], core), (0, 8 * share, 0))
    qkv_own = scatter_dp(near_and(qkv_near.astype(F32), qkv_far))
    own_cols = jnp.concatenate([qkv_own[: 8 * share], exp_own], axis=1).reshape(8, share, wide)
    own_small = jnp.pad(qkv_own[8 * share : 8 * share + 8][:, None], ((0, 0), (0, 7), (0, wide - third)))
    owned, pulled = lax.optimization_barrier((jnp.concatenate([own_cols, own_small], axis=1), pulled))
    owned = exchange(owned, CTX_AXES)
    grad_qkv, grad_expand, small_grads = unpack_call(owned, share, qkv_weight.shape[1], expand_weight.shape[1])
    small_grads = small_grads[:, 0, :spread].reshape(small_n)
    ge = jnp.sum(pulled.reshape(4, 2, toks, width).astype(F32), axis=0)
    own = tokens.astype(F32)
    own_c = own - jnp.mean(own, axis=2, keepdims=True)
    own_r = lax.rsqrt(jnp.mean(own_c * own_c, axis=2, keepdims=True) + EPSILON)
    own_h = own_c * own_r
    back = own_r * (ge - jnp.mean(ge, axis=2, keepdims=True) - own_h * jnp.mean(ge * own_h, axis=2, keepdims=True))
    input_grad = (cotangent.astype(F32) + back).astype(BF)
    part = [small_grads[n * share : (n + 1) * share] for n in range(8)]
    return (output, input_grad, part[0], part[1], part[2], part[3], grad_qkv, part[4], part[5], part[6],
            grad_dense, grad_expand, small_grads[8 * share :], grad_contract, part[7])


def general_plan(mesh):
    placed = (
        P("dp", "ctx", None),
        P("dp", "ctx"),
        P("dp", "ctx"),
        P(("dp", "ctx")),
        P(("dp", "ctx")),
        P(("dp", "ctx")),
        P(("dp", "ctx")),
        P(("dp", "ctx"), None),
        P(("dp", "ctx")),
        P(("dp", "ctx")),
        P(("dp", "ctx")),
        P(("dp", "ctx"), None),
        P(("dp", "ctx"), None),
        P(("dp", "ctx")),
        P(("dp", "ctx"), None),
        P(("dp", "ctx")),
        P("dp", "ctx", None),
    )
    return jax.shard_map(
        per_device,
        mesh=mesh,
        in_specs=placed,
        out_specs=(
            P("dp", "ctx", None),
            P("dp", "ctx", None),
            P(("dp", "ctx")),
            P(("dp", "ctx")),
            P(("dp", "ctx")),
            P(("dp", "ctx")),
            P(("dp", "ctx"), None),
            P(("dp", "ctx")),
            P(("dp", "ctx")),
            P(("dp", "ctx")),
            P(("dp", "ctx"), None),
            P(("dp", "ctx"), None),
            P(("dp", "ctx")),
            P(("dp", "ctx"), None),
            P(("dp", "ctx")),
        ),
        check_vma=False,
    )


def split_plan(mesh):
    fine = Mesh(mesh.devices.reshape(mesh.shape["dp"], 2, 2, 2), ALL_AXES)
    tok = P("dp", CTX_AXES, None)
    mark = P("dp", CTX_AXES)
    vec = P(ALL_AXES)
    mat = P(ALL_AXES, None)
    return jax.shard_map(
        split_device,
        mesh=fine,
        in_specs=(tok, mark, mark, vec, vec, vec, vec, mat, vec, vec, vec, mat, mat, vec, mat, vec, tok),
        out_specs=(tok, tok, vec, vec, vec, vec, mat, vec, vec, vec, mat, mat, vec, mat, vec),
        check_vma=False,
    )


def solution(mesh):
    if mesh.shape["ctx"] == 8 and mesh.shape["dp"] == 4:
        return split_plan(mesh)
    return general_plan(mesh)
```

```python
import math

import jax
import jax.numpy as jnp
from jax import lax
from jax.experimental import pallas as pl
from jax.experimental.pallas import tpu as pltpu
from jax.sharding import Mesh, PartitionSpec as P

HEAD_DIM = 64
ROT_DIMS = 16


NEG_BIG = -1e30
EPSILON = 1e-05


def from_behind(value, axis, by):
    size = lax.axis_size(axis)
    pairs = [(i, i + by) for i in range(size) if 0 <= i + by < size]
    return lax.ppermute(value, axis, pairs)


def shifted(value, axis, by):
    size = lax.axis_size(axis)
    return lax.ppermute(value, axis, [(i, (i + by) % size) for i in range(size)])


def normalize(values, gain_vec, shift_vec):
    centre = values - jnp.mean(values, axis=-1, keepdims=True)
    spread = jnp.mean(centre * centre, axis=-1, keepdims=True)
    return centre * lax.rsqrt(spread + EPSILON) * gain_vec + shift_vec


def angles(positions):
    ladder = jnp.arange(ROT_DIMS // 2).astype(jnp.float32)
    inverse = jnp.exp(ladder * (-2.0 * math.log(10000.0) / ROT_DIMS))
    phase_angle = positions.astype(jnp.float32)[..., None] * inverse
    return (jnp.cos(phase_angle)[..., None, :], jnp.sin(phase_angle)[..., None, :])


def rotate(field_in, cosine, sine_part):
    half_dims = ROT_DIMS // 2
    lower_half = field_in[..., :half_dims]
    upper_half = field_in[..., half_dims:ROT_DIMS]
    remainder = field_in[..., ROT_DIMS:]
    return jnp.concatenate(
        [
            lower_half * cosine - upper_half * sine_part,
            upper_half * cosine + lower_half * sine_part,
            remainder,
        ],
        axis=-1,
    )


def exact_gelu(pre_act):
    return jax.nn.gelu(pre_act, approximate=False)


def contract_last(left_side, right_side):
    return lax.dot_general(
        left_side, right_side, (((1,), (1,)), ((), ())), preferred_element_type=jnp.float32
    )


def visible(query_seg, query_start, key_seg, key_start):
    query_index = query_start + jnp.arange(query_seg.shape[1])
    key_index = key_start + jnp.arange(key_seg.shape[1])
    allowed = (key_index[None, None, :] <= query_index[None, :, None]) & (
        key_seg[:, None, :] == query_seg[:, :, None]
    )
    return allowed[:, :, None, :]


def pair_grads(query_side, stats_side, query_start, key_side, key_start):
    query_rows, d_mixed, query_seg = query_side
    log_total, delta_rows = stats_side
    key_rows, value_rows, key_seg = key_side
    score_scale = 1.0 / math.sqrt(HEAD_DIM)
    allowed = visible(query_seg, query_start, key_seg, key_start)
    scores = (
        jnp.einsum("bqhd,bkhd->bqhk", query_rows, key_rows, preferred_element_type=jnp.float32)
        * score_scale
    )
    prob_rows = jnp.where(
        allowed, jnp.exp(jnp.where(allowed, scores - log_total[..., None], NEG_BIG)), 0.0
    )
    d_prob = jnp.einsum("bqhd,bkhd->bqhk", d_mixed, value_rows, preferred_element_type=jnp.float32)
    d_scores = (prob_rows * (d_prob - delta_rows[..., None])).astype(jnp.bfloat16)
    d_query = (
        jnp.einsum("bqhk,bkhd->bqhd", d_scores, key_rows, preferred_element_type=jnp.float32)
        * score_scale
    )
    d_key = (
        jnp.einsum("bqhk,bqhd->bkhd", d_scores, query_rows, preferred_element_type=jnp.float32)
        * score_scale
    )
    d_value = jnp.einsum(
        "bqhk,bqhd->bkhd",
        prob_rows.astype(jnp.bfloat16),
        d_mixed,
        preferred_element_type=jnp.float32,
    )
    return (d_query, d_key, d_value)


def per_device(
    tokens,
    segments,
    positions,
    gain_attn,
    shift_attn,
    gain_mlp,
    shift_mlp,
    qkv_weight,
    query_bias,
    key_bias,
    value_bias,
    dense_weight,
    expand_weight,
    expand_bias,
    contract_weight,
    output_bias,
    cotangent,
):
    shards = (
        gain_attn,
        shift_attn,
        gain_mlp,
        shift_mlp,
        qkv_weight,
        query_bias,
        key_bias,
        value_bias,
        dense_weight,
        expand_weight,
        expand_bias,
        contract_weight,
        output_bias,
    )
    gathered = (
        lax.all_gather(shards[0], ("dp", "ctx"), axis=0, tiled=True),
        lax.all_gather(shards[1], ("dp", "ctx"), axis=0, tiled=True),
        lax.all_gather(shards[2], ("dp", "ctx"), axis=0, tiled=True),
        lax.all_gather(shards[3], ("dp", "ctx"), axis=0, tiled=True),
        lax.all_gather(shards[4], ("dp", "ctx"), axis=0, tiled=True),
        lax.all_gather(shards[5], ("dp", "ctx"), axis=0, tiled=True),
        lax.all_gather(shards[6], ("dp", "ctx"), axis=0, tiled=True),
        lax.all_gather(shards[7], ("dp", "ctx"), axis=0, tiled=True),
        lax.all_gather(shards[8], ("dp", "ctx"), axis=0, tiled=True),
        lax.all_gather(shards[9], ("dp", "ctx"), axis=0, tiled=True),
        lax.all_gather(shards[10], ("dp", "ctx"), axis=0, tiled=True),
        lax.all_gather(shards[11], ("dp", "ctx"), axis=0, tiled=True),
        lax.all_gather(shards[12], ("dp", "ctx"), axis=0, tiled=True),
    )
    seq_count, tok_count, model_width = tokens.shape
    row_count = seq_count * tok_count
    head_count = model_width // HEAD_DIM
    heads_shape = (seq_count, tok_count, head_count, HEAD_DIM)
    flat_shape = (seq_count, tok_count, model_width)
    full_gain_attn = gathered[0].astype(jnp.float32)
    full_shift_attn = gathered[1].astype(jnp.float32)
    full_gain_mlp = gathered[2].astype(jnp.float32)
    full_shift_mlp = gathered[3].astype(jnp.float32)
    full_query_bias = gathered[5].astype(jnp.float32)
    full_key_bias = gathered[6].astype(jnp.float32)
    full_value_bias = gathered[7].astype(jnp.float32)
    full_expand_bias = gathered[10].astype(jnp.float32)
    full_output_bias = gathered[12].astype(jnp.float32)
    flat_in = tokens.reshape(row_count, model_width).astype(jnp.float32)

    def both_norms(values, gain_one, shift_one, gain_two, shift_two):
        return (normalize(values, gain_one, shift_one), normalize(values, gain_two, shift_two))

    (norm_attn, norm_mlp), norm_pull = jax.vjp(
        both_norms, flat_in, full_gain_attn, full_shift_attn, full_gain_mlp, full_shift_mlp
    )
    attn_in = norm_attn.astype(jnp.bfloat16)
    mlp_in = norm_mlp.astype(jnp.bfloat16)
    packed = jnp.dot(attn_in, gathered[4], preferred_element_type=jnp.float32)
    query_raw = (packed[:, :model_width] + full_query_bias).reshape(heads_shape)
    key_raw = (packed[:, model_width : 2 * model_width] + full_key_bias).reshape(heads_shape)
    value_rows = (
        (packed[:, 2 * model_width :] + full_value_bias).astype(jnp.bfloat16).reshape(heads_shape)
    )
    cosine, sine_part = angles(positions)

    def turn_heads(field_in):
        return rotate(field_in, cosine, sine_part)

    query_turned, query_pull = jax.vjp(turn_heads, query_raw)
    key_turned, key_pull = jax.vjp(turn_heads, key_raw)
    query_rows = query_turned.astype(jnp.bfloat16)
    key_rows = key_turned.astype(jnp.bfloat16)
    key_flat = key_rows.reshape(flat_shape)
    value_flat = value_rows.reshape(flat_shape)
    ctx_count = lax.axis_size("ctx")
    ctx_index = lax.axis_index("ctx")
    here_start = ctx_index * tok_count
    score_scale = 1.0 / math.sqrt(HEAD_DIM)
    start_max = jnp.full((seq_count, tok_count, head_count), NEG_BIG, jnp.float32)
    key_blk = lax.all_gather(key_flat, "ctx", axis=1, tiled=True)
    value_blk = lax.all_gather(value_flat, "ctx", axis=1, tiled=True)
    seg_blk = lax.all_gather(segments, "ctx", axis=1, tiled=True)
    block_len = key_blk.shape[1]
    key_blk = key_blk.reshape(seq_count, block_len, head_count, HEAD_DIM)
    value_blk = value_blk.reshape(seq_count, block_len, head_count, HEAD_DIM)
    allowed = visible(segments, here_start, seg_blk, jnp.int32(0))
    scores = (
        jnp.einsum("bqhd,bkhd->bqhk", query_rows, key_blk, preferred_element_type=jnp.float32)
        * score_scale
    )
    scores = jnp.where(allowed, scores, NEG_BIG)
    new_max = jnp.maximum(start_max, jnp.max(scores, axis=-1))
    weights = jnp.where(allowed, jnp.exp(scores - new_max[..., None]), 0.0)
    new_sum = jnp.sum(weights, axis=-1)
    new_acc = jnp.einsum(
        "bqhk,bkhd->bqhd",
        weights.astype(jnp.bfloat16),
        value_blk,
        preferred_element_type=jnp.float32,
    )
    log_total = new_max + jnp.log(new_sum)
    mixed_full = new_acc / new_sum[..., None]
    mixed_rows = mixed_full.astype(jnp.bfloat16).reshape(row_count, model_width)
    hidden_pre = jnp.dot(mlp_in, gathered[9], preferred_element_type=jnp.float32) + full_expand_bias
    hidden_act, gelu_pull = jax.vjp(exact_gelu, hidden_pre)
    hidden_rows = hidden_act.astype(jnp.bfloat16)
    result = (
        flat_in
        + jnp.dot(mixed_rows, gathered[8], preferred_element_type=jnp.float32)
        + jnp.dot(hidden_rows, gathered[11], preferred_element_type=jnp.float32)
        + full_output_bias
    )
    output = result.astype(jnp.bfloat16).reshape(flat_shape)
    regathered = (
        lax.all_gather(shards[0], ("dp", "ctx"), axis=0, tiled=True),
        lax.all_gather(shards[1], ("dp", "ctx"), axis=0, tiled=True),
        lax.all_gather(shards[2], ("dp", "ctx"), axis=0, tiled=True),
        lax.all_gather(shards[3], ("dp", "ctx"), axis=0, tiled=True),
        lax.all_gather(shards[4], ("dp", "ctx"), axis=0, tiled=True),
        lax.all_gather(shards[5], ("dp", "ctx"), axis=0, tiled=True),
        lax.all_gather(shards[6], ("dp", "ctx"), axis=0, tiled=True),
        lax.all_gather(shards[7], ("dp", "ctx"), axis=0, tiled=True),
        lax.all_gather(shards[8], ("dp", "ctx"), axis=0, tiled=True),
        lax.all_gather(shards[9], ("dp", "ctx"), axis=0, tiled=True),
        lax.all_gather(shards[10], ("dp", "ctx"), axis=0, tiled=True),
        lax.all_gather(shards[11], ("dp", "ctx"), axis=0, tiled=True),
        lax.all_gather(shards[12], ("dp", "ctx"), axis=0, tiled=True),
    )
    back_qkv = regathered[4]
    back_dense = regathered[8]
    back_expand = regathered[9]
    back_contract = regathered[11]
    grad_rows = cotangent.reshape(row_count, model_width)
    grad_full = grad_rows.astype(jnp.float32)
    d_output_bias = jnp.sum(grad_full, axis=0)
    d_contract = jnp.einsum("rf,rd->fd", hidden_rows, grad_rows, preferred_element_type=jnp.float32)
    d_hidden = contract_last(grad_rows, back_contract)
    d_hidden_pre = gelu_pull(d_hidden)[0].astype(jnp.bfloat16)
    d_expand_bias = jnp.sum(d_hidden_pre.astype(jnp.float32), axis=0)
    d_expand = jnp.einsum("rd,rf->df", mlp_in, d_hidden_pre, preferred_element_type=jnp.float32)
    d_norm_mlp = contract_last(d_hidden_pre, back_expand)
    d_dense = jnp.einsum("ri,rd->id", mixed_rows, grad_rows, preferred_element_type=jnp.float32)
    d_mixed = contract_last(grad_rows, back_dense).astype(jnp.bfloat16).reshape(heads_shape)
    delta_rows = jnp.sum(d_mixed.astype(jnp.float32) * mixed_full, axis=-1)
    query_side = (query_rows, d_mixed, segments)
    stats_side = (log_total, delta_rows)

    def carry_step(step_num, loop_state):
        key_block, grad_block, d_query_acc = loop_state
        owner_dev = (ctx_index - step_num) % ctx_count
        key_side = (
            key_block[0].reshape(heads_shape),
            key_block[1].reshape(heads_shape),
            key_block[2],
        )
        d_query_part, d_key_part, d_value_part = pair_grads(
            query_side, stats_side, here_start, key_side, owner_dev * tok_count
        )
        grad_block = (
            grad_block[0] + d_key_part.reshape(flat_shape),
            grad_block[1] + d_value_part.reshape(flat_shape),
        )
        key_block = from_behind((key_block[0], key_block[1], key_block[2]), "ctx", 1)
        grad_block = (
            shifted(grad_block[0].astype(jnp.bfloat16), "ctx", 1).astype(jnp.float32),
            shifted(grad_block[1].astype(jnp.bfloat16), "ctx", 1).astype(jnp.float32),
        )
        return (key_block, grad_block, d_query_acc + d_query_part)

    zero_flat = jnp.zeros(flat_shape, jnp.float32)
    final_state = lax.fori_loop(
        0,
        ctx_count,
        carry_step,
        (
            (key_flat, value_flat, segments),
            (zero_flat, zero_flat),
            jnp.zeros(heads_shape, jnp.float32),
        ),
    )
    d_query_sum = final_state[2]
    d_key_sum = final_state[1][0].reshape(heads_shape)
    d_value_sum = final_state[1][1].reshape(heads_shape)
    d_query_raw = query_pull(d_query_sum)[0].astype(jnp.bfloat16).reshape(row_count, model_width)
    d_key_raw = key_pull(d_key_sum)[0].astype(jnp.bfloat16).reshape(row_count, model_width)
    d_value_low = d_value_sum.astype(jnp.bfloat16).reshape(row_count, model_width)
    d_query_bias = jnp.sum(d_query_raw.astype(jnp.float32), axis=0)
    d_key_bias = jnp.sum(d_key_raw.astype(jnp.float32), axis=0)
    d_value_bias = jnp.sum(d_value_low.astype(jnp.float32), axis=0)
    d_packed = jnp.concatenate([d_query_raw, d_key_raw, d_value_low], axis=1)
    d_qkv = jnp.einsum("rd,rp->dp", attn_in, d_packed, preferred_element_type=jnp.float32)
    d_norm_attn = contract_last(d_packed, back_qkv)
    d_flat, d_gain_attn, d_shift_attn, d_gain_mlp, d_shift_mlp = norm_pull(
        (d_norm_attn, d_norm_mlp)
    )
    input_grad = (grad_full + d_flat).astype(jnp.bfloat16).reshape(flat_shape)
    owned_grads = (
        lax.psum_scatter(d_gain_attn, ("dp", "ctx"), scatter_dimension=0, tiled=True),
        lax.psum_scatter(d_shift_attn, ("dp", "ctx"), scatter_dimension=0, tiled=True),
        lax.psum_scatter(d_gain_mlp, ("dp", "ctx"), scatter_dimension=0, tiled=True),
        lax.psum_scatter(d_shift_mlp, ("dp", "ctx"), scatter_dimension=0, tiled=True),
        lax.psum_scatter(d_qkv, ("dp", "ctx"), scatter_dimension=0, tiled=True),
        lax.psum_scatter(d_query_bias, ("dp", "ctx"), scatter_dimension=0, tiled=True),
        lax.psum_scatter(d_key_bias, ("dp", "ctx"), scatter_dimension=0, tiled=True),
        lax.psum_scatter(d_value_bias, ("dp", "ctx"), scatter_dimension=0, tiled=True),
        lax.psum_scatter(d_dense, ("dp", "ctx"), scatter_dimension=0, tiled=True),
        lax.psum_scatter(d_expand, ("dp", "ctx"), scatter_dimension=0, tiled=True),
        lax.psum_scatter(d_expand_bias, ("dp", "ctx"), scatter_dimension=0, tiled=True),
        lax.psum_scatter(d_contract, ("dp", "ctx"), scatter_dimension=0, tiled=True),
        lax.psum_scatter(d_output_bias, ("dp", "ctx"), scatter_dimension=0, tiled=True),
    )
    return (
        output,
        input_grad,
        owned_grads[0],
        owned_grads[1],
        owned_grads[2],
        owned_grads[3],
        owned_grads[4],
        owned_grads[5],
        owned_grads[6],
        owned_grads[7],
        owned_grads[8],
        owned_grads[9],
        owned_grads[10],
        owned_grads[11],
        owned_grads[12],
    )


LANES = 128
BLK = 256
ATT_ROWS = 512
ROWS = 512
BACK_ROWS = 1024
BF = jnp.bfloat16
F32 = jnp.float32
SWAP = [(0, 1), (1, 0)]
CTX_AXES = ("y", "x", "core")
ALL_AXES = ("dp", "y", "x", "core")


def dot_nn(a, b):
    return lax.dot_general(a, b, (((1,), (0,)), ((), ())), preferred_element_type=F32)


def dot_nt(a, b):
    return lax.dot_general(a, b, (((1,), (1,)), ((), ())), preferred_element_type=F32)


def dot_tn(a, b):
    return lax.dot_general(a, b, (((0,), (0,)), ((), ())), preferred_element_type=F32)


def whole(shape):
    return pl.BlockSpec(shape, lambda *ids: (0,) * len(shape))


def pre_body(x_ref, vec_ref, w_ref, b_ref, cs_ref, s1_ref, s2_ref, eq_ref, ek_ref,
             attn_ref, mlp_ref, q_ref, k_ref, v_ref):
    x = x_ref[...].astype(F32)
    centre = x - jnp.mean(x, axis=1, keepdims=True)
    spread = jnp.mean(centre * centre, axis=1, keepdims=True)
    xhat = centre * lax.rsqrt(spread + EPSILON)
    attn_in = (xhat * vec_ref[0:1, :] + vec_ref[1:2, :]).astype(BF)
    attn_ref[...] = xhat.astype(BF)
    mlp_ref[...] = (xhat * vec_ref[2:3, :] + vec_ref[3:4, :]).astype(BF)
    packed = dot_nn(attn_in, w_ref[...]) + b_ref[...]
    heads = w_ref.shape[1] // (3 * LANES)
    wide = heads * LANES
    cs, s1, s2 = cs_ref[...], s1_ref[...], s2_ref[...]
    half = ROT_DIMS // 2

    def turn(u):
        return u * cs + pltpu.roll(u, LANES - half, 1) * s1 + pltpu.roll(u, half, 1) * s2

    for h in range(heads):
        cols = slice(h * LANES, (h + 1) * LANES)
        q = turn(packed[:, h * LANES : (h + 1) * LANES])
        q_ref[:, cols] = (q.astype(BF).astype(F32) * (1.0 / math.sqrt(HEAD_DIM)) + eq_ref[...]).astype(BF)
        k = turn(packed[:, wide + h * LANES : wide + (h + 1) * LANES])
        k_ref[:, cols] = (k + ek_ref[...]).astype(BF)
        v_ref[:, cols] = packed[:, 2 * wide + h * LANES : 2 * wide + (h + 1) * LANES].astype(BF)


def pre_call(x, vecs, w_pad, b_pad, tables):
    rows, width = x.shape
    cols = w_pad.shape[1]
    third = cols // 3
    row_block = lambda n: pl.BlockSpec((ROWS, n), lambda i: (i, 0))
    return pl.pallas_call(
        pre_body,
        grid=(rows // ROWS,),
        in_specs=[row_block(width), whole(vecs.shape), whole(w_pad.shape), whole(b_pad.shape)]
        + [row_block(LANES)] * 5,
        out_specs=[row_block(width)] * 2 + [row_block(third)] * 3,
        out_shape=[jax.ShapeDtypeStruct((rows, width), BF)] * 2
        + [jax.ShapeDtypeStruct((rows, third), BF)] * 3,
        compiler_params=pltpu.CompilerParams(vmem_limit_bytes=56 << 20),
        cost_estimate=pl.CostEstimate(
            flops=2 * rows * width * cols, bytes_accessed=rows * (width * 6 + cols * 2 + LANES * 20), transcendentals=0
        ),
        name="norm_qkv",
    )(x, vecs, w_pad, b_pad, *tables)


def piece(ref, j):
    return ref[j * ATT_ROWS : (j + 1) * ATT_ROWS, :]


def causal(transposed):
    rows = lax.broadcasted_iota(jnp.int32, (ATT_ROWS, ATT_ROWS), 0)
    cols = lax.broadcasted_iota(jnp.int32, (ATT_ROWS, ATT_ROWS), 1)
    return cols >= rows if transposed else rows >= cols


def row_form(column):
    return jnp.transpose(jnp.broadcast_to(column, (ATT_ROWS, LANES)))[0:1, :]


def attn_body(q_ref, k_ref, v_ref, mixed_ref, full_ref, lse_ref):
    for i in range(q_ref.shape[0] // ATT_ROWS):
        q = piece(q_ref, i)
        scores = [dot_nt(q, piece(k_ref, j)) for j in range(i + 1)]
        scores[i] = jnp.where(causal(False), scores[i], NEG_BIG)
        top = scores[0]
        for s in scores[1:]:
            top = jnp.maximum(top, s)
        top = jnp.max(top, axis=1, keepdims=True)
        acc = None
        total = None
        for j in range(i + 1):
            p = jnp.exp(scores[j] - top)
            total = p if total is None else total + p
            part = dot_nn(p.astype(BF), piece(v_ref, j))
            acc = part if acc is None else acc + part
        total = jnp.sum(total, axis=1, keepdims=True)
        mixed = acc / total
        here = slice(i * ATT_ROWS, (i + 1) * ATT_ROWS)
        full_ref[here, :] = mixed
        mixed_ref[here, :] = mixed.astype(BF)
        lse_ref[0, i : i + 1, :] = row_form(top + jnp.log(total))


def attn_call(q, k, v):
    rows, cols = q.shape
    heads = cols // LANES
    col = pl.BlockSpec((rows, LANES), lambda h: (0, h))
    stats = pl.BlockSpec((1, rows // ATT_ROWS, ATT_ROWS), lambda h: (h, 0, 0))
    return pl.pallas_call(
        attn_body,
        grid=(heads,),
        in_specs=[col] * 3,
        out_specs=[col, col, stats],
        out_shape=[
            jax.ShapeDtypeStruct((rows, cols), BF),
            jax.ShapeDtypeStruct((rows, cols), F32),
            jax.ShapeDtypeStruct((heads, rows // ATT_ROWS, ATT_ROWS), F32),
        ],
        compiler_params=pltpu.CompilerParams(vmem_limit_bytes=48 << 20),
        cost_estimate=pl.CostEstimate(
            flops=heads * rows * rows * 2 * LANES * 4, bytes_accessed=rows * cols * 12, transcendentals=heads * rows * rows // 2
        ),
        name="attention",
    )(q, k, v)


def attn_back_body(q_ref, k_ref, v_ref, do_ref, full_ref, lse_ref, cs_ref, s1_ref, s2_ref,
                   dq_ref, dk_ref, dv_ref, dk_acc, dv_acc, kt_ref):
    blocks = q_ref.shape[0] // ATT_ROWS
    half = ROT_DIMS // 2
    keep = lax.broadcasted_iota(jnp.int32, (ATT_ROWS, LANES), 1) < HEAD_DIM

    def unturn(g, here):
        g = jnp.where(keep, g, 0.0)
        return (
            g * cs_ref[here, :]
            - pltpu.roll(g, LANES - half, 1) * s1_ref[here, :]
            - pltpu.roll(g, half, 1) * s2_ref[here, :]
        ).astype(BF)

    for j in range(blocks):
        kt_ref[j] = jnp.transpose(piece(k_ref, j).astype(F32)).astype(BF)
    for i in reversed(range(blocks)):
        here = slice(i * ATT_ROWS, (i + 1) * ATT_ROWS)
        q = q_ref[here, :]
        do = do_ref[here, :]
        delta = row_form(jnp.sum(do.astype(F32) * full_ref[here, :], axis=1, keepdims=True))
        lse = lse_ref[0, i : i + 1, :]
        dq = None
        for j in range(i + 1):
            k = piece(k_ref, j)
            scores = dot_nt(k, q)
            if j == i:
                scores = jnp.where(causal(True), scores, NEG_BIG)
            p = jnp.exp(scores - lse)
            dp = dot_nt(piece(v_ref, j), do)
            ds = (p * (dp - delta)).astype(BF)
            dv = dot_nn(p.astype(BF), do)
            dk = dot_nn(ds, q)
            if i == blocks - 1:
                dv_acc[j] = dv
                dk_acc[j] = dk
            else:
                dv_acc[j] += dv
                dk_acc[j] += dk
            part = dot_nn(kt_ref[j], ds)
            dq = part if dq is None else dq + part
        dq_ref[here, :] = unturn(jnp.transpose(dq) * (1.0 / math.sqrt(HEAD_DIM)), here)
        dk_ref[here, :] = unturn(dk_acc[i], here)
        dv_ref[here, :] = dv_acc[i].astype(BF)


def attn_back_call(q, k, v, do, full, lse, tables):
    rows, cols = q.shape
    heads = cols // LANES
    col = pl.BlockSpec((rows, LANES), lambda h: (0, h))
    one = pl.BlockSpec((rows, LANES), lambda h: (0, 0))
    stats = pl.BlockSpec((1, rows // ATT_ROWS, ATT_ROWS), lambda h: (h, 0, 0))
    return pl.pallas_call(
        attn_back_body,
        grid=(heads,),
        in_specs=[col] * 5 + [stats] + [one] * 3,
        out_specs=[col] * 3,
        scratch_shapes=[pltpu.VMEM((rows // ATT_ROWS, ATT_ROWS, LANES), F32)] * 2 + [pltpu.VMEM((rows // ATT_ROWS, LANES, ATT_ROWS), BF)],
        out_shape=[jax.ShapeDtypeStruct((rows, cols), BF)] * 3,
        compiler_params=pltpu.CompilerParams(vmem_limit_bytes=48 << 20),
        cost_estimate=pl.CostEstimate(
            flops=heads * rows * rows * 2 * LANES * 2, bytes_accessed=rows * cols * 18, transcendentals=0
        ),
        name="attention_back",
    )(q, k, v, do, full, lse, *tables)


def beside(one_ref, two_ref, axis):
    return jnp.concatenate([one_ref[...], two_ref[...]], axis=axis)


def mlp_body(m_ref, mixed_ref, we1_ref, we2_ref, be_ref, wd_ref, wc1_ref, wc2_ref, hid_ref, slope_ref, out_ref):
    pre = dot_nn(m_ref[...], beside(we1_ref, we2_ref, 1)) + be_ref[...]
    share = 0.5 * (1.0 + lax.erf(pre * math.sqrt(0.5)))
    hidden = (pre * share).astype(BF)
    hid_ref[...] = hidden
    slope_ref[...] = (share + pre * (jnp.exp(-0.5 * pre * pre) * (1.0 / math.sqrt(2.0 * math.pi)))).astype(BF)
    out_ref[...] = (dot_nn(mixed_ref[...], wd_ref[...]) + dot_nn(hidden, beside(wc1_ref, wc2_ref, 0))).astype(BF)


def mlp_call(mlp_in, mixed, w_exps, b_exp, w_den, w_cons):
    rows, width = mlp_in.shape
    hid = b_exp.shape[1]
    weights = (*w_exps, b_exp, w_den, *w_cons)
    row_block = lambda n: pl.BlockSpec((ROWS, n), lambda i: (i, 0))
    return pl.pallas_call(
        mlp_body,
        grid=(rows // ROWS,),
        in_specs=[row_block(width), row_block(mixed.shape[1])] + [whole(w.shape) for w in weights],
        out_specs=[row_block(hid), row_block(hid), row_block(width)],
        out_shape=[jax.ShapeDtypeStruct((rows, n), BF) for n in (hid, hid, width)],
        compiler_params=pltpu.CompilerParams(vmem_limit_bytes=56 << 20),
        cost_estimate=pl.CostEstimate(
            flops=6 * rows * width * hid, bytes_accessed=rows * (width * 4 + hid * 6), transcendentals=rows * hid * 2
        ),
        name="mlp_forward",
    )(mlp_in, mixed, *weights)


def first_or_add(ref, value, step):
    @pl.when(step == 0)
    def _():
        ref[...] = value

    @pl.when(step > 0)
    def _():
        ref[...] += value


def mlp_back_body(dy_ref, hid_ref, slope_ref, m_ref, mixed_ref, vec_ref, col_ref, we1_ref, we2_ref, wd_ref, wc1_ref, wc2_ref,
                  dmix_ref, pull_ref, near_ref, far_ref, dden_ref, stat_ref, dbias_ref,
                  dcon_ref, dexp_ref):
    step = pl.program_id(0)
    dy = dy_ref[...]
    dmix_ref[...] = dot_nt(dy, wd_ref[...]).astype(BF)
    dpre = (dot_nt(dy, beside(wc1_ref, wc2_ref, 0)) * slope_ref[...].astype(F32)).astype(BF)
    first_or_add(dcon_ref, dot_tn(hid_ref[...], dy), step)
    first_or_add(dden_ref, dot_tn(mixed_ref[...], dy), step)
    first_or_add(dexp_ref, dot_tn(m_ref[...], dpre), step)
    e = dot_nt(dpre, beside(we1_ref, we2_ref, 1))
    pull_ref[...] = (e * vec_ref[2:3, :]).astype(BF)
    first_or_add(dbias_ref, dot_nn(jnp.ones((8, dpre.shape[0]), BF), dpre)[0:1, :], step)

    @pl.when(step == pl.num_programs(0) - 1)
    def _():
        part = dcon_ref.shape[0] // 2
        plain, bias = dexp_ref[...], dbias_ref[...]
        w_exp = beside(we1_ref, we2_ref, 1).astype(F32)
        grad = plain * col_ref[:, 2:3] + bias * col_ref[:, 3:4]
        blocks = near_ref.shape[0]
        rows, lines = part // blocks, grad.shape[0] // (2 * blocks)
        for n in range(blocks):
            top = 2 * n * lines
            for ref, at in ((near_ref, 0), (far_ref, part)):
                value = jnp.concatenate(
                    [grad[top : top + lines, at : at + part], grad[top + lines : top + 2 * lines, at : at + part]], axis=1
                )
                ref[n, :lines, :] = value.astype(ref.dtype)
                ref[n, lines:, :] = dcon_ref[at + n * rows : at + (n + 1) * rows, :].astype(ref.dtype)
        stat_ref[:, 0:1] = jnp.sum(plain * w_exp, axis=1, keepdims=True)
        stat_ref[:, 1:2] = jnp.sum(bias * w_exp, axis=1, keepdims=True)


def mlp_back_call(dy, hidden, slope, xhat, mixed, vecs, vec_cols, w_exps, w_den, w_cons, n_dp):
    rows, width = dy.shape
    hid, mix = hidden.shape[1], mixed.shape[1]
    row_block = lambda n: pl.BlockSpec((BACK_ROWS, n), lambda i: (i, 0))
    both = (n_dp, width // (2 * n_dp) + hid // (2 * n_dp), width)
    full = [(both, F32), (both, BF), ((mix, width), F32), ((width, 2), F32), ((1, hid), F32)]
    weights = (vecs, vec_cols, *w_exps, w_den, *w_cons)
    return pl.pallas_call(
        mlp_back_body,
        grid=(rows // BACK_ROWS,),
        in_specs=[row_block(n) for n in (width, hid, hid, width, mix)] + [whole(w.shape) for w in weights],
        out_specs=[row_block(mix), row_block(width)] + [whole(f) for f, _ in full],
        out_shape=[jax.ShapeDtypeStruct((rows, mix), BF), jax.ShapeDtypeStruct((rows, width), BF)]
        + [jax.ShapeDtypeStruct(f, t) for f, t in full],
        scratch_shapes=[pltpu.VMEM((hid, width), F32), pltpu.VMEM((width, hid), F32)],
        compiler_params=pltpu.CompilerParams(vmem_limit_bytes=56 << 20),
        cost_estimate=pl.CostEstimate(
            flops=30 * rows * width * hid, bytes_accessed=rows * (width * 8 + hid * 6) + 8 * width * hid, transcendentals=0
        ),
        name="mlp_back",
    )(dy, hidden, slope, xhat, mixed, *weights)


def last_body(dq_ref, dk_ref, dv_ref, mpull_ref, vec_ref, w_ref, pull_ref, packed_ref):
    parts = []
    for ref in (dq_ref, dk_ref, dv_ref):
        wide = ref[...].astype(F32)
        parts += [wide[:, h * LANES : h * LANES + HEAD_DIM] for h in range(wide.shape[1] // LANES)]
    packed = jnp.concatenate(parts, axis=1).astype(BF)
    packed_ref[...] = packed
    e = dot_nt(packed, w_ref[...])
    pull_ref[...] = (e * vec_ref[0:1, :] + mpull_ref[...].astype(F32)).astype(BF)


def last_call(dq, dk, dv, mpull, vecs, w_qkv):
    rows, width = mpull.shape
    third, cols = dq.shape[1], w_qkv.shape[1]
    row_block = lambda n: pl.BlockSpec((ROWS, n), lambda i: (i, 0))
    return pl.pallas_call(
        last_body,
        grid=(rows // ROWS,),
        in_specs=[row_block(n) for n in (third, third, third, width)] + [whole(vecs.shape), whole(w_qkv.shape)],
        out_specs=[row_block(width), row_block(cols)],
        out_shape=[jax.ShapeDtypeStruct((rows, width), BF), jax.ShapeDtypeStruct((rows, cols), BF)],
        compiler_params=pltpu.CompilerParams(vmem_limit_bytes=56 << 20),
        cost_estimate=pl.CostEstimate(
            flops=2 * rows * width * cols, bytes_accessed=rows * (width * 6 + cols * 4) + 2 * width * cols, transcendentals=0
        ),
        name="input_pull",
    )(dq, dk, dv, mpull, vecs, w_qkv)


def qkv_grad_body(core_ref, xhat_ref, packed_ref, w_ref, col_ref, near_ref, far_ref, stat_ref, dbias_ref):
    @pl.when(pl.program_id(0) == 0)
    def _():
        dbias_ref[...] = dot_nn(jnp.ones((8, packed_ref.shape[0]), BF), packed_ref[...])[0:1, :]

    plain = dot_tn(xhat_ref[...], packed_ref[...])
    bias = dbias_ref[...]
    weight = w_ref[...].astype(F32)
    stat_ref[:, 0:1] = jnp.sum(plain * weight, axis=1, keepdims=True)
    stat_ref[:, 1:2] = jnp.sum(bias * weight, axis=1, keepdims=True)
    grad = plain * col_ref[:, 0:1] + bias * col_ref[:, 1:2]
    half = near_ref.shape[2]
    one, two = grad[:, :half], grad[:, half:]
    first = core_ref[0] == 0
    blocks, lines = near_ref.shape[0], near_ref.shape[1]
    rows = grad.shape[0] // blocks
    for ref, value in ((near_ref, jnp.where(first, one, two)), (far_ref, jnp.where(first, two, one))):
        for n in range(blocks):
            ref[n, :rows, :] = value[n * rows : (n + 1) * rows].astype(BF)
            ref[n, rows:, :] = jnp.zeros((lines - rows, half), BF)


def qkv_grad_call(core, xhat, packed, w_qkv, vec_cols, n_dp):
    rows, width = xhat.shape
    cols = packed.shape[1]
    steps = 2
    block = lambda n: pl.BlockSpec((width // steps, n), lambda i: (i, 0))
    out = (n_dp, width // n_dp + 16, cols // 2)
    out_block = pl.BlockSpec((n_dp // steps,) + out[1:], lambda i: (i, 0, 0))
    return pl.pallas_call(
        qkv_grad_body,
        grid=(steps,),
        in_specs=[
            pl.BlockSpec(memory_space=pltpu.SMEM),
            pl.BlockSpec((rows, width // steps), lambda i: (0, i)),
            whole(packed.shape),
            block(cols),
            block(vec_cols.shape[1]),
        ],
        out_specs=[out_block, out_block, block(2), whole((1, cols))],
        out_shape=[jax.ShapeDtypeStruct(out, BF)] * 2
        + [jax.ShapeDtypeStruct((width, 2), F32), jax.ShapeDtypeStruct((1, cols), F32)],
        compiler_params=pltpu.CompilerParams(vmem_limit_bytes=56 << 20),
        cost_estimate=pl.CostEstimate(flops=2 * rows * width * cols, bytes_accessed=rows * width * 4, transcendentals=0),
        name="qkv_grad",
    )(core, xhat, packed, w_qkv, vec_cols)


def pack_body(qkv_ref, exp_ref, small_ref, marks_ref, out_ref):
    qkv, exp, small = qkv_ref[...].astype(F32), exp_ref[...].astype(F32), small_ref[...].astype(F32)
    share, wide = qkv.shape[0], out_ref.shape[2]
    band = qkv.shape[1] // 12
    third = 3 * band // 2
    n_dp = 4
    strip = (wide - third) // n_dp
    line = jnp.concatenate([small[n : n + 1] for n in range(small.shape[0])] + [jnp.zeros((1, wide - small.size), F32)], axis=1)
    for c in range(2):
        marks = marks_ref[c]
        toks = marks.shape[1] // 3
        extra = jnp.concatenate(
            [
                line,
                jnp.concatenate([marks[:, : 2 * toks], jnp.zeros((1, wide - 2 * toks), F32)], axis=1),
                jnp.concatenate([marks[:, 2 * toks :], jnp.zeros((1, wide - toks), F32)], axis=1),
                jnp.zeros((5, wide), F32),
            ],
            axis=0,
        )
        for t in range(4):
            mine = jnp.concatenate([qkv[:, (4 * p + t) * band : (4 * p + t + 1) * band] for p in range(3)], axis=1)
            strips = [exp[:, (z * 8 + 2 * t + c) * strip : (z * 8 + 2 * t + c + 1) * strip] for z in range(n_dp)]
            cols = jnp.concatenate([mine[:, c * third : (c + 1) * third]] + strips, axis=1)
            out_ref[2 * t + c] = jnp.concatenate([cols, extra], axis=0).astype(BF)


def pack_call(qkv, exp, small, marks, wide):
    share = qkv.shape[0]
    return pl.pallas_call(
        pack_body,
        out_shape=jax.ShapeDtypeStruct((8, share + 8, wide), BF),
        cost_estimate=pl.CostEstimate(flops=0, bytes_accessed=qkv.size * 8, transcendentals=0),
        name="pack_columns",
    )(qkv, exp, small, marks)


def unpack_body(got_ref, qkv_ref, exp_ref, small_ref):
    share = qkv_ref.shape[0]
    band = qkv_ref.shape[1] // 12
    third = 3 * band // 2
    wide = got_ref.shape[2]
    strip = exp_ref.shape[1] // 32
    got = [got_ref[n].astype(F32) for n in range(8)]
    mine = [jnp.concatenate([got[2 * t][:share, :third], got[2 * t + 1][:share, :third]], axis=1) for t in range(4)]
    qkv_ref[...] = jnp.concatenate([mine[t][:, p * band : (p + 1) * band] for p in range(3) for t in range(4)], axis=1)
    exp_ref[...] = jnp.concatenate(
        [got[n][:share, third + z * strip : third + (z + 1) * strip] for z in range((wide - third) // strip) for n in range(8)],
        axis=1,
    )
    for c in range(2):
        small_ref[c] = (got[c] + got[2 + c] + got[4 + c] + got[6 + c])[share:, :]


def unpack_call(got, share, qkv_n, exp_n):
    extra = got.shape[1] - share
    return pl.pallas_call(
        unpack_body,
        out_shape=[
            jax.ShapeDtypeStruct((share, qkv_n), F32),
            jax.ShapeDtypeStruct((share, exp_n), F32),
            jax.ShapeDtypeStruct((2, extra, got.shape[2]), F32),
        ],
        cost_estimate=pl.CostEstimate(flops=0, bytes_accessed=got.size * 6, transcendentals=0),
        name="unpack_columns",
    )(got)


def tie(value, *others):
    return lax.optimization_barrier((value,) + others)[0]


def swap(value, axis):
    return lax.ppermute(value, axis, SWAP)


def exchange(value, axes):
    return lax.all_to_all(value, axes, 0, 0, tiled=True)


def by_xor(pieces, here):
    count = len(pieces)
    bit = 1
    while bit < count:
        flip = (here // bit) % 2 == 1
        pieces = [jnp.where(flip, pieces[k ^ bit], pieces[k]) for k in range(count)]
        bit *= 2
    return pieces


def along_dp(value, k):
    return lax.ppermute(value, "dp", [(z, z ^ k) for z in range(4)])


def gather_dp(value, after=None):
    pieces = [value] + [along_dp(value, k) for k in (1, 2, 3)]
    if after is not None:
        pieces = list(lax.optimization_barrier((*pieces, after))[:4])
    return jnp.stack(by_xor(pieces, lax.axis_index("dp")))


def scatter_dp(value):
    pieces = by_xor([value[k] for k in range(4)], lax.axis_index("dp"))
    got = [along_dp(pieces[k], k).astype(F32) for k in (1, 2, 3)]
    return (pieces[0].astype(F32) + got[0] + got[1] + got[2]).astype(BF)


def pick(first, second, core):
    return jnp.where(core == 0, first, second)


def halves_sum(halves, core):
    first, second = halves
    got = swap(pick(second, first, core).astype(BF), "core")
    return (pick(first, second, core) + got.astype(F32)).astype(BF)


def split_device(tokens, segments, positions, gain_attn, shift_attn, gain_mlp, shift_mlp, qkv_weight,
                 query_bias, key_bias, value_bias, dense_weight, expand_weight, expand_bias,
                 contract_weight, output_bias, cotangent):
    seqs, toks, width = tokens.shape
    rows = 8 * toks
    share = qkv_weight.shape[0]
    hidden_share = contract_weight.shape[0]
    n_dp = lax.axis_size("dp")
    heads = width // HEAD_DIM // 4
    band = heads * HEAD_DIM
    core = lax.axis_index("core")
    chip = lax.axis_index("y") * 2 + lax.axis_index("x")
    hop = [((z * 4 + t), (t * 4 + z)) for z in range(4) for t in range(4)]

    third = 3 * band // 2
    wide = third + n_dp * hidden_share
    vectors = (gain_attn, shift_attn, gain_mlp, shift_mlp, query_bias, key_bias, value_bias, output_bias)
    small = jnp.concatenate([v[None] for v in vectors] + [expand_bias.reshape(-1, share)], axis=0)
    small_n = small.size
    marks = jnp.concatenate([positions // 64, positions % 64, segments], axis=1)[:, None].astype(F32)
    cols = exchange(pack_call(qkv_weight, expand_weight, small, marks, wide), CTX_AXES)
    x_rows = exchange(tie(jnp.tile(tokens, (4, 1, 1)), cols), CTX_AXES).reshape(rows, width)
    dy_tiled = jnp.tile(cotangent, (4, 1, 1))
    dy_rows = exchange(tie(dy_tiled, x_rows), CTX_AXES).reshape(rows, width)
    weights = cols[:, :share].reshape(8 * share, wide)
    payload = jnp.concatenate([weights[:, :third], cols[:, share, :third]], axis=0)
    qkv_got = gather_dp(payload)
    exp_mine = weights[:, third:]
    half_n = 4 * share
    dense_moved = lax.ppermute(dense_weight, ("dp", "y", "x"), hop)
    low_mine = jnp.concatenate([contract_weight, dense_moved], axis=0)

    qkv_half = qkv_got[:, : 8 * share].reshape(width, third)
    qkv_mate = swap(qkv_half, "core")
    qkv_here = jnp.concatenate([pick(qkv_half, qkv_mate, core), pick(qkv_mate, qkv_half, core)], axis=1)
    w_pad = jnp.pad(qkv_here.reshape(width, 3 * heads, HEAD_DIM), ((0, 0), (0, 0), (0, LANES - HEAD_DIM)))
    w_pad = w_pad.reshape(width, 3 * heads * LANES)
    small = qkv_got[:, 8 * share :].reshape(n_dp * 8, third)[:, :small_n].astype(F32)
    vectors = [small[:, n * share : (n + 1) * share].reshape(width) for n in range(8)]
    vecs = jnp.stack(vectors[:4])
    vecs = tie(vecs, dy_tiled)
    vec_cols = vecs.T
    out_bias = vectors[7]
    biases = jnp.stack([lax.dynamic_slice(v, (chip * band,), (band,)) for v in vectors[4:7]])
    b_pad = jnp.pad(biases.reshape(3 * heads, HEAD_DIM), ((0, 0), (0, LANES - HEAD_DIM))).reshape(1, -1)
    exp_bias = small[:, 8 * share :].reshape(n_dp, 4, 2, hidden_share)
    exp_bias = lax.dynamic_index_in_dim(exp_bias, chip, 1, keepdims=False).transpose(1, 0, 2).reshape(2, -1)
    exp_bias = jnp.stack([pick(exp_bias[0], exp_bias[1], core), pick(exp_bias[1], exp_bias[0], core)]).reshape(1, -1)

    marks = cols[:, share + 1 : share + 3].astype(F32)
    pos = (marks[:, 0, :toks] * 64.0 + marks[:, 0, toks : 2 * toks]).reshape(rows, 1)
    seg = marks[:, 1, :toks].reshape(rows, 1).astype(jnp.int32)
    lane = jnp.arange(LANES)[None, :]
    half = ROT_DIMS // 2
    inverse = jnp.exp((lane % half).astype(F32) * (-2.0 * math.log(10000.0) / ROT_DIMS))
    angle = pos * inverse
    cosine, sine = jnp.cos(angle), jnp.sin(angle)
    table_c = jnp.where(lane < ROT_DIMS, cosine, jnp.where(lane < HEAD_DIM, 1.0, 0.0))
    table_1 = jnp.where(lane < half, -sine, 0.0)
    table_2 = jnp.where((lane >= half) & (lane < ROT_DIMS), sine, 0.0)
    docs = 16
    in_doc = (lane >= HEAD_DIM) & (lane < HEAD_DIM + docs)
    same = in_doc & (lane - HEAD_DIM == seg)
    mark_q = jnp.where(same, 1.0, 0.0)
    mark_k = jnp.where(in_doc & ~same, NEG_BIG, 0.0)

    xhat, mlp_in, q, k, v = pre_call(x_rows, vecs, w_pad, b_pad, (table_c, table_1, table_2, mark_q, mark_k))
    exp_got = gather_dp(tie(exp_mine, qkv_got), q).reshape(width, -1)
    low_got = gather_dp(tie(low_mine, qkv_got), q)
    mixed, mixed_full, lse = attn_call(q, k, v)

    half_rows = n_dp * hidden_share
    exp_mate, low_mate, _ = lax.optimization_barrier((swap(exp_got, "core"), swap(low_got, "core"), mixed))
    w_exps = (exp_got, exp_mate)
    w_cons = tuple(w[:, :hidden_share].reshape(half_rows, width) for w in (low_got, low_mate))
    den, den_mate = low_got[:, hidden_share:], low_mate[:, hidden_share:]
    w_den = jnp.stack([pick(den, den_mate, core), pick(den_mate, den, core)], axis=1).reshape(heads, HEAD_DIM, width)
    w_den = jnp.pad(w_den, ((0, 0), (0, LANES - HEAD_DIM), (0, 0))).reshape(heads * LANES, width)

    hidden, slope, out_part = mlp_call(mlp_in, mixed, w_exps, exp_bias, w_den, w_cons)
    out_got = exchange(out_part.reshape(8, toks, width), CTX_AXES)

    d_mixed, mlp_pull, low_near, low_far, d_den, mlp_stat, d_exp_bias = mlp_back_call(
        dy_rows, hidden, slope, xhat, mixed, vecs, vec_cols, w_exps, w_den, w_cons, n_dp
    )
    near_and = lambda near, far: (near + swap(far, "core").astype(F32)).astype(BF)
    d_den = d_den.reshape(heads, LANES, width)[:, :HEAD_DIM].reshape(4, 2, share, width)
    den_sum = halves_sum((d_den[:, 0], d_den[:, 1]), core)
    low_sum = jnp.concatenate([near_and(low_near, low_far), den_sum], axis=1)
    d_mixed, low_sum = lax.optimization_barrier((d_mixed, low_sum))
    low_sum = scatter_dp(low_sum)
    dq, dk, dv = attn_back_call(q, k, v, d_mixed, mixed_full, lse, (table_c, table_1, table_2))
    out_got, dq, low_sum = lax.optimization_barrier((out_got, dq, low_sum))
    out_sum = jnp.sum(out_got.reshape(4, 2, toks, width).astype(F32), axis=0)
    output = (tokens.astype(F32) + out_sum + out_bias).astype(BF)
    exp_own = jnp.concatenate([low_sum[:half_n, :half_rows], low_sum[:half_n, half_rows:]], axis=0)
    grad_contract = low_sum[half_n : half_n + hidden_share].astype(F32)
    grad_dense = lax.ppermute(low_sum[half_n + hidden_share :], ("dp", "y", "x"), hop).astype(F32)
    dq = tie(dq, output)
    pull, packed = last_call(dq, dk, dv, mlp_pull, vecs, qkv_here)
    pulled = exchange(pull.reshape(8, toks, width), CTX_AXES)
    core_arr = core.reshape(1).astype(jnp.int32)
    qkv_near, qkv_far, attn_stat, d_bias = qkv_grad_call(core_arr, tie(xhat, pull), packed, qkv_here, vec_cols, n_dp)
    d_bias = d_bias.reshape(3, band)
    d_exp_bias = d_exp_bias.reshape(2, n_dp, hidden_share)
    d_exp_bias = jnp.stack([pick(d_exp_bias[0], d_exp_bias[1], core), pick(d_exp_bias[1], d_exp_bias[0], core)], axis=1)
    d_out_bias = jnp.sum(cotangent.astype(F32), axis=(0, 1))
    lines = [v.reshape(-1, share) for v in (attn_stat[:, 0], attn_stat[:, 1], mlp_stat[:, 0], mlp_stat[:, 1])]
    for n in range(3):
        line = lax.dynamic_update_slice(jnp.zeros((width,), F32), d_bias[n], (chip * band,))
        lines.append(line.reshape(-1, share))
    lines.append(d_out_bias.reshape(-1, share))
    line = jnp.zeros((n_dp, 4, 2, hidden_share), F32)
    line = lax.dynamic_update_slice(line, d_exp_bias[:, None], (0, chip, 0, 0))
    lines.append(line.reshape(-1, hidden_share))
    lines = jnp.pad(jnp.concatenate(lines, axis=1), ((0, 0), (0, 2 * third - small_n))).reshape(n_dp, 8, 2 * third)
    spread = small_n // 2
    line_halves = [
        jnp.pad(lines[:, :, n * spread : (n + 1) * spread], ((0, 0), (0, 8), (0, third - spread))).astype(BF) for n in range(2)
    ]
    qkv_near = lax.dynamic_update_slice(qkv_near, pick(line_halves[0], line_halves[1], core), (0, 8 * share, 0))
    qkv_far = lax.dynamic_update_slice(qkv_far, pick(line_halves[1], line_halves[0], core), (0, 8 * share, 0))
    qkv_own = scatter_dp(near_and(qkv_near.astype(F32), qkv_far))
    own_cols = jnp.concatenate([qkv_own[: 8 * share], exp_own], axis=1).reshape(8, share, wide)
    own_small = jnp.pad(qkv_own[8 * share : 8 * share + 8][:, None], ((0, 0), (0, 7), (0, wide - third)))
    owned, pulled = lax.optimization_barrier((jnp.concatenate([own_cols, own_small], axis=1), pulled))
    owned = exchange(owned, CTX_AXES)
    grad_qkv, grad_expand, small_grads = unpack_call(owned, share, qkv_weight.shape[1], expand_weight.shape[1])
    small_grads = small_grads[:, 0, :spread].reshape(small_n)
    ge = jnp.sum(pulled.reshape(4, 2, toks, width).astype(F32), axis=0)
    own = tokens.astype(F32)
    own_c = own - jnp.mean(own, axis=2, keepdims=True)
    own_r = lax.rsqrt(jnp.mean(own_c * own_c, axis=2, keepdims=True) + EPSILON)
    own_h = own_c * own_r
    back = own_r * (ge - jnp.mean(ge, axis=2, keepdims=True) - own_h * jnp.mean(ge * own_h, axis=2, keepdims=True))
    input_grad = (cotangent.astype(F32) + back).astype(BF)
    part = [small_grads[n * share : (n + 1) * share] for n in range(8)]
    return (output, input_grad, part[0], part[1], part[2], part[3], grad_qkv, part[4], part[5], part[6],
            grad_dense, grad_expand, small_grads[8 * share :], grad_contract, part[7])


def general_plan(mesh):
    placed = (
        P("dp", "ctx", None),
        P("dp", "ctx"),
        P("dp", "ctx"),
        P(("dp", "ctx")),
        P(("dp", "ctx")),
        P(("dp", "ctx")),
        P(("dp", "ctx")),
        P(("dp", "ctx"), None),
        P(("dp", "ctx")),
        P(("dp", "ctx")),
        P(("dp", "ctx")),
        P(("dp", "ctx"), None),
        P(("dp", "ctx"), None),
        P(("dp", "ctx")),
        P(("dp", "ctx"), None),
        P(("dp", "ctx")),
        P("dp", "ctx", None),
    )
    return jax.shard_map(
        per_device,
        mesh=mesh,
        in_specs=placed,
        out_specs=(
            P("dp", "ctx", None),
            P("dp", "ctx", None),
            P(("dp", "ctx")),
            P(("dp", "ctx")),
            P(("dp", "ctx")),
            P(("dp", "ctx")),
            P(("dp", "ctx"), None),
            P(("dp", "ctx")),
            P(("dp", "ctx")),
            P(("dp", "ctx")),
            P(("dp", "ctx"), None),
            P(("dp", "ctx"), None),
            P(("dp", "ctx")),
            P(("dp", "ctx"), None),
            P(("dp", "ctx")),
        ),
        check_vma=False,
    )


def split_plan(mesh):
    fine = Mesh(mesh.devices.reshape(mesh.shape["dp"], 2, 2, 2), ALL_AXES)
    tok = P("dp", CTX_AXES, None)
    mark = P("dp", CTX_AXES)
    vec = P(ALL_AXES)
    mat = P(ALL_AXES, None)
    return jax.shard_map(
        split_device,
        mesh=fine,
        in_specs=(tok, mark, mark, vec, vec, vec, vec, mat, vec, vec, vec, mat, mat, vec, mat, vec, tok),
        out_specs=(tok, tok, vec, vec, vec, vec, mat, vec, vec, vec, mat, mat, vec, mat, vec),
        check_vma=False,
    )


def solution(mesh):
    if mesh.shape["ctx"] == 8 and mesh.shape["dp"] == 4:
        return split_plan(mesh)
    return general_plan(mesh)
```
